32 devices in a mesh: dp: 4 (over z), fsdp: 8 (over y, x, core).
Axes of the slice: x: 2, y: 2, z: 4, core: 2. Of those that a mesh axis runs over, the one named last changes fastest.
Arguments:
- images: bfloat16 [3072, 81, 1536], P(('dp', 'fsdp')), may hold values from -6 to 6
- embedding: bfloat16 [3072, 512], P(('dp', 'fsdp')), may hold values from -6 to 6
- episode: int32 [24576], P(('dp', 'fsdp')), may hold values from 0 to 3071, as said below
- valid_steps: int32 [3072], P(('dp', 'fsdp')), may hold values from 0 to 1, as said below
- targets: int32 [3072, 11], P(('dp', 'fsdp')), may hold values from 0 to 255
- master: float32 [6952960], P('fsdp'), may hold values from -2 to 3
- first_moment: float32 [6952960], P('fsdp'), may hold values from -0.008 to 0.008
- second_moment: float32 [6952960], P('fsdp'), may hold values from 0 to 0.000128, as said below
- average: float32 [6952960], P('fsdp'), may hold values from -2 to 3
Outputs:
- new_master: float32 [6952960], P('fsdp')
- new_first: float32 [6952960], P('fsdp')
- new_second: float32 [6952960], P('fsdp')
- new_average: float32 [6952960], P('fsdp')
- weight_copy: bfloat16 [6952960], P('fsdp')
- grad_norm: float32 [], replicated
- loss_sum: float32 [], replicated
- step_count: float32 [], replicated
The draws below stay inside these ranges and needn't reach their ends.
Inputs may be any that keep to these rules, and one draw needn't show every extreme that they name: Each frame's 8 tokens carry one id, the index of the first frame of its episode; every sequence of 6 frames begins an episode, and ids never fall inside a sequence. `valid_steps`: the last frame of every sequence is valid. `second_moment`: Positive.
All inputs are finite; a program needn't handle non-finite values.
Results may differ from the reference program's by a relative error of at most 0.014.
Values may be sent and summed in bfloat16 or wider, within the bound.
A program may use at most 320 MiB of HBM per device.

```python
import math
import jax
import jax.numpy as jnp
from jax import lax

D = 512
HEADS = 8
HD = 64
FF = 2048
E = 512
CIN = 1536
POS = 81
NT = 8
ACT = 11
BINS = 256
FRAMES_SEQ = 6
SEQ_DEV = 16
STEP = 10
FRAMES = 3072
P_SIZE = 6952960


def matrix_spreads():
    return [(E * 2 * CIN, 0.3 / math.sqrt(E)), (CIN * D, 1.0 / math.sqrt(CIN)), (D * NT, 1.0 / math.sqrt(D)), (3 * D * D, 1.0 / math.sqrt(D)), (D * D, 3.0 / math.sqrt(D)), (D * FF, 1.0 / math.sqrt(D)), (FF * D, 1.0 / math.sqrt(FF)), (D * ACT * BINS, 1.5 / math.sqrt(D))]


def spread_vector(gain_value):
    pieces = [jnp.full((amount,), spread, jnp.float32) for amount, spread in matrix_spreads()]
    pieces.append(jnp.full((4 * D,), gain_value, jnp.float32))
    return jnp.concatenate(pieces)


def weight_base(key):
    matrix_noise = jax.random.truncated_normal(key, -5.0, 5.0, (P_SIZE - 4 * D,), jnp.float32)
    matrices = matrix_noise * spread_vector(0.0)[:P_SIZE - 4 * D]
    rising = 0.6 + 1.2 * jnp.arange(D, dtype=jnp.float32) / (D - 1)
    wobble = jax.random.truncated_normal(jax.random.fold_in(key, 101), -3.0, 3.0, (4, D), jnp.float32)
    gain_rows = rising[None, :] * (1.0 + 0.1 * wobble)
    return jnp.concatenate([matrices, gain_rows.reshape(-1)])


def moment_scale():
    return jnp.concatenate([jnp.full((P_SIZE - 4 * D,), 0.0004, jnp.float32), jnp.full((4 * D,), 0.004, jnp.float32)])


def draw_master(key, part):
    shared = weight_base(key)
    return shared


def draw_average(key, part):
    shared = weight_base(key)
    key = jax.random.fold_in(key, 2)
    jitter = jax.random.truncated_normal(key, -5.0, 5.0, (P_SIZE,), jnp.float32)
    return shared + 0.05 * spread_vector(1.0) * jitter


def draw_first_moment(key, part):
    key = jax.random.fold_in(key, 4)
    size_key, sign_key = jax.random.split(key)
    magnitude = jnp.exp(jax.random.uniform(size_key, (P_SIZE,), jnp.float32, math.log(0.5), math.log(2.0)))
    signs = 2.0 * jax.random.randint(sign_key, (P_SIZE,), 0, 2).astype(jnp.float32) - 1.0
    return signs * magnitude * moment_scale()


def draw_second_moment(key, part):
    key = jax.random.fold_in(key, 5)
    factor = jnp.exp(jax.random.uniform(key, (P_SIZE,), jnp.float32, math.log(0.5), math.log(8.0)))
    scales = moment_scale()
    return factor * scales * scales


def draw_episode(key, part):
    key = jax.random.fold_in(key, 6)
    sequences = FRAMES // FRAMES_SEQ
    starts = jax.random.randint(key, (sequences, FRAMES_SEQ), 0, 3) == 0
    starts = starts.at[:, 0].set(True)
    starts = starts.at[sequences - 1, FRAMES_SEQ - 1].set(True)
    frame_index = jnp.arange(FRAMES, dtype=jnp.int32).reshape(sequences, FRAMES_SEQ)
    episode_start = lax.cummax(jnp.where(starts, frame_index, 0), axis=1)
    return jnp.repeat(episode_start.reshape(-1), NT)


def draw_valid_steps(key, part):
    key = jax.random.fold_in(key, 7)
    places = jnp.arange(FRAMES, dtype=jnp.int32)
    levels = jax.random.randint(key, (FRAMES,), 0, 1024)
    threshold = 128 + 768 * places // max(FRAMES - 1, 1)
    chosen = (levels < threshold) | (places % FRAMES_SEQ == FRAMES_SEQ - 1)
    return chosen.astype(jnp.int32)


def set_ends(drawn, stream_key, smallest, top_value):
    dims = drawn.shape
    spot = [jax.random.randint(jax.random.fold_in(stream_key, axis), (), 0, dims[axis]) for axis in range(len(dims))]
    drawn = drawn.at[tuple(spot)].set(smallest)
    longest = dims.index(max(dims))
    spot[longest] = (spot[longest] + 1) % dims[longest]
    return drawn.at[tuple(spot)].set(top_value)


def block_levels(rng, shape, cuts, low, top_value):
    def one(dim, shards_of):
        heights = jax.random.uniform(jax.random.fold_in(jax.random.fold_in(rng, 6), dim), (shards_of,), jnp.float32, low / len(cuts), top_value / len(cuts))
        return jnp.repeat(jnp.exp(heights), shape[dim] // shards_of).reshape((-1,) + (1,) * (len(shape) - dim - 1))

    level = one(*cuts[0])
    for cut in cuts[1:]:
        level = level * one(*cut)
    return level


def bell_draw(own_key, dims, width, bound, shards=(), kind=jnp.bfloat16):
    factor_of = block_levels(own_key, dims, shards, -0.22, 0.18) if shards else 1.0
    result = jax.random.normal(own_key, dims, jnp.float32) * width * factor_of
    return jnp.minimum(jnp.maximum(result, -bound), bound).astype(kind)


def setup_inputs(seed: int = 0) -> dict:
    seeds = jax.random.split(jax.random.key(seed), 10)
    return {
        "images": bell_draw(seeds[0], (FRAMES, POS, CIN), 1.0, 6.0, ((0, 32),)),
        "embedding": bell_draw(seeds[1], (FRAMES, E), 1.0, 6.0, ((0, 32),)),
        "episode": draw_episode(jax.random.fold_in(seeds[9], 71), 0),
        "valid_steps": draw_valid_steps(jax.random.fold_in(seeds[9], 71), 0),
        "targets": set_ends(jax.random.randint(seeds[4], (FRAMES, ACT), 0, BINS), jax.random.fold_in(seeds[4], 1), 0, BINS - 1).astype(jnp.int32),
        "master": draw_master(jax.random.fold_in(seeds[9], 71), 0),
        "first_moment": draw_first_moment(jax.random.fold_in(seeds[9], 71), 0),
        "second_moment": draw_second_moment(jax.random.fold_in(seeds[9], 71), 0),
        "average": draw_average(jax.random.fold_in(seeds[9], 71), 0),
    }


HIGHEST_PRECISION = lax.Precision.HIGHEST
MOMENT_DECAY = 0.5
LEARN_RATE = 0.02
WEIGHT_DECAY = 0.1
CLIP_NORM = 1.0
ADAM_EPSILON = 1e-08
AVERAGE_DECAY = 0.999

@jax.custom_vjp
def low(v):
    return lax.optimization_barrier(v.astype(jnp.bfloat16)).astype(jnp.float32)

@jax.custom_vjp
def low_back(v):
    return v

def low_keep(v):
    return (low(v), None)

def low_pass(kept, grad):
    return (grad,)

def back_keep(v):
    return (v, None)

def back_low(kept, grad):
    return (low(grad),)
low.defvjp(low_keep, low_pass)
low_back.defvjp(back_keep, back_low)

def layer_norm(values, scales):
    centre = lax.optimization_barrier(jnp.mean(values, axis=-1, keepdims=True))
    shifted = values - centre
    spread = lax.optimization_barrier(jnp.mean(shifted * shifted, axis=-1, keepdims=True))
    return shifted * lax.rsqrt(spread + 1e-05) * scales

def product(operand, matrix):
    return low_back(jnp.dot(low(operand), matrix, precision=HIGHEST_PRECISION))

def layout():
    return [(E, 2 * CIN), (CIN, D), (D, NT), (D, 3 * D), (D, D), (D, FF), (FF, D), (D, ACT * BINS), (4, D)]

def unpack(flat):
    pieces = []
    offset = 0
    for height, breadth in layout():
        pieces.append(flat[offset:offset + height * breadth].reshape(height, breadth))
        offset += height * breadth
    return pieces

def group_loss(flat, images, embedding, episode, valid_steps, targets):
    film_weight, conv_weight, learner_weight, triple_weight, output_weight, upward_weight, downward_weight, action_weight, norm_gains = unpack(flat)
    frames = images.shape[0]
    tokens = frames * NT
    shifts = product(embedding, film_weight)
    modulated = images * (1.0 + shifts[:, None, :CIN]) + shifts[:, None, CIN:]
    feature_grid = product(modulated.reshape(frames * POS, CIN), conv_weight)
    normed = layer_norm(feature_grid, norm_gains[0])
    maps = jax.nn.sigmoid(jnp.dot(normed, learner_weight, precision=HIGHEST_PRECISION))
    pooled = jnp.einsum('fpt,fpd->ftd', maps.reshape(frames, POS, NT), normed.reshape(frames, POS, D), precision=HIGHEST_PRECISION) / POS
    stream = pooled.reshape(tokens, D)
    triple = low(product(layer_norm(stream, norm_gains[1]), triple_weight))
    head_parts = triple.reshape(tokens, 3, HEADS, HD).transpose(1, 2, 0, 3)
    scores = low_back(jnp.einsum('hqd,hkd->hqk', head_parts[0], head_parts[1], precision=HIGHEST_PRECISION) * HD ** (-0.5))
    places = jnp.arange(tokens, dtype=jnp.int32)
    allowed = (episode[:, None] == episode[None, :]) & (places[None, :] <= places[:, None])
    scores = jnp.where(allowed[None], scores, -1e+30)
    shares = low(jax.nn.softmax(scores, axis=-1))
    attended = low_back(jnp.einsum('hqk,hkd->hqd', shares, head_parts[2], precision=HIGHEST_PRECISION))
    merged = attended.transpose(1, 0, 2).reshape(tokens, D)
    stream = stream + product(merged, output_weight)
    hidden = low(jax.nn.gelu(product(layer_norm(stream, norm_gains[2]), upward_weight)))
    stream = stream + product(hidden, downward_weight)
    final_rows = layer_norm(stream.reshape(frames, NT, D)[:, NT - 1], norm_gains[3])
    logits = product(final_rows, action_weight).reshape(frames, ACT, BINS)
    log_probs = jax.nn.log_softmax(logits, axis=-1)
    picked = jnp.take_along_axis(log_probs, targets[:, :, None], axis=-1)[:, :, 0]
    return -jnp.sum(valid_steps.astype(jnp.float32) * lax.optimization_barrier(jnp.sum(picked, axis=-1)))

def reference(images, embedding, episode, valid_steps, targets, master, first_moment, second_moment, average):
    weights = master.astype(jnp.bfloat16).astype(jnp.float32)
    group_frames = SEQ_DEV * FRAMES_SEQ
    groups = images.shape[0] // group_frames
    step_count = jnp.sum(valid_steps.astype(jnp.float32))
    inputs = (images.reshape(groups, group_frames, POS, CIN), embedding.reshape(groups, group_frames, E), episode.reshape(groups, group_frames * NT), valid_steps.reshape(groups, group_frames), targets.reshape(groups, group_frames, ACT))
    checked = jax.checkpoint(group_loss)

    def whole_loss(flat):

        def visit(running, block_inputs):
            part = checked(flat, block_inputs[0].astype(jnp.float32), block_inputs[1].astype(jnp.float32), block_inputs[2], block_inputs[3], block_inputs[4])
            return (running + part, None)
        summed, _ = lax.scan(visit, jnp.zeros((), jnp.float32), inputs)
        return (summed / step_count, summed)
    loss_value, pullback, loss_sum = jax.vjp(whole_loss, weights, has_aux=True)
    gradient, = pullback(jnp.ones((), jnp.float32))
    grad_norm = jnp.sqrt(jnp.sum(gradient * gradient))
    clipped = gradient * (CLIP_NORM / jnp.maximum(grad_norm, CLIP_NORM))
    new_first = MOMENT_DECAY * first_moment + (1.0 - MOMENT_DECAY) * clipped
    new_second = MOMENT_DECAY * second_moment + (1.0 - MOMENT_DECAY) * clipped * clipped
    correction = 1.0 - MOMENT_DECAY ** STEP
    new_master = master - LEARN_RATE * (new_first / correction / (jnp.sqrt(new_second / correction) + ADAM_EPSILON) + WEIGHT_DECAY * master)
    average_decay = min(AVERAGE_DECAY, (1.0 + STEP) / (10.0 + STEP))
    new_average = average_decay * average + (1.0 - average_decay) * new_master
    return (new_master, new_first, new_second, new_average, new_master.astype(jnp.bfloat16), grad_norm, loss_sum, step_count)
```

```python
import functools

import jax
import jax.numpy as jnp
from jax import lax
from jax.experimental import pallas as pl
from jax.experimental.pallas import tpu as pltpu
from jax.sharding import PartitionSpec as P

D = 512
HEADS = 8
HD = 64
FF = 2048
E = 512
CIN = 1536
POS = 81
NT = 8
ACT = 11
BINS = 256
STEP = 10
LANES = 128
GROUP = 16
CELLS = POS * GROUP
SLOTS = GROUP * NT

MOMENT_DECAY = 0.5
LEARN_RATE = 0.02
WEIGHT_DECAY = 0.1
CLIP_NORM = 1.0
ADAM_EPSILON = 1e-08
AVERAGE_DECAY = 0.999
BF = jnp.bfloat16
F32 = jnp.float32
MIB = 2**20

SHAPES = {
    "film": (E, 2 * CIN),
    "conv": (CIN, D),
    "learner": (D, NT),
    "triple": (D, 3 * D),
    "output": (D, D),
    "upward": (D, FF),
    "downward": (FF, D),
    "action": (D, ACT * BINS),
    "gains": (4, D),
}


def row_starts():
    starts, row = {}, 0
    for name, (height, breadth) in SHAPES.items():
        starts[name] = row
        row += height * breadth // LANES
    return starts, row


START, ROWS = row_starts()
FLAT_ROWS = ROWS + 16
HEAD_PART = START["triple"]


def mm(a, b):
    return jnp.dot(a, b, preferred_element_type=F32)


def mm_nt(a, b):
    return lax.dot_general(a, b, (((1,), (1,)), ((), ())), preferred_element_type=F32)


def mm_tn(a, b):
    return lax.dot_general(a, b, (((0,), (0,)), ((), ())), preferred_element_type=F32)


class Windows:
    def __init__(self, shards, shard_rows, size):
        self.shards, self.shard_rows, self.size = shards, shard_rows, size
        self.first = [shard_rows * k // 16 * 16 for k in range(shards)]

    def pieces(self, start, stop):
        inner, shared = [], []
        for k in range(self.shards):
            low, high = self.shard_rows * k, self.shard_rows * (k + 1)
            if k == self.shards - 1:
                high = (high + 15) // 16 * 16
            a, b = max(start, -(-low // 16) * 16), min(stop, high // 16 * 16)
            if a < b:
                inner.append((k, a - self.first[k], a, b - a))
            edge = low // 16 * 16
            if low % 16 and start <= edge < stop:
                shared.append((k - 1, edge - self.first[k - 1], k, edge - self.first[k], edge))
        return inner, shared

    def load(self, flat_ref, stage, edges, sem, parts):
        copies, fixes = [], []
        for start, stop, place in parts:
            inner, shared = self.pieces(start, stop)
            for k, offset, row, count in inner:
                copies.append(
                    pltpu.make_async_copy(
                        flat_ref.at[k, pl.ds(offset, count)],
                        stage.at[pl.ds(place + row - start, count)],
                        sem.at[len(copies)],
                    )
                )
            for k, offset, l, other, row in shared:
                for side, (window, at) in enumerate(((k, offset), (l, other))):
                    copies.append(
                        pltpu.make_async_copy(
                            flat_ref.at[window, pl.ds(at, 16)],
                            edges.at[len(fixes), side],
                            sem.at[len(copies)],
                        )
                    )
                fixes.append(place + row - start)
        for copy in copies:
            copy.start()
        for copy in copies:
            copy.wait()
        for index, row in enumerate(fixes):
            stage[pl.ds(row, 16), :] = edges[index, 0] + edges[index, 1]


def to_matrix(stage, place, spread, matrix, shape):
    height, breadth = shape
    wide = breadth // LANES
    rows = height * wide
    spread[pl.ds(0, rows), :] = stage[pl.ds(place, rows), :].astype(F32)
    for j in range(wide):
        matrix[:, LANES * j : LANES * (j + 1)] = spread[pl.ds(j, height, stride=wide), :].astype(BF)


def norm_rows(values):
    centre = jnp.mean(values, axis=-1, keepdims=True)
    shifted = values - centre
    inverse = lax.rsqrt(jnp.mean(shifted * shifted, axis=-1, keepdims=True) + 1e-05)
    return shifted * inverse, inverse


def norm_back(unit, inverse, gain, grad):
    scaled = grad * gain
    along = jnp.mean(scaled * unit, axis=-1, keepdims=True)
    return inverse * (scaled - jnp.mean(scaled, axis=-1, keepdims=True) - unit * along)


def own_frame(rows):
    frame = lax.broadcasted_iota(jnp.int32, (rows // GROUP, GROUP, SLOTS), 1).reshape(rows, SLOTS)
    return frame == lax.broadcasted_iota(jnp.int32, (rows, SLOTS), 1) // NT


def same_token():
    a = lax.broadcasted_iota(jnp.int32, (SLOTS, SLOTS), 0) % NT
    b = lax.broadcasted_iota(jnp.int32, (SLOTS, SLOTS), 1) % NT
    return (a == b).astype(BF)


def learner_mask():
    return own_frame(D)


def section_kernel(
    windows,
    images,
    embedding,
    flat,
    unit_out,
    inverse_out,
    pooled_out,
    shifts_out,
    conv_out,
    learner_out,
    gains_out,
    stage,
    spread,
    film,
    modulated,
    edges,
    sems,
):
    step = pl.program_id(0)

    @pl.when(step == 0)
    def _():
        learner_rows = HEAD_PART - START["learner"]
        windows.load(
            flat,
            stage,
            edges,
            sems,
            [(0, HEAD_PART, 0), (START["gains"], ROWS, HEAD_PART)],
        )
        to_matrix(stage, 0, spread, film, SHAPES["film"])
        shifts_out[...] = mm(embedding[...], film[...])
        to_matrix(stage, START["conv"], spread, conv_out, SHAPES["conv"])
        packed = stage[pl.ds(START["learner"], learner_rows), :].astype(F32)
        opened = jnp.broadcast_to(packed[:, None, :], (learner_rows, GROUP, LANES)).reshape(D, SLOTS)
        opened = jnp.where(learner_mask(), opened, 0.0).astype(BF)
        learner_out[...] = mm(opened, same_token()).astype(BF)
        gain_rows = stage[pl.ds(HEAD_PART, 16), :].astype(F32)
        for i in range(4):
            for j in range(4):
                gains_out[i : i + 1, LANES * j : LANES * (j + 1)] = gain_rows[4 * i + j : 4 * i + j + 1]

    here = pl.ds(pl.multiple_of(step * GROUP, GROUP), GROUP)
    scale = 1.0 + shifts_out[here, :CIN]
    offset = shifts_out[here, CIN:]
    modulated[...] = (images[...].astype(F32) * scale[None] + offset[None]).astype(BF).reshape(CELLS, CIN)
    unit, inverse = norm_rows(mm(modulated[...], conv_out[...]))
    unit_out[...] = unit.astype(BF)
    inverse_out[...] = inverse
    normed = (unit * gains_out[0:1, :]).astype(BF)
    maps = jax.nn.sigmoid(mm(normed, learner_out[...]))
    maps = jnp.where(own_frame(CELLS), maps, 0.0).astype(BF)
    pooled_out[...] = mm_tn(maps, normed) * (1.0 / POS)


def section(windows, images, embedding, flat):
    frames = images.shape[1]
    steps = frames // GROUP
    whole = lambda *shape: pl.BlockSpec(shape, lambda i: (0,) * len(shape))
    film_rows = SHAPES["film"][0] * SHAPES["film"][1] // LANES
    return pl.pallas_call(
        functools.partial(section_kernel, windows),
        grid=(steps,),
        in_specs=[
            pl.BlockSpec((POS, GROUP, CIN), lambda i: (0, i, 0)),
            whole(frames, E),
            pl.BlockSpec(memory_space=pl.ANY),
        ],
        out_specs=[
            pl.BlockSpec((CELLS, D), lambda i: (i, 0)),
            pl.BlockSpec((CELLS, 1), lambda i: (i, 0)),
            pl.BlockSpec((SLOTS, D), lambda i: (i, 0)),
            whole(frames, 2 * CIN),
            whole(CIN, D),
            whole(D, SLOTS),
            whole(4, D),
        ],
        out_shape=[
            jax.ShapeDtypeStruct((steps * CELLS, D), BF),
            jax.ShapeDtypeStruct((steps * CELLS, 1), F32),
            jax.ShapeDtypeStruct((frames * NT, D), F32),
            jax.ShapeDtypeStruct((frames, 2 * CIN), F32),
            jax.ShapeDtypeStruct((CIN, D), BF),
            jax.ShapeDtypeStruct((D, SLOTS), BF),
            jax.ShapeDtypeStruct((4, D), F32),
        ],
        scratch_shapes=[
            pltpu.VMEM((HEAD_PART + 16, LANES), BF),
            pltpu.VMEM((film_rows, LANES), F32),
            pltpu.VMEM(SHAPES["film"], BF),
            pltpu.VMEM((CELLS, CIN), BF),
            pltpu.VMEM((8, 2, 16, LANES), BF),
            pltpu.SemaphoreType.DMA((32,)),
        ],
        compiler_params=pltpu.CompilerParams(vmem_limit_bytes=60 * MIB),
        cost_estimate=pl.CostEstimate(
            flops=2 * frames * POS * CIN * D, bytes_accessed=frames * POS * CIN * 2, transcendentals=0
        ),
    )(images, embedding, flat)


def gelu_parts(x):
    inner = 0.7978845608028654 * (x + 0.044715 * x * x * x)
    bent = jnp.tanh(inner)
    value = 0.5 * x * (1.0 + bent)
    slope = 0.5 * (1.0 + bent) + 0.5 * x * (1.0 - bent * bent) * 0.7978845608028654 * (
        1.0 + 3.0 * 0.044715 * x * x
    )
    return value, slope


def layer_kernel(
    windows,
    start,
    flat,
    gains,
    episode_row,
    episode_last,
    valid,
    targets,
    grad_start,
    gradient,
    sums,
    stage,
    spread,
    triple,
    output,
    upward,
    downward,
    action,
    keys,
    values,
    grad_keys,
    grad_values,
    shares,
    first_normed,
    logits_back,
    edges,
    sems,
):
    tokens = start.shape[0]
    frames = tokens // NT
    place = {name: START[name] - HEAD_PART for name in SHAPES}
    windows.load(flat, stage, edges, sems, [(HEAD_PART, START["gains"], 0)])
    for name, matrix in (
        ("triple", triple),
        ("output", output),
        ("upward", upward),
        ("downward", downward),
        ("action", action),
    ):
        to_matrix(stage, place[name], spread, matrix, SHAPES[name])
    is_last = lax.broadcasted_iota(jnp.int32, (tokens, D), 0) % NT == NT - 1

    def take_last(rows):
        return jnp.sum(jnp.where(is_last, rows, 0.0).reshape(frames, NT, D), axis=1)

    def spread_last(rows):
        wide = jnp.broadcast_to(rows[:, None, :], (frames, NT, D)).reshape(tokens, D)
        return jnp.where(is_last, wide, 0.0)

    gain = [gains[i : i + 1, :] for i in range(4)]

    first_unit, first_inverse = norm_rows(start[...])
    first_normed[...] = (first_unit * gain[1]).astype(BF)
    last_start = take_last(start[...])
    last_unit, _ = norm_rows(last_start)
    last_normed = (last_unit * gain[1]).astype(BF)
    queries = mm(last_normed, triple[:, :D]).astype(BF)
    keys[...] = mm(first_normed[...], triple[:, D : 2 * D]).astype(BF)
    values[...] = mm(first_normed[...], triple[:, 2 * D :]).astype(BF)
    key_place = lax.broadcasted_iota(jnp.int32, (frames, tokens), 1)
    query_place = lax.broadcasted_iota(jnp.int32, (frames, tokens), 0) * NT + (NT - 1)
    allowed = (episode_last[...] == episode_row[...]) & (key_place <= query_place)
    attended = []
    for h in range(HEADS):
        own = slice(HD * h, HD * (h + 1))
        scores = mm_nt(queries[:, own], keys[:, own]) * HD ** (-0.5)
        scores = jnp.where(allowed, scores, -1e30)
        powers = jnp.exp(scores - jnp.max(scores, axis=-1, keepdims=True))
        part = powers / jnp.sum(powers, axis=-1, keepdims=True)
        shares[h] = part
        attended.append(mm(part.astype(BF), values[:, own]))
    merged = jnp.concatenate(attended, axis=1).astype(BF)
    middle = last_start + mm(merged, output[...])
    second_unit, second_inverse = norm_rows(middle)
    second_normed = (second_unit * gain[2]).astype(BF)
    activated, slope = gelu_parts(mm(second_normed, upward[...]))
    hidden = activated.astype(BF)
    end = middle + mm(hidden, downward[...])
    final_unit, final_inverse = norm_rows(end)
    final_rows = (final_unit * gain[3]).astype(BF)

    valid_flags = valid[...].astype(F32)
    bins = lax.broadcasted_iota(jnp.int32, (frames, BINS), 1)
    loss = jnp.zeros((frames, 1), F32)
    for a in range(ACT):
        own = slice(BINS * a, BINS * (a + 1))
        logits = mm(final_rows, action[:, own])
        shifted = logits - jnp.max(logits, axis=-1, keepdims=True)
        powers = jnp.exp(shifted)
        total = jnp.sum(powers, axis=-1, keepdims=True)
        hit = targets[:, a : a + 1] == bins
        loss += jnp.log(total) - jnp.sum(jnp.where(hit, shifted, 0.0), axis=-1, keepdims=True)
        logits_back[:, own] = ((powers / total - hit.astype(F32)) * valid_flags).astype(BF)
    place_row = lax.broadcasted_iota(jnp.int32, (8, LANES), 0)
    sums[...] = jnp.where(
        place_row == 0, jnp.sum(loss * valid_flags), jnp.where(place_row == 1, jnp.sum(valid_flags), 0.0)
    )

    def put(name, parts):
        height, breadth = SHAPES[name]
        wide = breadth // LANES
        rows = height * wide
        for j, part in parts:
            for i in range(part.shape[1] // LANES):
                spread[pl.ds(j + i, height, stride=wide), :] = part[:, LANES * i : LANES * (i + 1)]
        stage[pl.ds(place[name], rows), :] = spread[pl.ds(0, rows), :].astype(BF)

    def columns(left, right):
        for j in range(0, right.shape[1] // LANES, 2):
            yield j, mm_tn(left, right[:, LANES * j : LANES * (j + 2)])

    put("action", columns(final_rows, logits_back[...]))
    grad_final = mm_nt(logits_back[...], action[...])
    gain_final = jnp.sum(grad_final * final_unit, axis=0, keepdims=True)
    grad_last = norm_back(final_unit, final_inverse, gain[3], grad_final)
    rounded = grad_last.astype(BF)
    put("downward", columns(hidden, rounded))
    grad_upward = (mm_nt(rounded, downward[...]) * slope).astype(BF)
    put("upward", columns(second_normed, grad_upward))
    grad_second = mm_nt(grad_upward, upward[...])
    gain_second = jnp.sum(grad_second * second_unit, axis=0, keepdims=True)
    grad_last = grad_last + norm_back(second_unit, second_inverse, gain[2], grad_second)
    rounded = grad_last.astype(BF)
    put("output", columns(merged, rounded))
    grad_attended = mm_nt(rounded, output[...]).astype(BF)
    grad_queries = []
    for h in range(HEADS):
        own = slice(HD * h, HD * (h + 1))
        part = shares[h]
        grad_shares = mm_nt(grad_attended[:, own], values[:, own])
        grad_values[:, own] = mm_tn(part.astype(BF), grad_attended[:, own]).astype(BF)
        grad_scores = part * (grad_shares - jnp.sum(grad_shares * part, axis=-1, keepdims=True))
        grad_scores = grad_scores.astype(BF)
        grad_queries.append(mm(grad_scores, keys[:, own]) * HD ** (-0.5))
        grad_keys[:, own] = (mm_tn(grad_scores, queries[:, own]) * HD ** (-0.5)).astype(BF)
    grad_queries = jnp.concatenate(grad_queries, axis=1).astype(BF)

    def triple_parts():
        yield from columns(last_normed, grad_queries)
        for j, part in columns(first_normed[...], grad_keys[...]):
            yield j + D // LANES, part
        for j, part in columns(first_normed[...], grad_values[...]):
            yield j + 2 * D // LANES, part

    put("triple", triple_parts())
    grad_start[...] = (
        mm_nt(grad_keys[...], triple[:, D : 2 * D])
        + mm_nt(grad_values[...], triple[:, 2 * D :])
        + spread_last(mm_nt(grad_queries, triple[:, :D]))
    )
    grad_first = grad_start[...]
    gain_first = jnp.sum(grad_first * first_unit, axis=0, keepdims=True)
    grad_start[...] = norm_back(first_unit, first_inverse, gain[1], grad_first) + spread_last(grad_last)

    rows = []
    for part in (jnp.zeros((1, D), F32), gain_first, gain_second, gain_final):
        rows += [part[:, LANES * j : LANES * (j + 1)] for j in range(4)]
    stage[pl.ds(place["gains"], 16), :] = jnp.concatenate(rows, axis=0).astype(BF)
    out = pltpu.make_async_copy(stage, gradient, sems.at[0])
    out.start()
    out.wait()


def layer(windows, start, flat, gains, episode, valid, targets):
    tokens = start.shape[0]
    frames = tokens // NT
    vmem = pl.BlockSpec(memory_space=pltpu.VMEM)
    anywhere = pl.BlockSpec(memory_space=pl.ANY)
    rows = ROWS - HEAD_PART
    return pl.pallas_call(
        functools.partial(layer_kernel, windows),
        in_specs=[vmem, anywhere] + [vmem] * 5,
        out_specs=[vmem, anywhere, vmem],
        out_shape=[
            jax.ShapeDtypeStruct((tokens, D), F32),
            jax.ShapeDtypeStruct((rows, LANES), BF),
            jax.ShapeDtypeStruct((8, LANES), F32),
        ],
        scratch_shapes=[
            pltpu.VMEM((rows, LANES), BF),
            pltpu.VMEM((SHAPES["action"][0] * SHAPES["action"][1] // LANES, LANES), F32),
            pltpu.VMEM(SHAPES["triple"], BF),
            pltpu.VMEM(SHAPES["output"], BF),
            pltpu.VMEM(SHAPES["upward"], BF),
            pltpu.VMEM(SHAPES["downward"], BF),
            pltpu.VMEM(SHAPES["action"], BF),
            pltpu.VMEM((tokens, D), BF),
            pltpu.VMEM((tokens, D), BF),
            pltpu.VMEM((tokens, D), BF),
            pltpu.VMEM((tokens, D), BF),
            pltpu.VMEM((HEADS, frames, tokens), F32),
            pltpu.VMEM((tokens, D), BF),
            pltpu.VMEM((frames, ACT * BINS), BF),
            pltpu.VMEM((8, 2, 16, LANES), BF),
            pltpu.SemaphoreType.DMA((32,)),
        ],
        compiler_params=pltpu.CompilerParams(vmem_limit_bytes=60 * MIB),
    )(
        start,
        flat,
        gains,
        episode.reshape(1, tokens),
        episode.reshape(frames, NT)[:, NT - 1 :],
        valid.reshape(frames, 1),
        targets,
    )


BLOCK = 256


def section_back_kernel(
    images,
    embedding,
    shifts,
    unit,
    inverse,
    grad_start,
    conv,
    learner,
    gains,
    gradient,
    gain_out,
    grad_grid,
    grad_sum,
    learner_sum,
    gain_sum,
    modulated,
    grad_scale,
    conv_sum,
    spread,
    film_spread,
    stage,
    sems,
):
    step = pl.program_id(0)
    steps = pl.num_programs(0)
    frames = embedding.shape[0]
    groups = frames // GROUP
    flat_conv = START["conv"]

    @pl.when(step == 0)
    def _():
        learner_sum[...] = jnp.zeros_like(learner_sum)
        gain_sum[...] = jnp.zeros_like(gain_sum)

        @pl.loop(0, groups)
        def _(g):
            rows = pl.ds(pl.multiple_of(g * CELLS, 16), CELLS)
            here = unit[rows, :].astype(F32)
            normed = (here * gains[0:1, :]).astype(BF)
            maps = jax.nn.sigmoid(mm(normed, learner[...]))
            mask = own_frame(CELLS)
            tokens = (grad_start[pl.ds(pl.multiple_of(g * SLOTS, SLOTS), SLOTS), :] * (1.0 / POS)).astype(BF)
            grad_maps = mm_nt(normed, tokens)
            grad_logit = jnp.where(mask, grad_maps * maps * (1.0 - maps), 0.0).astype(BF)
            maps = jnp.where(mask, maps, 0.0).astype(BF)
            grad_normed = mm(maps, tokens) + mm_nt(grad_logit, learner[...])
            learner_sum[...] += mm_tn(normed, grad_logit)
            gain_sum[...] += jnp.sum(grad_normed * here, axis=0, keepdims=True)
            back = norm_back(here, inverse[rows, :], gains[0:1, :], grad_normed).astype(BF)
            grad_grid[rows, :] = back
            grad_sum[pl.ds(pl.multiple_of(g * GROUP, GROUP), GROUP), :] = jnp.sum(
                back.astype(F32).reshape(POS, GROUP, D), axis=0
            )

        total = learner_sum[...]
        high = total.astype(BF)
        token = same_token()
        spread_learner = mm(high, token) + mm((total - high.astype(F32)).astype(BF), token)
        spread_learner = jnp.where(learner_mask(), spread_learner, 0.0)
        stage[pl.ds(START["learner"], D * NT // LANES), :] = jnp.sum(
            spread_learner.reshape(D * NT // LANES, GROUP, LANES), axis=1
        ).astype(BF)
        gain_out[...] = gain_sum[...]

    channels = pl.ds(pl.multiple_of(step * BLOCK, BLOCK), BLOCK)
    weights = conv[channels, :]

    conv_sum[...] = jnp.zeros_like(conv_sum)
    for g in range(groups):
        rows = pl.ds(g * CELLS, CELLS)
        here = pl.ds(g * GROUP, GROUP)
        scale = 1.0 + shifts[0, here, :]
        offset = shifts[1, here, :]
        cells = images[:, here, :].astype(F32)
        modulated[...] = (cells * scale[None] + offset[None]).astype(BF).reshape(CELLS, BLOCK)
        back = grad_grid[rows, :]
        conv_sum[...] += mm_tn(modulated[...], back)
        grad_modulated = mm_nt(back, weights).reshape(POS, GROUP, BLOCK)
        grad_scale[here, :] = jnp.sum(grad_modulated * cells, axis=0)
    total = grad_sum[...]
    high = total.astype(BF)
    grad_offset = mm_nt(high, weights) + mm_nt((total - high.astype(F32)).astype(BF), weights)

    wide = D // LANES
    for j in range(wide):
        spread[pl.ds(j, BLOCK, stride=wide), :] = conv_sum[:, LANES * j : LANES * (j + 1)]
    stage[pl.ds(pl.multiple_of(flat_conv + step * BLOCK * wide, 16), BLOCK * wide), :] = spread[...].astype(BF)
    film_wide = 2 * CIN // LANES
    for side, grad in enumerate((grad_scale[...], grad_offset)):
        part = mm_tn(embedding[...], grad.astype(BF))
        for i in range(BLOCK // LANES):
            column = side * (CIN // LANES) + step * (BLOCK // LANES) + i
            film_spread[pl.ds(column, E, stride=film_wide), :] = part[:, LANES * i : LANES * (i + 1)]

    @pl.when(step == steps - 1)
    def _():
        stage[pl.ds(0, flat_conv), :] = film_spread[...].astype(BF)
        out = pltpu.make_async_copy(stage, gradient, sems.at[0])
        out.start()
        out.wait()


def section_back(images, embedding, shifts, unit, inverse, grad_start, conv, learner, gains):
    frames = embedding.shape[0]
    steps = CIN // BLOCK
    whole = lambda *shape: pl.BlockSpec(shape, lambda i: (0,) * len(shape))
    return pl.pallas_call(
        section_back_kernel,
        grid=(steps,),
        in_specs=[
            pl.BlockSpec((POS, frames, BLOCK), lambda i: (0, 0, i)),
            whole(frames, E),
            pl.BlockSpec((2, frames, BLOCK), lambda i: (0, 0, i)),
            whole(frames * POS, D),
            whole(frames * POS, 1),
            whole(frames * NT, D),
            whole(CIN, D),
            whole(D, SLOTS),
            whole(4, D),
        ],
        out_specs=[pl.BlockSpec(memory_space=pl.ANY), whole(1, D)],
        out_shape=[
            jax.ShapeDtypeStruct((HEAD_PART, LANES), BF),
            jax.ShapeDtypeStruct((1, D), F32),
        ],
        scratch_shapes=[
            pltpu.VMEM((frames * POS, D), BF),
            pltpu.VMEM((frames, D), F32),
            pltpu.VMEM((D, SLOTS), F32),
            pltpu.VMEM((1, D), F32),
            pltpu.VMEM((CELLS, BLOCK), BF),
            pltpu.VMEM((frames, BLOCK), F32),
            pltpu.VMEM((BLOCK, D), F32),
            pltpu.VMEM((BLOCK * D // LANES, LANES), F32),
            pltpu.VMEM((START["conv"], LANES), F32),
            pltpu.VMEM((HEAD_PART, LANES), BF),
            pltpu.SemaphoreType.DMA((1,)),
        ],
        compiler_params=pltpu.CompilerParams(vmem_limit_bytes=62 * MIB),
        cost_estimate=pl.CostEstimate(
            flops=4 * frames * POS * CIN * D, bytes_accessed=frames * POS * CIN * 2, transcendentals=0
        ),
    )(
        images,
        embedding,
        shifts.reshape(frames, 2, CIN).transpose(1, 0, 2),
        unit,
        inverse,
        grad_start,
        conv,
        learner,
        gains,
    )


def on_device(
    images, embedding, episode, valid_steps, targets, master, first_moment, second_moment, average
):
    images = images.transpose(1, 0, 2)
    own = master.astype(BF)
    whole_flat = lax.all_gather(own, "fsdp", axis=0, tiled=True)
    flat = jnp.pad(whole_flat.reshape(ROWS, LANES), ((0, FLAT_ROWS - ROWS), (0, 0)))[None]
    windows = Windows(1, ROWS, FLAT_ROWS)

    unit, inverse, start, shifts, conv, learner, gains = section(windows, images, embedding, flat)
    grad_start, late_gradient, sums = layer(windows, start, flat, gains, episode, valid_steps, targets)
    early_gradient, gain_grid = section_back(
        images, embedding, shifts, unit, inverse, grad_start, conv, learner, gains
    )
    late = late_gradient.at[START["gains"] - HEAD_PART : START["gains"] - HEAD_PART + 4].set(
        gain_grid.reshape(4, LANES).astype(BF)
    )
    gradient = jnp.concatenate([early_gradient, late]).reshape(-1)
    loss_sum, step_count = lax.psum((sums[0, 0], sums[1, 0]), ("dp", "fsdp"))
    partial_shard = lax.psum_scatter(gradient, "fsdp", scatter_dimension=0, tiled=True)
    grad_shard = lax.psum(partial_shard.astype(F32), "dp") / step_count
    squares = lax.psum(jnp.sum(grad_shard * grad_shard), "fsdp")
    grad_norm = jnp.sqrt(squares)
    clipped = grad_shard * (CLIP_NORM / jnp.maximum(grad_norm, CLIP_NORM))
    new_first = MOMENT_DECAY * first_moment + (1.0 - MOMENT_DECAY) * clipped
    new_second = MOMENT_DECAY * second_moment + (1.0 - MOMENT_DECAY) * clipped * clipped
    correction = 1.0 - MOMENT_DECAY**STEP
    new_master = master - LEARN_RATE * (
        new_first / correction / (jnp.sqrt(new_second / correction) + ADAM_EPSILON)
        + WEIGHT_DECAY * master
    )
    average_decay = min(AVERAGE_DECAY, (1.0 + STEP) / (10.0 + STEP))
    new_average = average_decay * average + (1.0 - average_decay) * new_master
    return (
        new_master,
        new_first,
        new_second,
        new_average,
        new_master.astype(BF),
        grad_norm,
        loss_sum,
        step_count,
    )


def solution(mesh):
    in_specs = (
        P(("dp", "fsdp"), None, None),
        P(("dp", "fsdp"), None),
        P(("dp", "fsdp")),
        P(("dp", "fsdp")),
        P(("dp", "fsdp"), None),
        P("fsdp"),
        P("fsdp"),
        P("fsdp"),
        P("fsdp"),
    )
    out_specs = (P("fsdp"), P("fsdp"), P("fsdp"), P("fsdp"), P("fsdp"), P(), P(), P())
    return jax.shard_map(
        on_device, mesh=mesh, in_specs=in_specs, out_specs=out_specs, check_vma=False
    )
```

```python
import functools

import jax
import jax.numpy as jnp
from jax import lax
from jax.experimental import pallas as pl
from jax.experimental.pallas import tpu as pltpu
from jax.sharding import PartitionSpec as P

D = 512
HEADS = 8
HD = 64
FF = 2048
E = 512
CIN = 1536
POS = 81
NT = 8
ACT = 11
BINS = 256
STEP = 10
LANES = 128
GROUP = 16
CELLS = POS * GROUP
SLOTS = GROUP * NT

MOMENT_DECAY = 0.5
LEARN_RATE = 0.02
WEIGHT_DECAY = 0.1
CLIP_NORM = 1.0
ADAM_EPSILON = 1e-08
AVERAGE_DECAY = 0.999
BF = jnp.bfloat16
F32 = jnp.float32
MIB = 2**20

SHAPES = {
    "film": (E, 2 * CIN),
    "conv": (CIN, D),
    "learner": (D, NT),
    "triple": (D, 3 * D),
    "output": (D, D),
    "upward": (D, FF),
    "downward": (FF, D),
    "action": (D, ACT * BINS),
    "gains": (4, D),
}


def row_starts():
    starts, row = {}, 0
    for name, (height, breadth) in SHAPES.items():
        starts[name] = row
        row += height * breadth // LANES
    return starts, row


START, ROWS = row_starts()
FLAT_ROWS = ROWS + 16
HEAD_PART = START["triple"]


def mm(a, b):
    return jnp.dot(a, b, preferred_element_type=F32)


def mm_nt(a, b):
    return lax.dot_general(a, b, (((1,), (1,)), ((), ())), preferred_element_type=F32)


def mm_tn(a, b):
    return lax.dot_general(a, b, (((0,), (0,)), ((), ())), preferred_element_type=F32)


class Windows:
    def __init__(self, shards, shard_rows, size):
        self.shards, self.shard_rows, self.size = shards, shard_rows, size
        self.first = [shard_rows * k // 16 * 16 for k in range(shards)]

    def pieces(self, start, stop):
        inner, shared = [], []
        for k in range(self.shards):
            low, high = self.shard_rows * k, self.shard_rows * (k + 1)
            if k == self.shards - 1:
                high = (high + 15) // 16 * 16
            a, b = max(start, -(-low // 16) * 16), min(stop, high // 16 * 16)
            if a < b:
                inner.append((k, a - self.first[k], a, b - a))
            edge = low // 16 * 16
            if low % 16 and start <= edge < stop:
                shared.append((k - 1, edge - self.first[k - 1], k, edge - self.first[k], edge))
        return inner, shared

    def load(self, flat_ref, stage, edges, sem, parts):
        copies, fixes = [], []
        for start, stop, place in parts:
            inner, shared = self.pieces(start, stop)
            for k, offset, row, count in inner:
                copies.append(
                    pltpu.make_async_copy(
                        flat_ref.at[k, pl.ds(offset, count)],
                        stage.at[pl.ds(place + row - start, count)],
                        sem.at[len(copies)],
                    )
                )
            for k, offset, l, other, row in shared:
                for side, (window, at) in enumerate(((k, offset), (l, other))):
                    copies.append(
                        pltpu.make_async_copy(
                            flat_ref.at[window, pl.ds(at, 16)],
                            edges.at[len(fixes), side],
                            sem.at[len(copies)],
                        )
                    )
                fixes.append(place + row - start)
        for copy in copies:
            copy.start()
        for copy in copies:
            copy.wait()
        for index, row in enumerate(fixes):
            stage[pl.ds(row, 16), :] = edges[index, 0] + edges[index, 1]


MESH = pl.DeviceIdType.MESH
CHUNK = 384
CHUNKS = 18
WINDOW = CHUNK * CHUNKS
CARRIED = 2 * CHUNKS // 3
TRADED = CHUNKS // 3
NEEDED = 13
READY, READY_TRADED = 9, 4
SENDS = ((0, 3, 2), (0, 1, 3), (0, 1, 2), (3, 1, 2))


def fits_ring(replicas, shards, shard_size):
    return shards == 8 and replicas % 2 == 0 and shard_size % LANES == 0 and shard_size <= LANES * (WINDOW - 16)


def gray(place):
    return place + (place // 2) * (1 - 2 * (place % 2))


class Ring:
    def __init__(self):
        self.me = lax.axis_index("fsdp")
        self.core = self.me % 2
        self.place = self.flip(gray(self.me // 2))
        self.replica = lax.axis_index("dp")
        self.half = self.replica % 2
        self.sibling = self.me + 1 - 2 * self.core
        self.after = self.device(self.place + 1)
        self.before = self.device(self.place + 3)
        self.partner = self.replica + 1 - 2 * self.half
        self.shards = lax.axis_size("fsdp")
        self.others = [(self.me + 1 + index) % self.shards for index in range(self.shards - 1)]

    def flip(self, place):
        return (place + self.core * (4 - 2 * place)) % 4

    def device(self, place):
        return gray(self.flip(place % 4)) * 2 + self.core

    def pick(self, table, place):
        found = jnp.int32(0)
        for index, value in enumerate(table):
            found = found + jnp.where(place == index, value, 0)
        return found


class Gather:
    def __init__(self, own, whole, gain_rows, around, straight, across, trade, own_sems):
        self.ring, self.own, self.whole, self.gain_rows = Ring(), own, whole, gain_rows
        self.around_sems, self.straight_sems, self.across_sems, self.trade_sems, self.own_sems = (
            around,
            straight,
            across,
            trade,
            own_sems,
        )
        core, place = self.ring.core, self.ring.place
        self.first = [CARRIED, jnp.where(core == 0, READY, 0), 0, 0]
        self.first_traded = [TRADED, jnp.where(core == 0, READY_TRADED, 0), 0, 0]

    def greet(self):
        barrier = pltpu.get_barrier_semaphore()
        for device in [{"fsdp": other} for other in self.ring.others] + [{"dp": self.ring.partner}]:
            pl.semaphore_signal(barrier, inc=1, device_id=device, device_id_type=MESH)
        pl.semaphore_wait(barrier, self.ring.shards)

    def gain_copy(self, index):
        return pltpu.make_async_remote_copy(
            src_ref=self.gain_rows,
            dst_ref=self.gain_rows,
            send_sem=self.own_sems.at[3 + index],
            recv_sem=self.own_sems.at[2],
            device_id={"fsdp": self.ring.others[index]},
            device_id_type=MESH,
        )

    def send_gains(self, place):
        @pl.when(self.ring.me == self.ring.shards - 1)
        def _():
            self.gain_rows[...] = self.own[pl.ds(place, 16), :]
            for index in range(self.ring.shards - 1):
                self.gain_copy(index).start()

    def take_gains(self):
        last = self.ring.me == self.ring.shards - 1

        @pl.when(last)
        def _():
            for index in range(self.ring.shards - 1):
                self.gain_copy(index).wait_send()

        @pl.when(jnp.logical_not(last))
        def _():
            self.gain_copy(0).wait_recv()

    def carried(self, j):
        return (j // 2) * 3 + (j % 2) * (1 + self.ring.half)

    def rows(self, i):
        return pl.ds(pl.multiple_of(i * CHUNK, 16), CHUNK)

    def copy(self, window, i, send_sem, recv_sem, device, own=False):
        source = self.own.at[self.rows(i)] if own else self.whole.at[window, self.rows(i)]
        return pltpu.make_async_remote_copy(
            src_ref=source,
            dst_ref=self.whole.at[window, self.rows(i)],
            send_sem=send_sem,
            recv_sem=recv_sem,
            device_id=device,
            device_id_type=MESH,
        )

    def around(self, origin, j, own=False):
        sems = self.around_sems
        return self.copy(
            self.ring.me if own else self.ring.device(origin),
            self.carried(j),
            sems.at[0, origin, j],
            sems.at[1, origin, j],
            {"fsdp": self.ring.after},
            own,
        )

    def straight(self, hops, j):
        place = self.ring.place
        return self.copy(
            self.ring.me,
            self.carried(j),
            self.straight_sems.at[hops - 1, j],
            self.around_sems.at[1, place, j],
            {"fsdp": self.ring.device(place + hops)},
            own=True,
        )

    def across(self, origin, i):
        sems = self.across_sems
        return self.copy(
            self.ring.device(origin), i, sems.at[0, origin, i], sems.at[1, origin, i], {"fsdp": self.ring.sibling}
        )

    def trade(self, origin, j, half):
        sems = self.trade_sems
        return self.copy(
            self.ring.device(origin),
            3 * j + 1 + half,
            sems.at[0, origin, j],
            sems.at[1, origin, j],
            {"dp": self.ring.partner},
        )

    def own_copies(self):
        ring = self.ring
        keep = pltpu.make_async_copy(self.own, self.whole.at[ring.me], self.own_sems.at[10])
        give = pltpu.make_async_remote_copy(
            src_ref=self.own,
            dst_ref=self.whole.at[ring.me],
            send_sem=self.own_sems.at[1],
            recv_sem=self.own_sems.at[0],
            device_id={"fsdp": ring.sibling},
            device_id_type=MESH,
        )
        return keep, give

    def take(self, origin, low, high, forward):
        low = jnp.where(self.ring.place == origin, high, low)

        @pl.loop(low, high)
        def _(j):
            self.around(origin, j).wait_recv()
            if forward:

                @pl.when(origin != (self.ring.place + 1) % 4)
                def _():
                    self.around(origin, j).start()

            @pl.when(j % 2 == 1)
            def _():
                self.trade(origin, j // 2, self.ring.half).start()

            self.across(origin, self.carried(j)).start()

    def take_traded(self, origin, low, high):
        other = 1 - self.ring.half
        low = jnp.where(self.ring.place == origin, high, low)

        @pl.loop(low, high)
        def _(j):
            self.trade(origin, j, other).wait_recv()
            self.across(origin, 3 * j + 1 + other).start()

    def wait_across(self, origin, low, high):
        sibling_place = (4 - self.ring.place) % 4
        low = jnp.where(sibling_place == origin, high, low)

        @pl.loop(low, high)
        def _(i):
            self.across(origin, i).wait_recv()

    def begin(self, gain_place):
        ring = self.ring
        self.greet()
        self.send_gains(gain_place)
        for origin in (0, 1):

            @pl.when(ring.place == origin)
            def _():
                @pl.loop(0, self.first[origin])
                def _(j):
                    self.around(origin, j, own=True).start()

        keep, give = self.own_copies()
        keep.start()
        give.start()
        for origin in (1, 0):
            self.take(origin, 0, self.first[origin], True)

        @pl.when(ring.place > 0)
        def _():
            @pl.loop(jnp.where(ring.place == 1, self.first[1], 0), CARRIED)
            def _(j):
                for hops in (1, 2, 3):
                    self.straight(hops, j).start()

        for origin in (1, 0):
            self.take_traded(origin, 0, self.first_traded[origin])
        self.take_gains()
        keep.wait()
        give.wait_recv()
        self.wait_across(0, 0, CHUNKS)
        self.wait_across(1, 0, jnp.where(ring.core == 1, NEEDED, 0))

    def go_on(self, step, steps):
        parts = steps - 1

        def bounds(at, count, first):
            return first + jnp.clip(at, 0, parts) * (count - first) // parts

        for origin in (1, 2, 3):
            first = self.first[origin]
            self.take(origin, bounds(step - 1, CARRIED, first), bounds(step, CARRIED, first), False)
        for origin in (1, 2, 3):
            first = self.first_traded[origin]
            self.take_traded(
                origin,
                bounds(step - 2, TRADED, first),
                jnp.where(step == steps - 1, TRADED, bounds(step - 1, TRADED, first)),
            )

        @pl.when(step == steps - 1)
        def _():
            self.finish()

    def finish(self):
        place = self.ring.place
        self.wait_across(1, jnp.where(self.ring.core == 1, NEEDED, 0), CHUNKS)
        self.wait_across(2, 0, CHUNKS)
        self.wait_across(3, 0, CHUNKS)
        self.own_copies()[1].wait_send()
        for origin in range(4):
            sent = jnp.where((place + 1) % 4 == origin, 0, self.first[origin])

            @pl.loop(0, sent)
            def _(j):
                self.around(origin, j).wait_send()

            @pl.loop(0, jnp.where(place == origin, 0, TRADED))
            def _(j):
                self.trade(origin, j, self.ring.half).wait_send()

            @pl.loop(0, jnp.where(place == origin, 0, CHUNKS))
            def _(i):
                self.across(origin, i).wait_send()

        @pl.when(place > 0)
        def _():
            @pl.loop(jnp.where(place == 1, self.first[1], 0), CARRIED)
            def _(j):
                for hops in (1, 2, 3):
                    self.straight(hops, j).wait_send()


GATHER_SCRATCH = [
    pltpu.VMEM((WINDOW, LANES), BF),
    pltpu.VMEM((16, LANES), BF),
    pltpu.SemaphoreType.DMA((2, 4, CARRIED)),
    pltpu.SemaphoreType.DMA((3, CARRIED)),
    pltpu.SemaphoreType.DMA((2, 4, CHUNKS)),
    pltpu.SemaphoreType.DMA((2, 4, TRADED)),
    pltpu.SemaphoreType.DMA((11,)),
]


def to_matrix(stage, place, spread, matrix, shape):
    height, breadth = shape
    wide = breadth // LANES
    rows = height * wide
    spread[pl.ds(0, rows), :] = stage[pl.ds(place, rows), :].astype(F32)
    for j in range(wide):
        matrix[:, LANES * j : LANES * (j + 1)] = spread[pl.ds(j, height, stride=wide), :].astype(BF)


def norm_rows(values):
    centre = jnp.mean(values, axis=-1, keepdims=True)
    shifted = values - centre
    inverse = lax.rsqrt(jnp.mean(shifted * shifted, axis=-1, keepdims=True) + 1e-05)
    return shifted * inverse, inverse


def norm_back(unit, inverse, gain, grad):
    scaled = grad * gain
    along = jnp.mean(scaled * unit, axis=-1, keepdims=True)
    return inverse * (scaled - jnp.mean(scaled, axis=-1, keepdims=True) - unit * along)


def own_frame(rows):
    frame = lax.broadcasted_iota(jnp.int32, (rows // GROUP, GROUP, SLOTS), 1).reshape(rows, SLOTS)
    return frame == lax.broadcasted_iota(jnp.int32, (rows, SLOTS), 1) // NT


def same_token():
    a = lax.broadcasted_iota(jnp.int32, (SLOTS, SLOTS), 0) % NT
    b = lax.broadcasted_iota(jnp.int32, (SLOTS, SLOTS), 1) % NT
    return (a == b).astype(BF)


def learner_mask():
    return own_frame(D)


def section_kernel(
    windows,
    images,
    embedding,
    flat,
    unit_out,
    inverse_out,
    pooled_out,
    shifts_out,
    conv_out,
    learner_out,
    gains_out,
    *rest,
):
    step = pl.program_id(0)
    if windows.shards > 1:
        master = flat
        flat, stage, spread, film, modulated, edges, sems, own, *gather_sems = rest
        gather = Gather(own, flat, *gather_sems)
    else:
        gather = None
        stage, spread, film, modulated, edges, sems = rest

    @pl.when(step == 0)
    def _():
        if gather:
            rows = master.shape[0]
            spread[pl.ds(0, 16), :] = jnp.zeros((16, LANES), F32)
            tail = rows // 16 * 16
            spread[pl.ds(tail, WINDOW - tail), :] = jnp.zeros((WINDOW - tail, LANES), F32)
            spread[pl.ds(gather.ring.me * rows % 16, rows), :] = master[...]
            own[...] = spread[pl.ds(0, WINDOW), :].astype(BF)
            gather.begin(START["gains"] - windows.first[-1])
        learner_rows = HEAD_PART - START["learner"]
        parts = [(0, HEAD_PART, 0)]
        if gather is None:
            parts.append((START["gains"], ROWS, HEAD_PART))
        windows.load(flat, stage, edges, sems, parts)
        if gather:
            stage[pl.ds(HEAD_PART, 16), :] = gather.gain_rows[...]
        to_matrix(stage, 0, spread, film, SHAPES["film"])
        shifts_out[...] = mm(embedding[...], film[...])
        to_matrix(stage, START["conv"], spread, conv_out, SHAPES["conv"])
        packed = stage[pl.ds(START["learner"], learner_rows), :].astype(F32)
        opened = jnp.broadcast_to(packed[:, None, :], (learner_rows, GROUP, LANES)).reshape(D, SLOTS)
        opened = jnp.where(learner_mask(), opened, 0.0).astype(BF)
        learner_out[...] = mm(opened, same_token()).astype(BF)
        gain_rows = stage[pl.ds(HEAD_PART, 16), :].astype(F32)
        for i in range(4):
            for j in range(4):
                gains_out[i : i + 1, LANES * j : LANES * (j + 1)] = gain_rows[4 * i + j : 4 * i + j + 1]

    here = pl.ds(pl.multiple_of(step * GROUP, GROUP), GROUP)
    scale = 1.0 + shifts_out[here, :CIN]
    offset = shifts_out[here, CIN:]
    modulated[...] = (images[...].astype(F32) * scale[None] + offset[None]).astype(BF).reshape(CELLS, CIN)
    unit, inverse = norm_rows(mm(modulated[...], conv_out[...]))
    unit_out[...] = unit.astype(BF)
    inverse_out[...] = inverse
    normed = (unit * gains_out[0:1, :]).astype(BF)
    maps = jax.nn.sigmoid(mm(normed, learner_out[...]))
    maps = jnp.where(own_frame(CELLS), maps, 0.0).astype(BF)
    pooled_out[...] = mm_tn(maps, normed) * (1.0 / POS)
    if gather:
        gather.go_on(step, pl.num_programs(0))


def section(windows, images, embedding, flat):
    frames = images.shape[1]
    steps = frames // GROUP
    whole = lambda *shape: pl.BlockSpec(shape, lambda i: (0,) * len(shape))
    gathers = windows.shards > 1
    film_rows = SHAPES["film"][0] * SHAPES["film"][1] // LANES
    return pl.pallas_call(
        functools.partial(section_kernel, windows),
        grid=(steps,),
        in_specs=[
            pl.BlockSpec((POS, GROUP, CIN), lambda i: (0, i, 0)),
            whole(frames, E),
            whole(*flat.shape) if gathers else pl.BlockSpec(memory_space=pl.ANY),
        ],
        out_specs=[
            pl.BlockSpec((CELLS, D), lambda i: (i, 0)),
            pl.BlockSpec((CELLS, 1), lambda i: (i, 0)),
            pl.BlockSpec((SLOTS, D), lambda i: (i, 0)),
            whole(frames, 2 * CIN),
            whole(CIN, D),
            whole(D, SLOTS),
            whole(4, D),
        ]
        + [pl.BlockSpec(memory_space=pl.ANY)] * gathers,
        out_shape=[
            jax.ShapeDtypeStruct((steps * CELLS, D), BF),
            jax.ShapeDtypeStruct((steps * CELLS, 1), F32),
            jax.ShapeDtypeStruct((frames * NT, D), F32),
            jax.ShapeDtypeStruct((frames, 2 * CIN), F32),
            jax.ShapeDtypeStruct((CIN, D), BF),
            jax.ShapeDtypeStruct((D, SLOTS), BF),
            jax.ShapeDtypeStruct((4, D), F32),
        ]
        + [jax.ShapeDtypeStruct((windows.shards, WINDOW, LANES), BF)] * gathers,
        scratch_shapes=[
            pltpu.VMEM((HEAD_PART + 16, LANES), BF),
            pltpu.VMEM((film_rows, LANES), F32),
            pltpu.VMEM(SHAPES["film"], BF),
            pltpu.VMEM((CELLS, CIN), BF),
            pltpu.VMEM((8, 2, 16, LANES), BF),
            pltpu.SemaphoreType.DMA((32,)),
        ]
        + GATHER_SCRATCH * gathers,
        compiler_params=pltpu.CompilerParams(
            vmem_limit_bytes=60 * MIB,
            **(dict(collective_id=0, has_side_effects=True) if gathers else {}),
        ),
        cost_estimate=pl.CostEstimate(
            flops=2 * frames * POS * CIN * D, bytes_accessed=frames * POS * CIN * 2, transcendentals=0
        ),
    )(images, embedding, flat)


def gelu_parts(x):
    inner = 0.7978845608028654 * (x + 0.044715 * x * x * x)
    bent = jnp.tanh(inner)
    value = 0.5 * x * (1.0 + bent)
    slope = 0.5 * (1.0 + bent) + 0.5 * x * (1.0 - bent * bent) * 0.7978845608028654 * (
        1.0 + 3.0 * 0.044715 * x * x
    )
    return value, slope


def layer_kernel(
    windows,
    start,
    flat,
    gains,
    episode_row,
    episode_last,
    valid,
    targets,
    grad_start,
    gradient,
    sums,
    stage,
    spread,
    triple,
    output,
    upward,
    downward,
    action,
    keys,
    values,
    grad_keys,
    grad_values,
    shares,
    first_normed,
    logits_back,
    edges,
    sems,
):
    tokens = start.shape[0]
    frames = tokens // NT
    place = {name: START[name] - HEAD_PART for name in SHAPES}
    windows.load(flat, stage, edges, sems, [(HEAD_PART, START["gains"], 0)])
    for name, matrix in (
        ("triple", triple),
        ("output", output),
        ("upward", upward),
        ("downward", downward),
        ("action", action),
    ):
        to_matrix(stage, place[name], spread, matrix, SHAPES[name])
    is_last = lax.broadcasted_iota(jnp.int32, (tokens, D), 0) % NT == NT - 1

    def take_last(rows):
        return jnp.sum(jnp.where(is_last, rows, 0.0).reshape(frames, NT, D), axis=1)

    def spread_last(rows):
        wide = jnp.broadcast_to(rows[:, None, :], (frames, NT, D)).reshape(tokens, D)
        return jnp.where(is_last, wide, 0.0)

    gain = [gains[i : i + 1, :] for i in range(4)]

    first_unit, first_inverse = norm_rows(start[...])
    first_normed[...] = (first_unit * gain[1]).astype(BF)
    last_start = take_last(start[...])
    last_unit, _ = norm_rows(last_start)
    last_normed = (last_unit * gain[1]).astype(BF)
    queries = mm(last_normed, triple[:, :D]).astype(BF)
    keys[...] = mm(first_normed[...], triple[:, D : 2 * D]).astype(BF)
    values[...] = mm(first_normed[...], triple[:, 2 * D :]).astype(BF)
    key_place = lax.broadcasted_iota(jnp.int32, (frames, tokens), 1)
    query_place = lax.broadcasted_iota(jnp.int32, (frames, tokens), 0) * NT + (NT - 1)
    allowed = (episode_last[...] == episode_row[...]) & (key_place <= query_place)
    attended = []
    for h in range(HEADS):
        own = slice(HD * h, HD * (h + 1))
        scores = mm_nt(queries[:, own], keys[:, own]) * HD ** (-0.5)
        scores = jnp.where(allowed, scores, -1e30)
        powers = jnp.exp(scores - jnp.max(scores, axis=-1, keepdims=True))
        part = powers / jnp.sum(powers, axis=-1, keepdims=True)
        shares[h] = part
        attended.append(mm(part.astype(BF), values[:, own]))
    merged = jnp.concatenate(attended, axis=1).astype(BF)
    middle = last_start + mm(merged, output[...])
    second_unit, second_inverse = norm_rows(middle)
    second_normed = (second_unit * gain[2]).astype(BF)
    activated, slope = gelu_parts(mm(second_normed, upward[...]))
    hidden = activated.astype(BF)
    end = middle + mm(hidden, downward[...])
    final_unit, final_inverse = norm_rows(end)
    final_rows = (final_unit * gain[3]).astype(BF)

    valid_flags = valid[...].astype(F32)
    bins = lax.broadcasted_iota(jnp.int32, (frames, BINS), 1)
    loss = jnp.zeros((frames, 1), F32)
    for a in range(ACT):
        own = slice(BINS * a, BINS * (a + 1))
        logits = mm(final_rows, action[:, own])
        shifted = logits - jnp.max(logits, axis=-1, keepdims=True)
        powers = jnp.exp(shifted)
        total = jnp.sum(powers, axis=-1, keepdims=True)
        hit = targets[:, a : a + 1] == bins
        loss += jnp.log(total) - jnp.sum(jnp.where(hit, shifted, 0.0), axis=-1, keepdims=True)
        logits_back[:, own] = ((powers / total - hit.astype(F32)) * valid_flags).astype(BF)
    place_row = lax.broadcasted_iota(jnp.int32, (8, LANES), 0)
    sums[...] = jnp.where(
        place_row == 0, jnp.sum(loss * valid_flags), jnp.where(place_row == 1, jnp.sum(valid_flags), 0.0)
    )

    def put(name, parts):
        height, breadth = SHAPES[name]
        wide = breadth // LANES
        rows = height * wide
        for j, part in parts:
            for i in range(part.shape[1] // LANES):
                spread[pl.ds(j + i, height, stride=wide), :] = part[:, LANES * i : LANES * (i + 1)]
        stage[pl.ds(place[name], rows), :] = spread[pl.ds(0, rows), :].astype(BF)

    def columns(left, right):
        for j in range(0, right.shape[1] // LANES, 2):
            yield j, mm_tn(left, right[:, LANES * j : LANES * (j + 2)])

    put("action", columns(final_rows, logits_back[...]))
    grad_final = mm_nt(logits_back[...], action[...])
    gain_final = jnp.sum(grad_final * final_unit, axis=0, keepdims=True)
    grad_last = norm_back(final_unit, final_inverse, gain[3], grad_final)
    rounded = grad_last.astype(BF)
    put("downward", columns(hidden, rounded))
    grad_upward = (mm_nt(rounded, downward[...]) * slope).astype(BF)
    put("upward", columns(second_normed, grad_upward))
    grad_second = mm_nt(grad_upward, upward[...])
    gain_second = jnp.sum(grad_second * second_unit, axis=0, keepdims=True)
    grad_last = grad_last + norm_back(second_unit, second_inverse, gain[2], grad_second)
    rounded = grad_last.astype(BF)
    put("output", columns(merged, rounded))
    grad_attended = mm_nt(rounded, output[...]).astype(BF)
    grad_queries = []
    for h in range(HEADS):
        own = slice(HD * h, HD * (h + 1))
        part = shares[h]
        grad_shares = mm_nt(grad_attended[:, own], values[:, own])
        grad_values[:, own] = mm_tn(part.astype(BF), grad_attended[:, own]).astype(BF)
        grad_scores = part * (grad_shares - jnp.sum(grad_shares * part, axis=-1, keepdims=True))
        grad_scores = grad_scores.astype(BF)
        grad_queries.append(mm(grad_scores, keys[:, own]) * HD ** (-0.5))
        grad_keys[:, own] = (mm_tn(grad_scores, queries[:, own]) * HD ** (-0.5)).astype(BF)
    grad_queries = jnp.concatenate(grad_queries, axis=1).astype(BF)

    def triple_parts():
        yield from columns(last_normed, grad_queries)
        for j, part in columns(first_normed[...], grad_keys[...]):
            yield j + D // LANES, part
        for j, part in columns(first_normed[...], grad_values[...]):
            yield j + 2 * D // LANES, part

    put("triple", triple_parts())
    grad_start[...] = (
        mm_nt(grad_keys[...], triple[:, D : 2 * D])
        + mm_nt(grad_values[...], triple[:, 2 * D :])
        + spread_last(mm_nt(grad_queries, triple[:, :D]))
    )
    grad_first = grad_start[...]
    gain_first = jnp.sum(grad_first * first_unit, axis=0, keepdims=True)
    grad_start[...] = norm_back(first_unit, first_inverse, gain[1], grad_first) + spread_last(grad_last)

    rows = []
    for part in (jnp.zeros((1, D), F32), gain_first, gain_second, gain_final):
        rows += [part[:, LANES * j : LANES * (j + 1)] for j in range(4)]
    stage[pl.ds(place["gains"], 16), :] = jnp.concatenate(rows, axis=0).astype(BF)
    out = pltpu.make_async_copy(stage, gradient, sems.at[0])
    out.start()
    out.wait()


def layer(windows, start, flat, gains, episode, valid, targets):
    tokens = start.shape[0]
    frames = tokens // NT
    vmem = pl.BlockSpec(memory_space=pltpu.VMEM)
    anywhere = pl.BlockSpec(memory_space=pl.ANY)
    rows = ROWS - HEAD_PART
    return pl.pallas_call(
        functools.partial(layer_kernel, windows),
        in_specs=[vmem, anywhere] + [vmem] * 5,
        out_specs=[vmem, anywhere, vmem],
        out_shape=[
            jax.ShapeDtypeStruct((tokens, D), F32),
            jax.ShapeDtypeStruct((rows, LANES), BF),
            jax.ShapeDtypeStruct((8, LANES), F32),
        ],
        scratch_shapes=[
            pltpu.VMEM((rows, LANES), BF),
            pltpu.VMEM((SHAPES["action"][0] * SHAPES["action"][1] // LANES, LANES), F32),
            pltpu.VMEM(SHAPES["triple"], BF),
            pltpu.VMEM(SHAPES["output"], BF),
            pltpu.VMEM(SHAPES["upward"], BF),
            pltpu.VMEM(SHAPES["downward"], BF),
            pltpu.VMEM(SHAPES["action"], BF),
            pltpu.VMEM((tokens, D), BF),
            pltpu.VMEM((tokens, D), BF),
            pltpu.VMEM((tokens, D), BF),
            pltpu.VMEM((tokens, D), BF),
            pltpu.VMEM((HEADS, frames, tokens), F32),
            pltpu.VMEM((tokens, D), BF),
            pltpu.VMEM((frames, ACT * BINS), BF),
            pltpu.VMEM((8, 2, 16, LANES), BF),
            pltpu.SemaphoreType.DMA((32,)),
        ],
        compiler_params=pltpu.CompilerParams(vmem_limit_bytes=60 * MIB),
    )(
        start,
        flat,
        gains,
        episode.reshape(1, tokens),
        episode.reshape(frames, NT)[:, NT - 1 :],
        valid.reshape(frames, 1),
        targets,
    )


BLOCK = 256


def section_back_kernel(
    images,
    embedding,
    shifts,
    unit,
    inverse,
    grad_start,
    conv,
    learner,
    gains,
    gradient,
    gain_out,
    grad_grid,
    grad_sum,
    learner_sum,
    gain_sum,
    modulated,
    grad_scale,
    conv_sum,
    spread,
    film_spread,
    stage,
    sems,
):
    step = pl.program_id(0)
    steps = pl.num_programs(0)
    frames = embedding.shape[0]
    groups = frames // GROUP
    flat_conv = START["conv"]

    @pl.when(step == 0)
    def _():
        learner_sum[...] = jnp.zeros_like(learner_sum)
        gain_sum[...] = jnp.zeros_like(gain_sum)

        @pl.loop(0, groups)
        def _(g):
            rows = pl.ds(pl.multiple_of(g * CELLS, 16), CELLS)
            here = unit[rows, :].astype(F32)
            normed = (here * gains[0:1, :]).astype(BF)
            maps = jax.nn.sigmoid(mm(normed, learner[...]))
            mask = own_frame(CELLS)
            tokens = (grad_start[pl.ds(pl.multiple_of(g * SLOTS, SLOTS), SLOTS), :] * (1.0 / POS)).astype(BF)
            grad_maps = mm_nt(normed, tokens)
            grad_logit = jnp.where(mask, grad_maps * maps * (1.0 - maps), 0.0).astype(BF)
            maps = jnp.where(mask, maps, 0.0).astype(BF)
            grad_normed = mm(maps, tokens) + mm_nt(grad_logit, learner[...])
            learner_sum[...] += mm_tn(normed, grad_logit)
            gain_sum[...] += jnp.sum(grad_normed * here, axis=0, keepdims=True)
            back = norm_back(here, inverse[rows, :], gains[0:1, :], grad_normed).astype(BF)
            grad_grid[rows, :] = back
            grad_sum[pl.ds(pl.multiple_of(g * GROUP, GROUP), GROUP), :] = jnp.sum(
                back.astype(F32).reshape(POS, GROUP, D), axis=0
            )

        total = learner_sum[...]
        high = total.astype(BF)
        token = same_token()
        spread_learner = mm(high, token) + mm((total - high.astype(F32)).astype(BF), token)
        spread_learner = jnp.where(learner_mask(), spread_learner, 0.0)
        stage[pl.ds(START["learner"], D * NT // LANES), :] = jnp.sum(
            spread_learner.reshape(D * NT // LANES, GROUP, LANES), axis=1
        ).astype(BF)
        gain_out[...] = gain_sum[...]

    channels = pl.ds(pl.multiple_of(step * BLOCK, BLOCK), BLOCK)
    weights = conv[channels, :]

    conv_sum[...] = jnp.zeros_like(conv_sum)
    for g in range(groups):
        rows = pl.ds(g * CELLS, CELLS)
        here = pl.ds(g * GROUP, GROUP)
        scale = 1.0 + shifts[0, here, :]
        offset = shifts[1, here, :]
        cells = images[:, here, :].astype(F32)
        modulated[...] = (cells * scale[None] + offset[None]).astype(BF).reshape(CELLS, BLOCK)
        back = grad_grid[rows, :]
        conv_sum[...] += mm_tn(modulated[...], back)
        grad_modulated = mm_nt(back, weights).reshape(POS, GROUP, BLOCK)
        grad_scale[here, :] = jnp.sum(grad_modulated * cells, axis=0)
    total = grad_sum[...]
    high = total.astype(BF)
    grad_offset = mm_nt(high, weights) + mm_nt((total - high.astype(F32)).astype(BF), weights)

    wide = D // LANES
    for j in range(wide):
        spread[pl.ds(j, BLOCK, stride=wide), :] = conv_sum[:, LANES * j : LANES * (j + 1)]
    stage[pl.ds(pl.multiple_of(flat_conv + step * BLOCK * wide, 16), BLOCK * wide), :] = spread[...].astype(BF)
    film_wide = 2 * CIN // LANES
    for side, grad in enumerate((grad_scale[...], grad_offset)):
        part = mm_tn(embedding[...], grad.astype(BF))
        for i in range(BLOCK // LANES):
            column = side * (CIN // LANES) + step * (BLOCK // LANES) + i
            film_spread[pl.ds(column, E, stride=film_wide), :] = part[:, LANES * i : LANES * (i + 1)]

    @pl.when(step == steps - 1)
    def _():
        stage[pl.ds(0, flat_conv), :] = film_spread[...].astype(BF)
        out = pltpu.make_async_copy(stage, gradient, sems.at[0])
        out.start()
        out.wait()


def section_back(images, embedding, shifts, unit, inverse, grad_start, conv, learner, gains):
    frames = embedding.shape[0]
    steps = CIN // BLOCK
    whole = lambda *shape: pl.BlockSpec(shape, lambda i: (0,) * len(shape))
    return pl.pallas_call(
        section_back_kernel,
        grid=(steps,),
        in_specs=[
            pl.BlockSpec((POS, frames, BLOCK), lambda i: (0, 0, i)),
            whole(frames, E),
            pl.BlockSpec((2, frames, BLOCK), lambda i: (0, 0, i)),
            whole(frames * POS, D),
            whole(frames * POS, 1),
            whole(frames * NT, D),
            whole(CIN, D),
            whole(D, SLOTS),
            whole(4, D),
        ],
        out_specs=[pl.BlockSpec(memory_space=pl.ANY), whole(1, D)],
        out_shape=[
            jax.ShapeDtypeStruct((HEAD_PART, LANES), BF),
            jax.ShapeDtypeStruct((1, D), F32),
        ],
        scratch_shapes=[
            pltpu.VMEM((frames * POS, D), BF),
            pltpu.VMEM((frames, D), F32),
            pltpu.VMEM((D, SLOTS), F32),
            pltpu.VMEM((1, D), F32),
            pltpu.VMEM((CELLS, BLOCK), BF),
            pltpu.VMEM((frames, BLOCK), F32),
            pltpu.VMEM((BLOCK, D), F32),
            pltpu.VMEM((BLOCK * D // LANES, LANES), F32),
            pltpu.VMEM((START["conv"], LANES), F32),
            pltpu.VMEM((HEAD_PART, LANES), BF),
            pltpu.SemaphoreType.DMA((1,)),
        ],
        compiler_params=pltpu.CompilerParams(vmem_limit_bytes=62 * MIB),
        cost_estimate=pl.CostEstimate(
            flops=4 * frames * POS * CIN * D, bytes_accessed=frames * POS * CIN * 2, transcendentals=0
        ),
    )(
        images,
        embedding,
        shifts.reshape(frames, 2, CIN).transpose(1, 0, 2),
        unit,
        inverse,
        grad_start,
        conv,
        learner,
        gains,
    )


def on_device(
    images, embedding, episode, valid_steps, targets, master, first_moment, second_moment, average
):
    images = images.transpose(1, 0, 2)
    replicas, shards = lax.axis_size("dp"), lax.axis_size("fsdp")
    if fits_ring(replicas, shards, master.shape[0]):
        windows = Windows(shards, master.shape[0] // LANES, WINDOW)
        flat = master.reshape(-1, LANES)
    else:
        whole_flat = lax.all_gather(master.astype(BF), "fsdp", axis=0, tiled=True)
        flat = jnp.pad(whole_flat.reshape(ROWS, LANES), ((0, FLAT_ROWS - ROWS), (0, 0)))[None]
        windows = Windows(1, ROWS, FLAT_ROWS)

    unit, inverse, start, shifts, conv, learner, gains, *gathered = section(
        windows, images, embedding, flat
    )
    if gathered:
        (flat,) = gathered
    grad_start, late_gradient, sums = layer(windows, start, flat, gains, episode, valid_steps, targets)
    early_gradient, gain_grid = section_back(
        images, embedding, shifts, unit, inverse, grad_start, conv, learner, gains
    )
    late = late_gradient.at[START["gains"] - HEAD_PART : START["gains"] - HEAD_PART + 4].set(
        gain_grid.reshape(4, LANES).astype(BF)
    )
    gradient = jnp.concatenate([early_gradient, late]).reshape(-1)
    loss_sum, step_count = lax.psum((sums[0, 0], sums[1, 0]), ("dp", "fsdp"))
    partial_shard = lax.psum_scatter(gradient, "fsdp", scatter_dimension=0, tiled=True)
    grad_shard = lax.psum(partial_shard.astype(F32), "dp") / step_count
    squares = lax.psum(jnp.sum(grad_shard * grad_shard), "fsdp")
    grad_norm = jnp.sqrt(squares)
    clipped = grad_shard * (CLIP_NORM / jnp.maximum(grad_norm, CLIP_NORM))
    new_first = MOMENT_DECAY * first_moment + (1.0 - MOMENT_DECAY) * clipped
    new_second = MOMENT_DECAY * second_moment + (1.0 - MOMENT_DECAY) * clipped * clipped
    correction = 1.0 - MOMENT_DECAY**STEP
    new_master = master - LEARN_RATE * (
        new_first / correction / (jnp.sqrt(new_second / correction) + ADAM_EPSILON)
        + WEIGHT_DECAY * master
    )
    average_decay = min(AVERAGE_DECAY, (1.0 + STEP) / (10.0 + STEP))
    new_average = average_decay * average + (1.0 - average_decay) * new_master
    return (
        new_master,
        new_first,
        new_second,
        new_average,
        new_master.astype(BF),
        grad_norm,
        loss_sum,
        step_count,
    )


def solution(mesh):
    in_specs = (
        P(("dp", "fsdp"), None, None),
        P(("dp", "fsdp"), None),
        P(("dp", "fsdp")),
        P(("dp", "fsdp")),
        P(("dp", "fsdp"), None),
        P("fsdp"),
        P("fsdp"),
        P("fsdp"),
        P("fsdp"),
    )
    out_specs = (P("fsdp"), P("fsdp"), P("fsdp"), P("fsdp"), P("fsdp"), P(), P(), P())
    return jax.shard_map(
        on_device, mesh=mesh, in_specs=in_specs, out_specs=out_specs, check_vma=False
    )
```

```python
import functools

import jax
import jax.numpy as jnp
from jax import lax
from jax.experimental import pallas as pl
from jax.experimental.pallas import tpu as pltpu
from jax.sharding import PartitionSpec as P

D = 512
HEADS = 8
HD = 64
FF = 2048
E = 512
CIN = 1536
POS = 81
NT = 8
ACT = 11
BINS = 256
STEP = 10
LANES = 128
GROUP = 16
CELLS = POS * GROUP
SLOTS = GROUP * NT

MOMENT_DECAY = 0.5
LEARN_RATE = 0.02
WEIGHT_DECAY = 0.1
CLIP_NORM = 1.0
ADAM_EPSILON = 1e-08
AVERAGE_DECAY = 0.999
BF = jnp.bfloat16
F32 = jnp.float32
MIB = 2**20

SHAPES = {
    "film": (E, 2 * CIN),
    "conv": (CIN, D),
    "learner": (D, NT),
    "triple": (D, 3 * D),
    "output": (D, D),
    "upward": (D, FF),
    "downward": (FF, D),
    "action": (D, ACT * BINS),
    "gains": (4, D),
}


def row_starts():
    starts, row = {}, 0
    for name, (height, breadth) in SHAPES.items():
        starts[name] = row
        row += height * breadth // LANES
    return starts, row


START, ROWS = row_starts()
FLAT_ROWS = ROWS + 16
HEAD_PART = START["triple"]
LATE_ROWS = ROWS - HEAD_PART + 112


def mm(a, b):
    return jnp.dot(a, b, preferred_element_type=F32)


def mm_nt(a, b):
    return lax.dot_general(a, b, (((1,), (1,)), ((), ())), preferred_element_type=F32)


def mm_tn(a, b):
    return lax.dot_general(a, b, (((0,), (0,)), ((), ())), preferred_element_type=F32)


class Windows:
    def __init__(self, shards, shard_rows, size):
        self.shards, self.shard_rows, self.size = shards, shard_rows, size
        self.first = [shard_rows * k // 16 * 16 for k in range(shards)]

    def pieces(self, start, stop):
        inner, shared = [], []
        for k in range(self.shards):
            low, high = self.shard_rows * k, self.shard_rows * (k + 1)
            if k == self.shards - 1:
                high = (high + 15) // 16 * 16
            a, b = max(start, -(-low // 16) * 16), min(stop, high // 16 * 16)
            if a < b:
                inner.append((k, a - self.first[k], a, b - a))
            edge = low // 16 * 16
            if low % 16 and start <= edge < stop:
                shared.append((k - 1, edge - self.first[k - 1], k, edge - self.first[k], edge))
        return inner, shared

    def load(self, flat_ref, stage, edges, sem, parts):
        copies, fixes = [], []
        for start, stop, place in parts:
            inner, shared = self.pieces(start, stop)
            for k, offset, row, count in inner:
                copies.append(
                    pltpu.make_async_copy(
                        flat_ref.at[k, pl.ds(offset, count)],
                        stage.at[pl.ds(place + row - start, count)],
                        sem.at[len(copies)],
                    )
                )
            for k, offset, l, other, row in shared:
                for side, (window, at) in enumerate(((k, offset), (l, other))):
                    copies.append(
                        pltpu.make_async_copy(
                            flat_ref.at[window, pl.ds(at, 16)],
                            edges.at[len(fixes), side],
                            sem.at[len(copies)],
                        )
                    )
                fixes.append(place + row - start)
        for copy in copies:
            copy.start()
        for copy in copies:
            copy.wait()
        for index, row in enumerate(fixes):
            stage[pl.ds(row, 16), :] = edges[index, 0] + edges[index, 1]


MESH = pl.DeviceIdType.MESH
CHUNK = 384
CHUNKS = 18
WINDOW = CHUNK * CHUNKS
CARRIED = 2 * CHUNKS // 3
TRADED = CHUNKS // 3
NEEDED = 13
READY, READY_TRADED = 9, 4
SENDS = ((0, 3, 2), (0, 1, 3), (0, 1, 2), (3, 1, 2))


def fits_ring(replicas, shards, shard_size):
    return shards == 8 and replicas == 4 and shard_size % LANES == 0 and shard_size <= LANES * (WINDOW - 16)


def gray(place):
    return place + (place // 2) * (1 - 2 * (place % 2))


class Ring:
    def __init__(self):
        self.me = lax.axis_index("fsdp")
        self.core = self.me % 2
        self.place = self.flip(gray(self.me // 2))
        self.replica = lax.axis_index("dp")
        self.half = self.replica % 2
        self.sibling = self.me + 1 - 2 * self.core
        self.after = self.device(self.place + 1)
        self.before = self.device(self.place + 3)
        self.partner = self.replica + 1 - 2 * self.half
        self.shards = lax.axis_size("fsdp")
        self.others = [(self.me + 1 + index) % self.shards for index in range(self.shards - 1)]

    def flip(self, place):
        return (place + self.core * (4 - 2 * place)) % 4

    def device(self, place):
        return gray(self.flip(place % 4)) * 2 + self.core

    def pick(self, table, place):
        found = jnp.int32(0)
        for index, value in enumerate(table):
            found = found + jnp.where(place == index, value, 0)
        return found


class Gather:
    def __init__(self, own, whole, gain_rows, around, straight, across, trade, own_sems):
        self.ring, self.own, self.whole, self.gain_rows = Ring(), own, whole, gain_rows
        self.around_sems, self.straight_sems, self.across_sems, self.trade_sems, self.own_sems = (
            around,
            straight,
            across,
            trade,
            own_sems,
        )
        core, place = self.ring.core, self.ring.place
        self.first = [CARRIED, jnp.where(core == 0, READY, 0), 0, 0]
        self.first_traded = [TRADED, jnp.where(core == 0, READY_TRADED, 0), 0, 0]

    def greet(self):
        barrier = pltpu.get_barrier_semaphore()
        for device in [{"fsdp": other} for other in self.ring.others] + [{"dp": self.ring.partner}]:
            pl.semaphore_signal(barrier, inc=1, device_id=device, device_id_type=MESH)
        pl.semaphore_wait(barrier, self.ring.shards)

    def gain_copy(self, index):
        return pltpu.make_async_remote_copy(
            src_ref=self.gain_rows,
            dst_ref=self.gain_rows,
            send_sem=self.own_sems.at[3 + index],
            recv_sem=self.own_sems.at[2],
            device_id={"fsdp": self.ring.others[index]},
            device_id_type=MESH,
        )

    def send_gains(self, place):
        @pl.when(self.ring.me == self.ring.shards - 1)
        def _():
            self.gain_rows[...] = self.own[pl.ds(place, 16), :]
            for index in range(self.ring.shards - 1):
                self.gain_copy(index).start()

    def take_gains(self):
        last = self.ring.me == self.ring.shards - 1

        @pl.when(last)
        def _():
            for index in range(self.ring.shards - 1):
                self.gain_copy(index).wait_send()

        @pl.when(jnp.logical_not(last))
        def _():
            self.gain_copy(0).wait_recv()

    def carried(self, j):
        return (j // 2) * 3 + (j % 2) * (1 + self.ring.half)

    def rows(self, i):
        return pl.ds(pl.multiple_of(i * CHUNK, 16), CHUNK)

    def copy(self, window, i, send_sem, recv_sem, device, own=False):
        source = self.own.at[self.rows(i)] if own else self.whole.at[window, self.rows(i)]
        return pltpu.make_async_remote_copy(
            src_ref=source,
            dst_ref=self.whole.at[window, self.rows(i)],
            send_sem=send_sem,
            recv_sem=recv_sem,
            device_id=device,
            device_id_type=MESH,
        )

    def around(self, origin, j, own=False):
        sems = self.around_sems
        return self.copy(
            self.ring.me if own else self.ring.device(origin),
            self.carried(j),
            sems.at[0, origin, j],
            sems.at[1, origin, j],
            {"fsdp": self.ring.after},
            own,
        )

    def straight(self, hops, j):
        place = self.ring.place
        return self.copy(
            self.ring.me,
            self.carried(j),
            self.straight_sems.at[hops - 1, j],
            self.around_sems.at[1, place, j],
            {"fsdp": self.ring.device(place + hops)},
            own=True,
        )

    def across(self, origin, i):
        sems = self.across_sems
        return self.copy(
            self.ring.device(origin), i, sems.at[0, origin, i], sems.at[1, origin, i], {"fsdp": self.ring.sibling}
        )

    def trade(self, origin, j, half):
        sems = self.trade_sems
        return self.copy(
            self.ring.device(origin),
            3 * j + 1 + half,
            sems.at[0, origin, j],
            sems.at[1, origin, j],
            {"dp": self.ring.partner},
        )

    def own_copies(self):
        ring = self.ring
        keep = pltpu.make_async_copy(self.own, self.whole.at[ring.me], self.own_sems.at[10])
        give = pltpu.make_async_remote_copy(
            src_ref=self.own,
            dst_ref=self.whole.at[ring.me],
            send_sem=self.own_sems.at[1],
            recv_sem=self.own_sems.at[0],
            device_id={"fsdp": ring.sibling},
            device_id_type=MESH,
        )
        return keep, give

    def take(self, origin, low, high, forward):
        low = jnp.where(self.ring.place == origin, high, low)

        @pl.loop(low, high)
        def _(j):
            self.around(origin, j).wait_recv()
            if forward:

                @pl.when(origin != (self.ring.place + 1) % 4)
                def _():
                    self.around(origin, j).start()

            @pl.when(j % 2 == 1)
            def _():
                self.trade(origin, j // 2, self.ring.half).start()

            self.across(origin, self.carried(j)).start()

    def take_traded(self, origin, low, high):
        other = 1 - self.ring.half
        low = jnp.where(self.ring.place == origin, high, low)

        @pl.loop(low, high)
        def _(j):
            self.trade(origin, j, other).wait_recv()
            self.across(origin, 3 * j + 1 + other).start()

    def wait_across(self, origin, low, high):
        sibling_place = (4 - self.ring.place) % 4
        low = jnp.where(sibling_place == origin, high, low)

        @pl.loop(low, high)
        def _(i):
            self.across(origin, i).wait_recv()

    def begin(self, gain_place):
        ring = self.ring
        self.greet()
        self.send_gains(gain_place)
        for origin in (0, 1):

            @pl.when(ring.place == origin)
            def _():
                @pl.loop(0, self.first[origin])
                def _(j):
                    self.around(origin, j, own=True).start()

        keep, give = self.own_copies()
        keep.start()
        give.start()
        for origin in (1, 0):
            self.take(origin, 0, self.first[origin], True)

        @pl.when(ring.place > 0)
        def _():
            @pl.loop(jnp.where(ring.place == 1, self.first[1], 0), CARRIED)
            def _(j):
                for hops in (1, 2, 3):
                    self.straight(hops, j).start()

        for origin in (1, 0):
            self.take_traded(origin, 0, self.first_traded[origin])
        self.take_gains()
        keep.wait()
        give.wait_recv()
        self.wait_across(0, 0, CHUNKS)
        self.wait_across(1, 0, jnp.where(ring.core == 1, NEEDED, 0))

    def go_on(self, step, steps):
        parts = steps - 1

        def bounds(at, count, first):
            return first + jnp.clip(at, 0, parts) * (count - first) // parts

        for origin in (1, 2, 3):
            first = self.first[origin]
            self.take(origin, bounds(step - 1, CARRIED, first), bounds(step, CARRIED, first), False)
        for origin in (1, 2, 3):
            first = self.first_traded[origin]
            self.take_traded(
                origin,
                bounds(step - 2, TRADED, first),
                jnp.where(step == steps - 1, TRADED, bounds(step - 1, TRADED, first)),
            )

        @pl.when(step == steps - 1)
        def _():
            self.finish()

    def finish(self):
        place = self.ring.place
        self.wait_across(1, jnp.where(self.ring.core == 1, NEEDED, 0), CHUNKS)
        self.wait_across(2, 0, CHUNKS)
        self.wait_across(3, 0, CHUNKS)
        self.own_copies()[1].wait_send()
        for origin in range(4):
            sent = jnp.where((place + 1) % 4 == origin, 0, self.first[origin])

            @pl.loop(0, sent)
            def _(j):
                self.around(origin, j).wait_send()

            @pl.loop(0, jnp.where(place == origin, 0, TRADED))
            def _(j):
                self.trade(origin, j, self.ring.half).wait_send()

            @pl.loop(0, jnp.where(place == origin, 0, CHUNKS))
            def _(i):
                self.across(origin, i).wait_send()

        @pl.when(place > 0)
        def _():
            @pl.loop(jnp.where(place == 1, self.first[1], 0), CARRIED)
            def _(j):
                for hops in (1, 2, 3):
                    self.straight(hops, j).wait_send()


GATHER_SCRATCH = [
    pltpu.VMEM((WINDOW, LANES), BF),
    pltpu.VMEM((16, LANES), BF),
    pltpu.SemaphoreType.DMA((2, 4, CARRIED)),
    pltpu.SemaphoreType.DMA((3, CARRIED)),
    pltpu.SemaphoreType.DMA((2, 4, CHUNKS)),
    pltpu.SemaphoreType.DMA((2, 4, TRADED)),
    pltpu.SemaphoreType.DMA((11,)),
]


def to_matrix(stage, place, spread, matrix, shape):
    height, breadth = shape
    wide = breadth // LANES
    rows = height * wide
    spread[pl.ds(0, rows), :] = stage[pl.ds(place, rows), :].astype(F32)
    for j in range(wide):
        matrix[:, LANES * j : LANES * (j + 1)] = spread[pl.ds(j, height, stride=wide), :].astype(BF)


def norm_rows(values):
    centre = jnp.mean(values, axis=-1, keepdims=True)
    shifted = values - centre
    inverse = lax.rsqrt(jnp.mean(shifted * shifted, axis=-1, keepdims=True) + 1e-05)
    return shifted * inverse, inverse


def norm_back(unit, inverse, gain, grad):
    scaled = grad * gain
    along = jnp.mean(scaled * unit, axis=-1, keepdims=True)
    return inverse * (scaled - jnp.mean(scaled, axis=-1, keepdims=True) - unit * along)


def own_frame(rows):
    frame = lax.broadcasted_iota(jnp.int32, (rows // GROUP, GROUP, SLOTS), 1).reshape(rows, SLOTS)
    return frame == lax.broadcasted_iota(jnp.int32, (rows, SLOTS), 1) // NT


def same_token():
    a = lax.broadcasted_iota(jnp.int32, (SLOTS, SLOTS), 0) % NT
    b = lax.broadcasted_iota(jnp.int32, (SLOTS, SLOTS), 1) % NT
    return (a == b).astype(BF)


def learner_mask():
    return own_frame(D)


def section_kernel(
    windows,
    images,
    embedding,
    flat,
    grid_out,
    pooled_out,
    shifts_out,
    conv_out,
    learner_out,
    gains_out,
    *rest,
):
    step = pl.program_id(0)
    if windows.shards > 1:
        master = flat
        flat, stage, spread, film, modulated, edges, sems, own, *gather_sems = rest
        gather = Gather(own, flat, *gather_sems)
    else:
        gather = None
        stage, spread, film, modulated, edges, sems = rest

    @pl.when(step == 0)
    def _():
        if gather:
            rows = master.shape[0]
            spread[pl.ds(0, 16), :] = jnp.zeros((16, LANES), F32)
            tail = rows // 16 * 16
            spread[pl.ds(tail, WINDOW - tail), :] = jnp.zeros((WINDOW - tail, LANES), F32)
            spread[pl.ds(gather.ring.me * rows % 16, rows), :] = master[...]
            own[...] = spread[pl.ds(0, WINDOW), :].astype(BF)
            gather.begin(START["gains"] - windows.first[-1])
        learner_rows = HEAD_PART - START["learner"]
        parts = [(0, HEAD_PART, 0)]
        if gather is None:
            parts.append((START["gains"], ROWS, HEAD_PART))
        windows.load(flat, stage, edges, sems, parts)
        if gather:
            stage[pl.ds(HEAD_PART, 16), :] = gather.gain_rows[...]
        to_matrix(stage, 0, spread, film, SHAPES["film"])
        shifts_out[...] = mm(embedding[...], film[...])
        to_matrix(stage, START["conv"], spread, conv_out, SHAPES["conv"])
        packed = stage[pl.ds(START["learner"], learner_rows), :].astype(F32)
        opened = jnp.broadcast_to(packed[:, None, :], (learner_rows, GROUP, LANES)).reshape(D, SLOTS)
        opened = jnp.where(learner_mask(), opened, 0.0).astype(BF)
        learner_out[...] = mm(opened, same_token()).astype(BF)
        gain_rows = stage[pl.ds(HEAD_PART, 16), :].astype(F32)
        for i in range(4):
            for j in range(4):
                gains_out[i : i + 1, LANES * j : LANES * (j + 1)] = gain_rows[4 * i + j : 4 * i + j + 1]

    here = pl.ds(pl.multiple_of(step * GROUP, GROUP), GROUP)
    scale = 1.0 + shifts_out[here, :CIN]
    offset = shifts_out[here, CIN:]
    modulated[...] = (images[...].astype(F32) * scale[None] + offset[None]).astype(BF).reshape(CELLS, CIN)
    grid = mm(modulated[...], conv_out[...])
    grid_out[...] = grid.astype(BF)
    unit, _ = norm_rows(grid)
    normed = (unit * gains_out[0:1, :]).astype(BF)
    maps = jax.nn.sigmoid(mm(normed, learner_out[...]))
    maps = jnp.where(own_frame(CELLS), maps, 0.0).astype(BF)
    pooled_out[...] = mm_tn(maps, normed) * (1.0 / POS)
    if gather:
        gather.go_on(step, pl.num_programs(0))


def section(windows, images, embedding, flat):
    frames = images.shape[1]
    steps = frames // GROUP
    whole = lambda *shape: pl.BlockSpec(shape, lambda i: (0,) * len(shape))
    gathers = windows.shards > 1
    film_rows = SHAPES["film"][0] * SHAPES["film"][1] // LANES
    return pl.pallas_call(
        functools.partial(section_kernel, windows),
        grid=(steps,),
        in_specs=[
            pl.BlockSpec((POS, GROUP, CIN), lambda i: (0, i, 0)),
            whole(frames, E),
            whole(*flat.shape) if gathers else pl.BlockSpec(memory_space=pl.ANY),
        ],
        out_specs=[
            pl.BlockSpec((CELLS, D), lambda i: (i, 0)),
            pl.BlockSpec((SLOTS, D), lambda i: (i, 0)),
            whole(frames, 2 * CIN),
            whole(CIN, D),
            whole(D, SLOTS),
            whole(4, D),
        ]
        + [pl.BlockSpec(memory_space=pl.ANY)] * gathers,
        out_shape=[
            jax.ShapeDtypeStruct((steps * CELLS, D), BF),
            jax.ShapeDtypeStruct((frames * NT, D), F32),
            jax.ShapeDtypeStruct((frames, 2 * CIN), F32),
            jax.ShapeDtypeStruct((CIN, D), BF),
            jax.ShapeDtypeStruct((D, SLOTS), BF),
            jax.ShapeDtypeStruct((4, D), F32),
        ]
        + [jax.ShapeDtypeStruct((windows.shards, WINDOW, LANES), BF)] * gathers,
        scratch_shapes=[
            pltpu.VMEM((HEAD_PART + 16, LANES), BF),
            pltpu.VMEM((film_rows, LANES), F32),
            pltpu.VMEM(SHAPES["film"], BF),
            pltpu.VMEM((CELLS, CIN), BF),
            pltpu.VMEM((8, 2, 16, LANES), BF),
            pltpu.SemaphoreType.DMA((32,)),
        ]
        + GATHER_SCRATCH * gathers,
        compiler_params=pltpu.CompilerParams(
            vmem_limit_bytes=60 * MIB,
            **(dict(collective_id=0, has_side_effects=True) if gathers else {}),
        ),
        cost_estimate=pl.CostEstimate(
            flops=2 * frames * POS * CIN * D, bytes_accessed=frames * POS * CIN * 2, transcendentals=0
        ),
    )(images, embedding, flat)


def gelu_parts(x):
    inner = 0.7978845608028654 * (x + 0.044715 * x * x * x)
    bent = jnp.tanh(inner)
    value = 0.5 * x * (1.0 + bent)
    slope = 0.5 * (1.0 + bent) + 0.5 * x * (1.0 - bent * bent) * 0.7978845608028654 * (
        1.0 + 3.0 * 0.044715 * x * x
    )
    return value, slope


def layer_kernel(
    windows,
    start,
    flat,
    gains,
    episode_row,
    episode_last,
    valid,
    targets,
    grad_start,
    gradient,
    sums,
    stage,
    spread,
    triple,
    output,
    upward,
    downward,
    action,
    keys,
    values,
    grad_keys,
    grad_values,
    shares,
    first_normed,
    logits_back,
    edges,
    sems,
):
    tokens = start.shape[0]
    frames = tokens // NT
    place = {name: START[name] - HEAD_PART for name in SHAPES}
    windows.load(flat, stage, edges, sems, [(HEAD_PART, START["gains"], 0)])
    for name, matrix in (
        ("triple", triple),
        ("output", output),
        ("upward", upward),
        ("downward", downward),
        ("action", action),
    ):
        to_matrix(stage, place[name], spread, matrix, SHAPES[name])
    is_last = lax.broadcasted_iota(jnp.int32, (tokens, D), 0) % NT == NT - 1

    def take_last(rows):
        return jnp.sum(jnp.where(is_last, rows, 0.0).reshape(frames, NT, D), axis=1)

    def spread_last(rows):
        wide = jnp.broadcast_to(rows[:, None, :], (frames, NT, D)).reshape(tokens, D)
        return jnp.where(is_last, wide, 0.0)

    gain = [gains[i : i + 1, :] for i in range(4)]

    first_unit, first_inverse = norm_rows(start[...])
    first_normed[...] = (first_unit * gain[1]).astype(BF)
    last_start = take_last(start[...])
    last_unit, _ = norm_rows(last_start)
    last_normed = (last_unit * gain[1]).astype(BF)
    queries = mm(last_normed, triple[:, :D]).astype(BF)
    keys[...] = mm(first_normed[...], triple[:, D : 2 * D]).astype(BF)
    values[...] = mm(first_normed[...], triple[:, 2 * D :]).astype(BF)
    key_place = lax.broadcasted_iota(jnp.int32, (frames, tokens), 1)
    query_place = lax.broadcasted_iota(jnp.int32, (frames, tokens), 0) * NT + (NT - 1)
    allowed = (episode_last[...] == episode_row[...]) & (key_place <= query_place)
    attended = []
    for h in range(HEADS):
        own = slice(HD * h, HD * (h + 1))
        scores = mm_nt(queries[:, own], keys[:, own]) * HD ** (-0.5)
        scores = jnp.where(allowed, scores, -1e30)
        powers = jnp.exp(scores - jnp.max(scores, axis=-1, keepdims=True))
        part = powers / jnp.sum(powers, axis=-1, keepdims=True)
        shares[h] = part
        attended.append(mm(part.astype(BF), values[:, own]))
    merged = jnp.concatenate(attended, axis=1).astype(BF)
    middle = last_start + mm(merged, output[...])
    second_unit, second_inverse = norm_rows(middle)
    second_normed = (second_unit * gain[2]).astype(BF)
    activated, slope = gelu_parts(mm(second_normed, upward[...]))
    hidden = activated.astype(BF)
    end = middle + mm(hidden, downward[...])
    final_unit, final_inverse = norm_rows(end)
    final_rows = (final_unit * gain[3]).astype(BF)

    valid_flags = valid[...].astype(F32)
    bins = lax.broadcasted_iota(jnp.int32, (frames, BINS), 1)
    loss = jnp.zeros((frames, 1), F32)
    for a in range(ACT):
        own = slice(BINS * a, BINS * (a + 1))
        logits = mm(final_rows, action[:, own])
        shifted = logits - jnp.max(logits, axis=-1, keepdims=True)
        powers = jnp.exp(shifted)
        total = jnp.sum(powers, axis=-1, keepdims=True)
        hit = targets[:, a : a + 1] == bins
        loss += jnp.log(total) - jnp.sum(jnp.where(hit, shifted, 0.0), axis=-1, keepdims=True)
        logits_back[:, own] = ((powers / total - hit.astype(F32)) * valid_flags).astype(BF)
    place_row = lax.broadcasted_iota(jnp.int32, (8, LANES), 0)
    sums[...] = jnp.where(
        place_row == 0, jnp.sum(loss * valid_flags), jnp.where(place_row == 1, jnp.sum(valid_flags), 0.0)
    )

    def put(name, parts):
        height, breadth = SHAPES[name]
        wide = breadth // LANES
        rows = height * wide
        for j, part in parts:
            for i in range(part.shape[1] // LANES):
                spread[pl.ds(j + i, height, stride=wide), :] = part[:, LANES * i : LANES * (i + 1)]
        stage[pl.ds(place[name], rows), :] = spread[pl.ds(0, rows), :].astype(BF)

    def columns(left, right):
        for j in range(0, right.shape[1] // LANES, 2):
            yield j, mm_tn(left, right[:, LANES * j : LANES * (j + 2)])

    put("action", columns(final_rows, logits_back[...]))
    grad_final = mm_nt(logits_back[...], action[...])
    gain_final = jnp.sum(grad_final * final_unit, axis=0, keepdims=True)
    grad_last = norm_back(final_unit, final_inverse, gain[3], grad_final)
    rounded = grad_last.astype(BF)
    put("downward", columns(hidden, rounded))
    grad_upward = (mm_nt(rounded, downward[...]) * slope).astype(BF)
    put("upward", columns(second_normed, grad_upward))
    grad_second = mm_nt(grad_upward, upward[...])
    gain_second = jnp.sum(grad_second * second_unit, axis=0, keepdims=True)
    grad_last = grad_last + norm_back(second_unit, second_inverse, gain[2], grad_second)
    rounded = grad_last.astype(BF)
    put("output", columns(merged, rounded))
    grad_attended = mm_nt(rounded, output[...]).astype(BF)
    grad_queries = []
    for h in range(HEADS):
        own = slice(HD * h, HD * (h + 1))
        part = shares[h]
        grad_shares = mm_nt(grad_attended[:, own], values[:, own])
        grad_values[:, own] = mm_tn(part.astype(BF), grad_attended[:, own]).astype(BF)
        grad_scores = part * (grad_shares - jnp.sum(grad_shares * part, axis=-1, keepdims=True))
        grad_scores = grad_scores.astype(BF)
        grad_queries.append(mm(grad_scores, keys[:, own]) * HD ** (-0.5))
        grad_keys[:, own] = (mm_tn(grad_scores, queries[:, own]) * HD ** (-0.5)).astype(BF)
    grad_queries = jnp.concatenate(grad_queries, axis=1).astype(BF)

    def triple_parts():
        yield from columns(last_normed, grad_queries)
        for j, part in columns(first_normed[...], grad_keys[...]):
            yield j + D // LANES, part
        for j, part in columns(first_normed[...], grad_values[...]):
            yield j + 2 * D // LANES, part

    put("triple", triple_parts())
    grad_start[...] = (
        mm_nt(grad_keys[...], triple[:, D : 2 * D])
        + mm_nt(grad_values[...], triple[:, 2 * D :])
        + spread_last(mm_nt(grad_queries, triple[:, :D]))
    )
    grad_first = grad_start[...]
    gain_first = jnp.sum(grad_first * first_unit, axis=0, keepdims=True)
    grad_start[...] = norm_back(first_unit, first_inverse, gain[1], grad_first) + spread_last(grad_last)

    rows = []
    for part in (jnp.zeros((1, D), F32), gain_first, gain_second, gain_final):
        rows += [part[:, LANES * j : LANES * (j + 1)] for j in range(4)]
    stage[pl.ds(place["gains"], 16), :] = jnp.concatenate(rows, axis=0).astype(BF)
    stage[pl.ds(place["gains"] + 16, LATE_ROWS - place["gains"] - 16), :] = jnp.zeros(
        (LATE_ROWS - place["gains"] - 16, LANES), BF
    )
    out = pltpu.make_async_copy(stage, gradient, sems.at[0])
    out.start()
    out.wait()


def layer(windows, start, flat, gains, episode, valid, targets):
    tokens = start.shape[0]
    frames = tokens // NT
    vmem = pl.BlockSpec(memory_space=pltpu.VMEM)
    anywhere = pl.BlockSpec(memory_space=pl.ANY)
    rows = LATE_ROWS
    return pl.pallas_call(
        functools.partial(layer_kernel, windows),
        in_specs=[vmem, anywhere] + [vmem] * 5,
        out_specs=[vmem, anywhere, vmem],
        out_shape=[
            jax.ShapeDtypeStruct((tokens, D), F32),
            jax.ShapeDtypeStruct((rows, LANES), BF),
            jax.ShapeDtypeStruct((8, LANES), F32),
        ],
        scratch_shapes=[
            pltpu.VMEM((rows, LANES), BF),
            pltpu.VMEM((SHAPES["action"][0] * SHAPES["action"][1] // LANES, LANES), F32),
            pltpu.VMEM(SHAPES["triple"], BF),
            pltpu.VMEM(SHAPES["output"], BF),
            pltpu.VMEM(SHAPES["upward"], BF),
            pltpu.VMEM(SHAPES["downward"], BF),
            pltpu.VMEM(SHAPES["action"], BF),
            pltpu.VMEM((tokens, D), BF),
            pltpu.VMEM((tokens, D), BF),
            pltpu.VMEM((tokens, D), BF),
            pltpu.VMEM((tokens, D), BF),
            pltpu.VMEM((HEADS, frames, tokens), F32),
            pltpu.VMEM((tokens, D), BF),
            pltpu.VMEM((frames, ACT * BINS), BF),
            pltpu.VMEM((8, 2, 16, LANES), BF),
            pltpu.SemaphoreType.DMA((32,)),
        ],
        compiler_params=pltpu.CompilerParams(vmem_limit_bytes=60 * MIB),
    )(
        start,
        flat,
        gains,
        episode.reshape(1, tokens),
        episode.reshape(frames, NT)[:, NT - 1 :],
        valid.reshape(frames, 1),
        targets,
    )


BLOCK = 256
BLOCKS = CIN // BLOCK
ITEM = 576
LAST_ITEM = 288
FIRST_ITEM = 672
SLAB = WINDOW + LAST_ITEM
EARLY = WINDOW // ITEM
FILM_ITEMS = 2 * BLOCKS
CONV_ITEMS = 8
LATE_ID = EARLY
LAST_ID = LATE_ID + FILM_ITEMS
IDS = LAST_ID + 1
LAG = 2
FIRST_FILM, FIRST_CONV, LAST_UNIT = 8, 10, 19
COMPUTE_UNITS = 6 + 2 * BLOCKS
UNITS = LAST_UNIT + 7 * LAG + 1
CONV_BEFORE = (0, 0, 1, 3, 4, 6, 8)
OWN_CONV = 1280
TAIL_CONV = 1152
FILM_FIRST = (0, 272)
FILM_HEIGHT = (288, 240)
SQUARES = 2


def added(parts):
    total = parts[0].astype(F32)
    for part in parts[1:]:
        total = total + part.astype(F32)
    return total


class Reduce:
    def __init__(self, shard_rows, early, film, conv, patch, own, sibling, ring_in, z_in, sems, z_sems, load_sems, patch_sem):
        self.ring = ring = Ring()
        self.shard_rows, self.early = shard_rows, early
        self.film, self.conv, self.patch = film, conv, patch
        self.own, self.sibling, self.ring_in, self.z_in = own, sibling, ring_in, z_in
        self.sems, self.z_sems, self.load_sems, self.patch_sem = sems, z_sems, load_sems, patch_sem
        self.low = 2 - ring.core
        self.line = ring.replica + ring.core * (3 - 2 * ring.replica)

    def greet(self):
        barrier = pltpu.get_barrier_semaphore()
        devices = [{"fsdp": other} for other in self.ring.others]
        devices += [{"dp": (self.ring.replica + hops) % 4} for hops in (1, 2, 3)]
        for device in devices:
            pl.semaphore_signal(barrier, inc=1, device_id=device, device_id_type=MESH)
        pl.semaphore_wait(barrier, len(devices))

    def along(self, line):
        return {"dp": line + self.ring.core * (3 - 2 * line)}

    def stage_of(self, q):
        return (self.ring.place + 7 - q) % 4

    def window_row(self, device):
        return pl.multiple_of(self.shard_rows * device // 16 * 16 - HEAD_PART, 16)

    def rows(self, row, count):
        return pl.ds(pl.multiple_of(row, 16), count)

    def remote(self, source, target, send_sem, recv_sem, device):
        return pltpu.make_async_remote_copy(
            src_ref=source,
            dst_ref=target,
            send_sem=send_sem,
            recv_sem=recv_sem,
            device_id=device,
            device_id_type=MESH,
        )

    def to_sibling(self, source, q, ident, row, count):
        return self.remote(
            source,
            self.sibling.at[q, self.rows(row, count)],
            self.sems.at[0, q, ident],
            self.sems.at[1, q, ident],
            {"fsdp": self.ring.sibling},
        )

    def to_next(self, q, ident, row, count):
        rows = self.rows(row, count)
        return self.remote(
            self.own.at[q, rows],
            self.ring_in.at[q, rows],
            self.sems.at[2, q, ident],
            self.sems.at[3, q, ident],
            {"fsdp": self.ring.after},
        )

    def to_line(self, which, line, slot, ident, row, count, forward=False):
        rows = self.rows(row, count)
        return self.remote(
            self.z_in.at[1, rows] if forward else self.own.at[self.ring.place, rows],
            self.z_in.at[slot, rows],
            self.z_sems.at[which, ident],
            self.z_sems.at[2 + slot, ident],
            self.along(line),
        )

    def load(self, q, ident, source_row, row, count):
        return pltpu.make_async_copy(
            self.early.at[self.rows(source_row, count)],
            self.own.at[q, self.rows(row, count)],
            self.load_sems.at[q, ident],
        )

    def load_patch(self):
        last = pl.ds(self.shard_rows * 7 // 16 * 16 - HEAD_PART + (EARLY - 1) * ITEM, ITEM)
        return pltpu.make_async_copy(self.early.at[last], self.patch, self.patch_sem.at[0])

    def start_early(self):
        ring = self.ring
        other = 1 - ring.core

        def sibling_device(q):
            place = (q + other * (4 - 2 * q)) % 4
            return gray(place) * 2 + other

        @pl.when(ring.core == 0)
        def _():
            self.load_patch().start()
            for i in range(3):
                self.load(1, i, FIRST_ITEM * i, WINDOW - 3 * FIRST_ITEM + FIRST_ITEM * i, FIRST_ITEM).start()

        @pl.when(ring.core == 1)
        def _():
            for i in range(3):
                self.to_sibling(
                    self.early.at[pl.ds(FIRST_ITEM * i, FIRST_ITEM)],
                    1,
                    i,
                    WINDOW - 3 * FIRST_ITEM + FIRST_ITEM * i,
                    FIRST_ITEM,
                ).start()

        @pl.loop(0, EARLY)
        def _(i):
            @pl.loop(self.low, 4)
            def _(q):
                self.load(q, i, self.window_row(ring.device(q)) + ITEM * i, ITEM * i, ITEM).start()

            @pl.loop(2 - other, 4)
            def _(q):
                @pl.when((ring.core == 1) | (q != 2) | (i != EARLY - 1))
                def _():
                    row = self.window_row(sibling_device(q)) + ITEM * i
                    self.to_sibling(self.early.at[self.rows(row, ITEM)], q, i, ITEM * i, ITEM).start()

    def patch_gains(self, gain_rows):
        place = START["gains"] - (self.shard_rows * 7 // 16 * 16 + (EARLY - 1) * ITEM)

        @pl.when(self.ring.core == 0)
        def _():
            self.load_patch().wait()
            self.patch[pl.ds(place, 16), :] = (self.patch[pl.ds(place, 16), :].astype(F32) + gain_rows).astype(BF)
            self.to_sibling(self.patch, 2, EARLY - 1, (EARLY - 1) * ITEM, ITEM).start()

        @pl.when(self.ring.core == 1)
        def _():
            self.load(2, EARLY - 1, 0, (EARLY - 1) * ITEM, ITEM).wait()
            here = pl.ds((EARLY - 1) * ITEM + place, 16)
            self.own[2, here, :] = (self.own[2, here, :].astype(F32) + gain_rows).astype(BF)

    def give_film(self, step):
        for half in range(2):
            item = 2 * step + half
            row = ITEM * item
            tiles = [half * (CIN // LANES) + 2 * step + a for a in range(2)]
            conv_rows = self.rows(96 * item, 96)
            for core in range(2):
                first, height = FILM_FIRST[core], FILM_HEIGHT[core]

                @pl.when(self.ring.core == core)
                def _():
                    for a in range(2):
                        self.own[0, self.rows(row + height * a, height), :] = self.film[
                            tiles[a], first : first + height, :
                        ]
                    if core == 1:
                        self.own[0, self.rows(row + 2 * height, 96), :] = self.conv[conv_rows, :]

                @pl.when(self.ring.core != core)
                def _():
                    for a in range(2):
                        self.to_sibling(
                            self.film.at[tiles[a], pl.ds(first, height)],
                            0,
                            LATE_ID + item,
                            row + height * a,
                            height,
                        ).start()
                    if core == 1:
                        self.to_sibling(
                            self.conv.at[conv_rows], 0, LATE_ID + item, row + 2 * height, 96
                        ).start()

    def give_conv(self, step):
        ring = self.ring

        @pl.loop(ring.pick(CONV_BEFORE, step), ring.pick(CONV_BEFORE, step + 1))
        def _(i):
            source = self.rows(OWN_CONV + ITEM * i, ITEM)

            @pl.when(ring.core == 0)
            def _():
                self.own[1, self.rows(ITEM * i, ITEM), :] = self.conv[source, :]

            @pl.when(ring.core == 1)
            def _():
                self.to_sibling(self.conv.at[source], 1, LATE_ID + i, ITEM * i, ITEM).start()

        @pl.when(step == BLOCKS - 1)
        def _():
            mine = pl.ds(OWN_CONV + CONV_ITEMS * ITEM, LAST_ITEM)
            tail = pl.ds(TAIL_CONV, LAST_ITEM)

            @pl.when(ring.core == 0)
            def _():
                self.own[1, pl.ds(CONV_ITEMS * ITEM, LAST_ITEM), :] = self.conv[mine, :]
                self.to_sibling(self.conv.at[tail], 0, LAST_ID, WINDOW, LAST_ITEM).start()

            @pl.when(ring.core == 1)
            def _():
                self.own[0, pl.ds(WINDOW, LAST_ITEM), :] = self.conv[tail, :]
                self.to_sibling(self.conv.at[mine], 1, LAST_ID, CONV_ITEMS * ITEM, LAST_ITEM).start()

    def add_up(self, q, row, count, others):
        @pl.loop(0, count // 96)
        def _(block):
            rows = self.rows(row + block * 96, 96)
            parts = [self.own[q, rows, :]] + [ref[which, rows, :] for ref, which in others]
            self.own[q, rows, :] = added(parts).astype(BF)

    def hop_ring(self, q, ident, row, count, loaded):
        stage = self.stage_of(q)
        if loaded:
            skip = (self.ring.core == 1) & (q == 2) & (ident == EARLY - 1)

            @pl.when(jnp.logical_not(skip))
            def _():
                self.load(q, ident, 0, row, count).wait()

        self.to_sibling(self.own.at[q, self.rows(row, count)], q, ident, row, count).wait_recv()

        @pl.when(stage == 0)
        def _():
            self.add_up(q, row, count, [(self.sibling, q)])

        @pl.when(stage > 0)
        def _():
            self.to_next(q, ident, row, count).wait_recv()
            self.add_up(q, row, count, [(self.sibling, q), (self.ring_in, q)])

        @pl.when(stage < 3)
        def _():
            self.to_next(q, ident, row, count).start()

        @pl.when((stage == 3) & (self.line == 0))
        def _():
            self.to_line(0, 1, 0, ident, row, count).start()

        @pl.when((stage == 3) & (self.line == 3))
        def _():
            self.to_line(0, 2, 0, ident, row, count).start()

    def hop_line(self, ident, row, count):
        place = self.ring.place

        @pl.when(self.line == 2)
        def _():
            self.to_line(0, 1, 0, ident, row, count).wait_recv()
            self.add_up(place, row, count, [(self.z_in, 0)])
            self.to_line(0, 1, 1, ident, row, count).start()

        @pl.when(self.line == 1)
        def _():
            self.to_line(0, 1, 0, ident, row, count).wait_recv()
            self.to_line(0, 1, 1, ident, row, count).wait_recv()
            self.add_up(place, row, count, [(self.z_in, 0), (self.z_in, 1)])
            self.to_line(0, 0, 0, ident, row, count).start()
            self.to_line(1, 2, 1, ident, row, count).start()

    def hop_back(self, ident, row, count):
        @pl.when(self.line == 2)
        def _():
            self.to_line(0, 1, 1, ident, row, count).wait_recv()
            self.to_line(1, 3, 0, ident, row, count, forward=True).start()

        @pl.when(self.line != 2)
        def _():
            self.to_line(0, 1, 0, ident, row, count).wait_recv()

    def streams(self):
        core = self.ring.core

        def first(unit):
            return (unit >= 0) & (unit < 3), unit, WINDOW - 3 * FIRST_ITEM + FIRST_ITEM * unit

        def film(unit):
            item = unit - FIRST_FILM
            return (item >= 0) & (item < FILM_ITEMS), LATE_ID + item, ITEM * item

        def conv(unit):
            at = unit - FIRST_CONV
            item = at - jnp.where(at > 0, 1, 0) - jnp.where(at > 5, 1, 0)
            there = (at >= 0) & (at != 1) & (at != 5) & (item < CONV_ITEMS)
            return there, LATE_ID + item, ITEM * item

        def last(unit):
            return unit == LAST_UNIT, LAST_ID, jnp.where(core == 0, CONV_ITEMS * ITEM, WINDOW)

        return [
            (1, core == 0, FIRST_ITEM, first, True),
            (0, core >= 0, ITEM, film, False),
            (1, core == 0, ITEM, conv, False),
            (1 - core, core >= 0, LAST_ITEM, last, False),
        ]

    def advance(self, unit):
        ring, line = self.ring, self.line

        def early(at):
            return (at >= 0) & (at < EARLY), at, ITEM * at

        @pl.loop(self.low, 4)
        def _(q):
            there, ident, row = early(unit - LAG * self.stage_of(q))

            @pl.when(there)
            def _():
                self.hop_ring(q, ident, row, ITEM, True)

        streams = self.streams()
        for q, has, count, item, loaded in streams:
            there, ident, row = item(unit - LAG * self.stage_of(q))

            @pl.when(has & there)
            def _():
                self.hop_ring(q, ident, row, count, loaded)

        owners = [(ring.place >= self.low, ITEM, early)]
        owners += [(has & (ring.place == q), count, item) for q, has, count, item, _ in streams]
        for owner, count, item in owners:
            there, ident, row = item(unit - LAG * jnp.where(line == 2, 4, 5))

            @pl.when(owner & there & ((line == 1) | (line == 2)))
            def _():
                self.hop_line(ident, row, count)

            there, ident, row = item(unit - LAG * jnp.where(line == 3, 7, 6))

            @pl.when(owner & there & (line != 1))
            def _():
                self.hop_back(ident, row, count)

    def finish(self):
        ring, line = self.ring, self.line
        other = 1 - ring.core

        def sent(q, ident, row, count, owner):
            @pl.when(self.stage_of(q) < 3)
            def _():
                self.to_next(q, ident, row, count).wait_send()

            @pl.when(owner)
            def _():
                self.to_line(0, 1, 0, ident, row, count).wait_send()

                @pl.when((line == 1) | (line == 2))
                def _():
                    self.to_line(1, 1, 0, ident, row, count).wait_send()

        def given(q, ident, row, count):
            self.to_sibling(self.own.at[q, self.rows(row, count)], q, ident, row, count).wait_send()

        @pl.loop(0, EARLY)
        def _(i):
            @pl.loop(self.low, 4)
            def _(q):
                sent(q, i, ITEM * i, ITEM, q == ring.place)

            @pl.loop(2 - other, 4)
            def _(q):
                given(q, i, ITEM * i, ITEM)

            sent(0, LATE_ID + i, ITEM * i, ITEM, ring.place == 0)
            given(0, LATE_ID + i, ITEM * i, ITEM)

        @pl.when(ring.core == 0)
        def _():
            for i in range(3):
                sent(1, i, WINDOW - FIRST_ITEM * (3 - i), FIRST_ITEM, ring.place == 1)

            @pl.loop(0, CONV_ITEMS)
            def _(i):
                sent(1, LATE_ID + i, ITEM * i, ITEM, ring.place == 1)

            sent(1, LAST_ID, CONV_ITEMS * ITEM, LAST_ITEM, ring.place == 1)
            given(0, LAST_ID, WINDOW, LAST_ITEM)

        @pl.when(ring.core == 1)
        def _():
            for i in range(3):
                given(1, i, WINDOW - FIRST_ITEM * (3 - i), FIRST_ITEM)

            @pl.loop(0, CONV_ITEMS)
            def _(i):
                given(1, LATE_ID + i, ITEM * i, ITEM)

            given(1, LAST_ID, CONV_ITEMS * ITEM, LAST_ITEM)
            sent(0, LAST_ID, WINDOW, LAST_ITEM, ring.place == 0)

    def assemble(self, spread):
        ring, line = self.ring, self.line
        place = ring.place

        whole = self.sibling

        @pl.when((line == 0) | (line == 3))
        def _():
            whole[place] = self.z_in[0]

        @pl.when(line == 1)
        def _():
            whole[place] = self.own[place]

        @pl.when(line == 2)
        def _():
            whole[place] = self.z_in[1]

        wide = 2 * CIN // LANES
        for core in range(2):
            height = FILM_HEIGHT[core]

            @pl.when(ring.me == core)
            def _():
                for step in range(BLOCKS):
                    for half in range(2):
                        row = ITEM * (2 * step + half)
                        for a in range(2):
                            tile = half * (CIN // LANES) + 2 * step + a
                            spread[pl.ds(tile, height, stride=wide), :] = whole[
                                0, row + height * a : row + height * (a + 1), :
                            ].astype(F32)
                        if core == 1:
                            spread[pl.ds(height * wide + 96 * (2 * step + half), 96), :] = whole[
                                0, row + 2 * height : row + 2 * height + 96, :
                            ].astype(F32)
                if core == 1:
                    spread[pl.ds(height * wide + TAIL_CONV, LAST_ITEM), :] = whole[0, WINDOW:SLAB, :].astype(F32)

        @pl.when(ring.me > 1)
        def _():
            spread[pl.ds(0, WINDOW), :] = whole[place, 0:WINDOW, :].astype(F32)

    def shard_offset(self):
        me = self.ring.me
        second = self.shard_rows - FILM_FIRST[1] * (2 * CIN // LANES)
        return jnp.where(me == 1, second, self.shard_rows * me % 16)


class Sums:
    def __init__(self, plane, line, plane_sems, line_sems):
        self.ring = Ring()
        self.plane, self.line, self.plane_sems, self.line_sems = plane, line, plane_sems, line_sems

    def plane_copy(self, which, index):
        me = self.ring.me
        return pltpu.make_async_remote_copy(
            src_ref=self.plane.at[which, me],
            dst_ref=self.plane.at[which, me],
            send_sem=self.plane_sems.at[0, which, index],
            recv_sem=self.plane_sems.at[1, which, index],
            device_id={"fsdp": self.ring.others[index]},
            device_id_type=MESH,
        )

    def line_copy(self, hops):
        own = self.ring.replica
        return pltpu.make_async_remote_copy(
            src_ref=self.line.at[own],
            dst_ref=self.line.at[own],
            send_sem=self.line_sems.at[0, hops - 1],
            recv_sem=self.line_sems.at[1, hops - 1],
            device_id={"dp": (own + hops) % 4},
            device_id_type=MESH,
        )

    def give(self, which, value):
        self.plane[which, self.ring.me] = value
        for index in range(self.ring.shards - 1):
            self.plane_copy(which, index).start()

    def take(self, which):
        for index in range(self.ring.shards - 1):
            self.plane_copy(which, index).wait()
        return jnp.sum(self.plane[which], axis=0)

    def give_line(self, value):
        self.line[self.ring.replica] = value
        for hops in (1, 2, 3):
            self.line_copy(hops).start()

    def take_line(self):
        for hops in (1, 2, 3):
            self.line_copy(hops).wait()
        return jnp.sum(self.line[...], axis=0)


def section_back_kernel(
    windows,
    images,
    embedding,
    shifts,
    conv,
    learner,
    gains,
    grid,
    grad_start,
    *rest,
):
    step = pl.program_id(0)
    steps = pl.num_programs(0)
    frames = embedding.shape[0]
    groups = frames // GROUP
    reduces = windows.shards > 1
    if reduces:
        late, sums_in, *rest = rest
    gradient, small_out, *rest = rest
    (
        grad_grid,
        grad_sum,
        learner_sum,
        gain_sum,
        modulated,
        grad_scale,
        conv_sum,
        conv_spread,
        film,
        conv_flat,
        fetch_sems,
        *rest,
    ) = rest
    if reduces:
        patch, own, sibling, ring_in, z_in, sems, z_sems, load_sems, patch_sem, *rest = rest
        reduce = Reduce(
            windows.shard_rows, late, film, conv_flat, patch, own, sibling, ring_in, z_in, sems, z_sems, load_sems, patch_sem
        )
        sums = Sums(*rest)
    wide = D // LANES

    @pl.when(step == 0)
    def _():
        if reduces:
            reduce.greet()
            reduce.start_early()
            sums.give(0, sums_in[...])
        learner_sum[...] = jnp.zeros_like(learner_sum)
        gain_sum[...] = jnp.zeros_like(gain_sum)

        def first_part(fetched, tokens_fetched):
            def fetch(g, slot):
                return (
                    pltpu.make_async_copy(
                        grid.at[pl.ds(pl.multiple_of(g * CELLS, 16), CELLS)], fetched.at[slot], fetch_sems.at[slot]
                    ),
                    pltpu.make_async_copy(
                        grad_start.at[pl.ds(pl.multiple_of(g * SLOTS, SLOTS), SLOTS)],
                        tokens_fetched.at[slot],
                        fetch_sems.at[2 + slot],
                    ),
                )

            for copy in fetch(0, 0):
                copy.start()

            @pl.loop(0, groups)
            def _(g):
                slot = g % 2
                for copy in fetch(g, slot):
                    copy.wait()

                @pl.when(g + 1 < groups)
                def _():
                    for copy in fetch(g + 1, 1 - slot):
                        copy.start()

                rows = pl.ds(pl.multiple_of(g * CELLS, 16), CELLS)
                unit, inverse = norm_rows(fetched[slot].astype(F32))
                normed = (unit * gains[0:1, :]).astype(BF)
                maps = jax.nn.sigmoid(mm(normed, learner[...]))
                mask = own_frame(CELLS)
                tokens = (tokens_fetched[slot] * (1.0 / POS)).astype(BF)
                grad_maps = mm_nt(normed, tokens)
                grad_logit = jnp.where(mask, grad_maps * maps * (1.0 - maps), 0.0).astype(BF)
                maps = jnp.where(mask, maps, 0.0).astype(BF)
                grad_normed = mm(maps, tokens) + mm_nt(grad_logit, learner[...])
                learner_sum[...] += mm_tn(normed, grad_logit)
                gain_sum[...] += jnp.sum(grad_normed * unit, axis=0, keepdims=True)
                back = norm_back(unit, inverse, gains[0:1, :], grad_normed).astype(BF)
                grad_grid[rows, :] = back
                grad_sum[pl.ds(pl.multiple_of(g * GROUP, GROUP), GROUP), :] = jnp.sum(
                    back.astype(F32).reshape(POS, GROUP, D), axis=0
                )
                if reduces:
                    reduce.advance(g)

        pl.run_scoped(
            first_part, pltpu.VMEM((2, CELLS, D), BF), pltpu.VMEM((2, SLOTS, D), F32)
        )

        total = learner_sum[...]
        high = total.astype(BF)
        token = same_token()
        spread_learner = mm(high, token) + mm((total - high.astype(F32)).astype(BF), token)
        spread_learner = jnp.where(learner_mask(), spread_learner, 0.0)
        conv_flat[pl.ds(CIN * wide, D * NT // LANES), :] = jnp.sum(
            spread_learner.reshape(D * NT // LANES, GROUP, LANES), axis=1
        ).astype(BF)
        if reduces:
            rows = [gain_sum[:, LANES * j : LANES * (j + 1)] for j in range(wide)]
            reduce.patch_gains(jnp.concatenate(rows + [jnp.zeros((16 - wide, LANES), F32)], axis=0))
            sums.give_line(sums.take(0))
        else:
            small_out[...] = gain_sum[...]

    channels = pl.ds(pl.multiple_of(step * BLOCK, BLOCK), BLOCK)
    weights = conv[channels, :]

    conv_sum[...] = jnp.zeros_like(conv_sum)
    for g in range(groups):
        rows = pl.ds(g * CELLS, CELLS)
        here = pl.ds(g * GROUP, GROUP)
        scale = 1.0 + shifts[0, here, :]
        offset = shifts[1, here, :]
        cells = images[:, here, :].astype(F32)
        modulated[...] = (cells * scale[None] + offset[None]).astype(BF).reshape(CELLS, BLOCK)
        back = grad_grid[rows, :]
        conv_sum[...] += mm_tn(modulated[...], back)
        grad_modulated = mm_nt(back, weights).reshape(POS, GROUP, BLOCK)
        grad_scale[here, :] = jnp.sum(grad_modulated * cells, axis=0)
        if reduces and g == groups // 2 - 1:
            reduce.advance(6 + 2 * step)
    total = grad_sum[...]
    high = total.astype(BF)
    grad_offset = mm_nt(high, weights) + mm_nt((total - high.astype(F32)).astype(BF), weights)

    for j in range(wide):
        conv_spread[pl.ds(j, BLOCK, stride=wide), :] = conv_sum[:, LANES * j : LANES * (j + 1)]
    conv_flat[pl.ds(pl.multiple_of(step * BLOCK * wide, 16), BLOCK * wide), :] = conv_spread[...].astype(BF)
    for side, grad in enumerate((grad_scale[...], grad_offset)):
        part = mm_tn(embedding[...], grad.astype(BF)).astype(BF)
        for i in range(BLOCK // LANES):
            film[side * (CIN // LANES) + step * (BLOCK // LANES) + i] = part[:, LANES * i : LANES * (i + 1)]
    if reduces:
        reduce.give_film(step)
        reduce.give_conv(step)
        reduce.advance(7 + 2 * step)

    @pl.when(step == steps - 1)
    def _():
        if not reduces:
            copies = [
                pltpu.make_async_copy(film, gradient[0], fetch_sems.at[0]),
                pltpu.make_async_copy(conv_flat, gradient[1], fetch_sems.at[1]),
            ]
            for copy in copies:
                copy.start()
            for copy in copies:
                copy.wait()
            return

        @pl.loop(COMPUTE_UNITS, UNITS)
        def _(unit):
            reduce.advance(unit)

        def last_part(spread):
            count = gradient.shape[0]
            reduce.assemble(spread)
            offset = reduce.shard_offset()
            squares = jnp.zeros((8, LANES), F32)

            def move(block, squares):
                part = spread[pl.ds(offset + block * 8, 8), :]
                spread[pl.ds(pl.multiple_of(block * 8, 8), 8), :] = part
                kept = lax.broadcasted_iota(jnp.int32, (8, LANES), 0) + block * 8 < windows.shard_rows
                part = jnp.where(kept, part, 0.0)
                return squares + part * part

            squares = lax.fori_loop(0, count // 8, move, squares)
            out = pltpu.make_async_copy(spread.at[pl.ds(0, count)], gradient, fetch_sems.at[0])
            out.start()
            sums.give(1, squares)
            total = sums.take_line()
            total_squares = jnp.sum(sums.take(1))
            place_row = lax.broadcasted_iota(jnp.int32, (8, LANES), 0)
            small_out[...] = jnp.where(place_row == SQUARES, total_squares, total)
            reduce.finish()
            out.wait()

        pl.run_scoped(last_part, pltpu.VMEM((SLAB + 8, LANES), F32))


def section_back(windows, images, embedding, shifts, conv, learner, gains, grid, grad_start, late, sums):
    frames = embedding.shape[0]
    reduces = windows.shards > 1
    whole = lambda *shape: pl.BlockSpec(
        shape, lambda i: (0,) * len(shape), pipeline_mode=pl.Buffered(1)
    )
    anywhere = pl.BlockSpec(memory_space=pl.ANY)
    shard_rows = -(-windows.shard_rows // 8) * 8
    film_shape = jax.ShapeDtypeStruct((2 * CIN // LANES, E, LANES), BF)
    conv_shape = jax.ShapeDtypeStruct(((CIN * D + D * NT) // LANES, LANES), BF)
    slab = lambda count: pltpu.VMEM((count, SLAB, LANES), BF)
    scratch = [
        pltpu.VMEM((frames * POS, D), BF),
        pltpu.VMEM((frames, D), F32),
        pltpu.VMEM((D, SLOTS), F32),
        pltpu.VMEM((1, D), F32),
        pltpu.VMEM((CELLS, BLOCK), BF),
        pltpu.VMEM((frames, BLOCK), F32),
        pltpu.VMEM((BLOCK, D), F32),
        pltpu.VMEM((BLOCK * D // LANES, LANES), F32),
        pltpu.VMEM(film_shape.shape, BF),
        pltpu.VMEM(conv_shape.shape, BF),
        pltpu.SemaphoreType.DMA((4,)),
    ]
    if reduces:
        scratch += [
            pltpu.VMEM((ITEM, LANES), BF),
            slab(4),
            slab(4),
            slab(4),
            slab(2),
            pltpu.SemaphoreType.DMA((4, 4, IDS)),
            pltpu.SemaphoreType.DMA((4, IDS)),
            pltpu.SemaphoreType.DMA((4, EARLY)),
            pltpu.SemaphoreType.DMA((1,)),
            pltpu.VMEM((2, 8, 8, LANES), F32),
            pltpu.VMEM((4, 8, LANES), F32),
            pltpu.SemaphoreType.DMA((2, 2, 7)),
            pltpu.SemaphoreType.DMA((2, 3)),
        ]
        outs = [jax.ShapeDtypeStruct((shard_rows, LANES), F32), jax.ShapeDtypeStruct((8, LANES), F32)]
        out_specs = [anywhere, whole(8, LANES)]
    else:
        outs = [(film_shape, conv_shape), jax.ShapeDtypeStruct((1, D), F32)]
        out_specs = [(anywhere, anywhere), whole(1, D)]
    return pl.pallas_call(
        functools.partial(section_back_kernel, windows),
        grid=(BLOCKS,),
        in_specs=[
            pl.BlockSpec((POS, frames, BLOCK), lambda i: (0, 0, i)),
            whole(frames, E),
            pl.BlockSpec((2, frames, BLOCK), lambda i: (0, 0, i)),
            whole(CIN, D),
            whole(D, SLOTS),
            whole(4, D),
            anywhere,
            anywhere,
        ]
        + [anywhere, whole(8, LANES)] * reduces,
        out_specs=out_specs,
        out_shape=outs,
        scratch_shapes=scratch,
        compiler_params=pltpu.CompilerParams(
            vmem_limit_bytes=63 * MIB,
            **(dict(collective_id=1, has_side_effects=True) if reduces else {}),
        ),
        cost_estimate=pl.CostEstimate(
            flops=4 * frames * POS * CIN * D, bytes_accessed=frames * POS * CIN * 2, transcendentals=0
        ),
    )(
        images,
        embedding,
        shifts.reshape(frames, 2, CIN).transpose(1, 0, 2),
        conv,
        learner,
        gains,
        grid,
        grad_start,
        *([late, sums] if reduces else []),
    )


def on_device(
    images, embedding, episode, valid_steps, targets, master, first_moment, second_moment, average
):
    images = images.transpose(1, 0, 2)
    replicas, shards = lax.axis_size("dp"), lax.axis_size("fsdp")
    if fits_ring(replicas, shards, master.shape[0]):
        windows = Windows(shards, master.shape[0] // LANES, WINDOW)
        flat = master.reshape(-1, LANES)
    else:
        whole_flat = lax.all_gather(master.astype(BF), "fsdp", axis=0, tiled=True)
        flat = jnp.pad(whole_flat.reshape(ROWS, LANES), ((0, FLAT_ROWS - ROWS), (0, 0)))[None]
        windows = Windows(1, ROWS, FLAT_ROWS)

    grid, start, shifts, conv, learner, gains, *gathered = section(windows, images, embedding, flat)
    if gathered:
        (flat,) = gathered
    grad_start, late, sums = layer(windows, start, flat, gains, episode, valid_steps, targets)
    back, small = section_back(
        windows, images, embedding, shifts, conv, learner, gains, grid, grad_start, late, sums
    )
    if gathered:
        loss_sum, step_count, squares = small[0, 0], small[1, 0], small[SQUARES, 0]
        inverse_count = 1.0 / step_count
        grad_shard = back.reshape(-1)[: master.shape[0]] * inverse_count
        squares = squares * inverse_count * inverse_count
    else:
        film, conv_flat = back
        at = START["gains"] - HEAD_PART
        late = late[: ROWS - HEAD_PART].at[at : at + 4].set(small.reshape(4, LANES).astype(BF))
        gradient = jnp.concatenate([film.transpose(1, 0, 2).reshape(-1, LANES), conv_flat, late])
        loss_sum, step_count = lax.psum((sums[0, 0], sums[1, 0]), ("dp", "fsdp"))
        partial_shard = lax.psum_scatter(gradient.reshape(-1), "fsdp", scatter_dimension=0, tiled=True)
        grad_shard = lax.psum(partial_shard.astype(F32), "dp") / step_count
        squares = lax.psum(jnp.sum(grad_shard * grad_shard), "fsdp")
    grad_norm = jnp.sqrt(squares)
    clipped = grad_shard * (CLIP_NORM / jnp.maximum(grad_norm, CLIP_NORM))
    new_first = MOMENT_DECAY * first_moment + (1.0 - MOMENT_DECAY) * clipped
    new_second = MOMENT_DECAY * second_moment + (1.0 - MOMENT_DECAY) * clipped * clipped
    correction = 1.0 - MOMENT_DECAY**STEP
    new_master = master - LEARN_RATE * (
        new_first / correction / (jnp.sqrt(new_second / correction) + ADAM_EPSILON)
        + WEIGHT_DECAY * master
    )
    average_decay = min(AVERAGE_DECAY, (1.0 + STEP) / (10.0 + STEP))
    new_average = average_decay * average + (1.0 - average_decay) * new_master
    return (
        new_master,
        new_first,
        new_second,
        new_average,
        new_master.astype(BF),
        grad_norm,
        loss_sum,
        step_count,
    )


def solution(mesh):
    in_specs = (
        P(("dp", "fsdp"), None, None),
        P(("dp", "fsdp"), None),
        P(("dp", "fsdp")),
        P(("dp", "fsdp")),
        P(("dp", "fsdp"), None),
        P("fsdp"),
        P("fsdp"),
        P("fsdp"),
        P("fsdp"),
    )
    out_specs = (P("fsdp"), P("fsdp"), P("fsdp"), P("fsdp"), P("fsdp"), P(), P(), P())
    return jax.shard_map(
        on_device, mesh=mesh, in_specs=in_specs, out_specs=out_specs, check_vma=False
    )
```

```python
import functools

import jax
import jax.numpy as jnp
from jax import lax
from jax.experimental import pallas as pl
from jax.experimental.pallas import tpu as pltpu
from jax.sharding import PartitionSpec as P

D = 512
HEADS = 8
HD = 64
FF = 2048
E = 512
CIN = 1536
POS = 81
NT = 8
ACT = 11
BINS = 256
STEP = 10
LANES = 128
GROUP = 16
CELLS = POS * GROUP
SLOTS = GROUP * NT

MOMENT_DECAY = 0.5
LEARN_RATE = 0.02
WEIGHT_DECAY = 0.1
CLIP_NORM = 1.0
ADAM_EPSILON = 1e-08
AVERAGE_DECAY = 0.999
BF = jnp.bfloat16
F32 = jnp.float32
MIB = 2**20

SHAPES = {
    "film": (E, 2 * CIN),
    "conv": (CIN, D),
    "learner": (D, NT),
    "triple": (D, 3 * D),
    "output": (D, D),
    "upward": (D, FF),
    "downward": (FF, D),
    "action": (D, ACT * BINS),
    "gains": (4, D),
}


def row_starts():
    starts, row = {}, 0
    for name, (height, breadth) in SHAPES.items():
        starts[name] = row
        row += height * breadth // LANES
    return starts, row


START, ROWS = row_starts()
FLAT_ROWS = ROWS + 16
HEAD_PART = START["triple"]
LATE_ROWS = ROWS - HEAD_PART + 112


def mm(a, b):
    return jnp.dot(a, b, preferred_element_type=F32)


def mm_nt(a, b):
    return lax.dot_general(a, b, (((1,), (1,)), ((), ())), preferred_element_type=F32)


def mm_tn(a, b):
    return lax.dot_general(a, b, (((0,), (0,)), ((), ())), preferred_element_type=F32)


class Windows:
    def __init__(self, shards, shard_rows, size):
        self.shards, self.shard_rows, self.size = shards, shard_rows, size
        self.first = [shard_rows * k // 16 * 16 for k in range(shards)]

    def pieces(self, start, stop):
        inner, shared = [], []
        for k in range(self.shards):
            low, high = self.shard_rows * k, self.shard_rows * (k + 1)
            if k == self.shards - 1:
                high = (high + 15) // 16 * 16
            a, b = max(start, -(-low // 16) * 16), min(stop, high // 16 * 16)
            if a < b:
                inner.append((k, a - self.first[k], a, b - a))
            edge = low // 16 * 16
            if low % 16 and start <= edge < stop:
                shared.append((k - 1, edge - self.first[k - 1], k, edge - self.first[k], edge))
        return inner, shared

    def load(self, flat_ref, stage, edges, sem, parts):
        copies, fixes = [], []
        for start, stop, place in parts:
            inner, shared = self.pieces(start, stop)
            for k, offset, row, count in inner:
                copies.append(
                    pltpu.make_async_copy(
                        flat_ref.at[k, pl.ds(offset, count)],
                        stage.at[pl.ds(place + row - start, count)],
                        sem.at[len(copies)],
                    )
                )
            for k, offset, l, other, row in shared:
                for side, (window, at) in enumerate(((k, offset), (l, other))):
                    copies.append(
                        pltpu.make_async_copy(
                            flat_ref.at[window, pl.ds(at, 16)],
                            edges.at[len(fixes), side],
                            sem.at[len(copies)],
                        )
                    )
                fixes.append(place + row - start)
        for copy in copies:
            copy.start()
        for copy in copies:
            copy.wait()
        for index, row in enumerate(fixes):
            stage[pl.ds(row, 16), :] = edges[index, 0] + edges[index, 1]


MESH = pl.DeviceIdType.MESH
CHUNK = 768
CHUNKS = 9
WINDOW = CHUNK * CHUNKS
CARRIED = 2 * CHUNKS // 3
TRADED = CHUNKS // 3
NEEDED = 7
READY, READY_TRADED = 5, 2
TAKEN = ((0, 2, 4, 6, 6, 6), (0, 0, 2, 4, 6, 6))


def fits_ring(replicas, shards, shard_size):
    return shards == 8 and replicas == 4 and shard_size % LANES == 0 and shard_size <= LANES * (WINDOW - 16)


def gray(place):
    return place + (place // 2) * (1 - 2 * (place % 2))


class Ring:
    def __init__(self):
        self.me = lax.axis_index("fsdp")
        self.core = self.me % 2
        self.place = self.flip(gray(self.me // 2))
        self.replica = lax.axis_index("dp")
        self.half = self.replica % 2
        self.sibling = self.me + 1 - 2 * self.core
        self.after = self.device(self.place + 1)
        self.before = self.device(self.place + 3)
        self.partner = self.replica + 1 - 2 * self.half
        self.shards = lax.axis_size("fsdp")
        self.others = [(self.me + 1 + index) % self.shards for index in range(self.shards - 1)]

    def flip(self, place):
        return (place + self.core * (4 - 2 * place)) % 4

    def device(self, place):
        return gray(self.flip(place % 4)) * 2 + self.core

    def pick(self, table, place):
        found = jnp.int32(0)
        for index, value in enumerate(table):
            found = found + jnp.where(place == index, value, 0)
        return found


class Gather:
    def __init__(self, own, whole, gain_rows, around, across, trade, own_sems):
        self.ring, self.own, self.whole, self.gain_rows = Ring(), own, whole, gain_rows
        self.around_sems, self.across_sems, self.trade_sems, self.own_sems = around, across, trade, own_sems
        core, place = self.ring.core, self.ring.place
        self.first = [CARRIED, jnp.where(core == 0, READY, 0), 0, 0]
        self.first_traded = [TRADED, jnp.where(core == 0, READY_TRADED, 0), 0, 0]

    def greet(self):
        barrier = pltpu.get_barrier_semaphore()
        for device in [{"fsdp": other} for other in self.ring.others] + [{"dp": self.ring.partner}]:
            pl.semaphore_signal(barrier, inc=1, device_id=device, device_id_type=MESH)
        pl.semaphore_wait(barrier, self.ring.shards)

    def gain_copy(self, index):
        return pltpu.make_async_remote_copy(
            src_ref=self.gain_rows,
            dst_ref=self.gain_rows,
            send_sem=self.own_sems.at[3 + index],
            recv_sem=self.own_sems.at[2],
            device_id={"fsdp": self.ring.others[index]},
            device_id_type=MESH,
        )

    def send_gains(self, place):
        @pl.when(self.ring.me == self.ring.shards - 1)
        def _():
            self.gain_rows[...] = self.own[pl.ds(place, 16), :]
            for index in range(self.ring.shards - 1):
                self.gain_copy(index).start()

    def take_gains(self):
        last = self.ring.me == self.ring.shards - 1

        @pl.when(last)
        def _():
            for index in range(self.ring.shards - 1):
                self.gain_copy(index).wait_send()

        @pl.when(jnp.logical_not(last))
        def _():
            self.gain_copy(0).wait_recv()

    def carried(self, j):
        return (j // 2) * 3 + (j % 2) * (1 + self.ring.half)

    def rows(self, i):
        return pl.ds(pl.multiple_of(i * CHUNK, 16), CHUNK)

    def copy(self, window, i, send_sem, recv_sem, device, own=False):
        source = self.own.at[self.rows(i)] if own else self.whole.at[window, self.rows(i)]
        return pltpu.make_async_remote_copy(
            src_ref=source,
            dst_ref=self.whole.at[window, self.rows(i)],
            send_sem=send_sem,
            recv_sem=recv_sem,
            device_id=device,
            device_id_type=MESH,
        )

    def around(self, origin, j, own=False):
        sems = self.around_sems
        return self.copy(
            self.ring.me if own else self.ring.device(origin),
            self.carried(j),
            sems.at[0, origin, j],
            sems.at[1, origin, j],
            {"fsdp": self.ring.after},
            own,
        )

    def across(self, origin, i):
        sems = self.across_sems
        return self.copy(
            self.ring.device(origin), i, sems.at[0, origin, i], sems.at[1, origin, i], {"fsdp": self.ring.sibling}
        )

    def trade(self, origin, j, half):
        sems = self.trade_sems
        return self.copy(
            self.ring.device(origin),
            3 * j + 1 + half,
            sems.at[0, origin, j],
            sems.at[1, origin, j],
            {"dp": self.ring.partner},
        )

    def own_copies(self):
        ring = self.ring
        keep = pltpu.make_async_copy(self.own, self.whole.at[ring.me], self.own_sems.at[10])
        give = pltpu.make_async_remote_copy(
            src_ref=self.own,
            dst_ref=self.whole.at[ring.me],
            send_sem=self.own_sems.at[1],
            recv_sem=self.own_sems.at[0],
            device_id={"fsdp": ring.sibling},
            device_id_type=MESH,
        )
        return keep, give

    def take(self, origin, low, high):
        low = jnp.where(self.ring.place == origin, high, low)

        @pl.loop(low, high)
        def _(j):
            self.around(origin, j).wait_recv()

            @pl.when(origin != (self.ring.place + 1) % 4)
            def _():
                self.around(origin, j).start()

            @pl.when(j % 2 == 1)
            def _():
                self.trade(origin, j // 2, self.ring.half).start()

            self.across(origin, self.carried(j)).start()

    def take_traded(self, origin, low, high):
        other = 1 - self.ring.half
        low = jnp.where(self.ring.place == origin, high, low)

        @pl.loop(low, high)
        def _(j):
            self.trade(origin, j, other).wait_recv()
            self.across(origin, 3 * j + 1 + other).start()

    def wait_across(self, origin, low, high):
        sibling_place = (4 - self.ring.place) % 4
        low = jnp.where(sibling_place == origin, high, low)

        @pl.loop(low, high)
        def _(i):
            self.across(origin, i).wait_recv()

    def send_own(self, low, high):
        @pl.loop(low, high)
        def _(j):
            self.around(self.ring.place, j, own=True).start()

    def begin(self, gain_place):
        place = self.ring.place
        first = self.first[1]
        self.greet()
        self.send_gains(gain_place)
        self.send_own(0, jnp.where(place == 1, first, jnp.where(place == 2, 0, CARRIED)))
        keep, give = self.own_copies()
        keep.start()
        give.start()
        self.take(3, 0, jnp.where(place == 0, CARRIED, 0))
        self.take(1, 0, first)
        self.take(0, 0, CARRIED)
        self.send_own(jnp.where(place == 1, first, jnp.where(place == 2, 0, CARRIED)), CARRIED)
        self.take(3, 0, jnp.where(place == 1, CARRIED, 0))
        for origin in (1, 0):
            self.take_traded(origin, 0, self.first_traded[origin])
        self.take_gains()
        keep.wait()
        give.wait_recv()
        self.wait_across(0, 0, CHUNKS)
        self.wait_across(1, 0, jnp.where(self.ring.core == 1, NEEDED, 0))

    def taken(self, origin, step):
        hops = (self.ring.place + 4 - origin) % 4
        early = (origin == 3) & (hops < 3)
        count = jnp.where(hops == 2, self.ring.pick(TAKEN[0], step), self.ring.pick(TAKEN[1], step))
        count = jnp.where((hops == 1) | (origin == 3), jnp.where(step >= 0, CARRIED, 0), count)
        return jnp.maximum(jnp.where(early, CARRIED, count), self.first[origin])

    def go_on(self, step, steps):
        for origin in (3, 2, 1):
            self.take(origin, self.taken(origin, step - 1), self.taken(origin, step))
        for origin in (3, 2, 1):
            first = self.first_traded[origin]
            low = jnp.maximum(first, jnp.where(step == 0, 0, self.taken(origin, step - 2) // 2))
            high = jnp.maximum(first, jnp.where(step == steps - 1, TRADED, self.taken(origin, step - 1) // 2))
            self.take_traded(origin, low, high)

        @pl.when(step == steps - 1)
        def _():
            self.finish()

    def finish(self):
        place = self.ring.place
        self.wait_across(1, jnp.where(self.ring.core == 1, NEEDED, 0), CHUNKS)
        self.wait_across(2, 0, CHUNKS)
        self.wait_across(3, 0, CHUNKS)
        self.own_copies()[1].wait_send()
        for origin in range(4):

            @pl.loop(0, jnp.where((place + 1) % 4 == origin, 0, CARRIED))
            def _(j):
                self.around(origin, j).wait_send()

            @pl.loop(0, jnp.where(place == origin, 0, TRADED))
            def _(j):
                self.trade(origin, j, self.ring.half).wait_send()

            @pl.loop(0, jnp.where(place == origin, 0, CHUNKS))
            def _(i):
                self.across(origin, i).wait_send()


GATHER_SCRATCH = [
    pltpu.VMEM((WINDOW, LANES), BF),
    pltpu.VMEM((16, LANES), BF),
    pltpu.SemaphoreType.DMA((2, 4, CARRIED)),
    pltpu.SemaphoreType.DMA((2, 4, CHUNKS)),
    pltpu.SemaphoreType.DMA((2, 4, TRADED)),
    pltpu.SemaphoreType.DMA((11,)),
]


def to_matrix(stage, place, spread, matrix, shape, height=512):
    wide = shape[1] // LANES
    for top in range(0, shape[0], height):
        rows = height * wide
        spread[pl.ds(0, rows), :] = stage[pl.ds(place + top * wide, rows), :].astype(F32)
        for j in range(wide):
            matrix[top : top + height, LANES * j : LANES * (j + 1)] = spread[
                pl.ds(j, height, stride=wide), :
            ].astype(BF)


def norm_rows(values):
    centre = jnp.mean(values, axis=-1, keepdims=True)
    shifted = values - centre
    inverse = lax.rsqrt(jnp.mean(shifted * shifted, axis=-1, keepdims=True) + 1e-05)
    return shifted * inverse, inverse


def norm_back(unit, inverse, gain, grad):
    scaled = grad * gain
    along = jnp.mean(scaled * unit, axis=-1, keepdims=True)
    return inverse * (scaled - jnp.mean(scaled, axis=-1, keepdims=True) - unit * along)


def own_frame(rows):
    frame = lax.broadcasted_iota(jnp.int32, (rows // GROUP, GROUP, SLOTS), 1).reshape(rows, SLOTS)
    return frame == lax.broadcasted_iota(jnp.int32, (rows, SLOTS), 1) // NT


def same_token():
    a = lax.broadcasted_iota(jnp.int32, (SLOTS, SLOTS), 0) % NT
    b = lax.broadcasted_iota(jnp.int32, (SLOTS, SLOTS), 1) % NT
    return (a == b).astype(BF)


def learner_mask():
    return own_frame(D)


def section_kernel(
    windows,
    images,
    embedding,
    flat,
    grid_out,
    pooled_out,
    shifts_out,
    conv_out,
    learner_out,
    gains_out,
    *rest,
):
    step = pl.program_id(0)
    if windows.shards > 1:
        master = flat
        flat, stage, spread, film, modulated, edges, sems, own, *gather_sems = rest
        gather = Gather(own, flat, *gather_sems)
    else:
        gather = None
        stage, spread, film, modulated, edges, sems = rest

    @pl.when(step == 0)
    def _():
        if gather:
            rows = master.shape[0]
            spread[pl.ds(0, 16), :] = jnp.zeros((16, LANES), F32)
            tail = rows // 16 * 16
            spread[pl.ds(tail, WINDOW - tail), :] = jnp.zeros((WINDOW - tail, LANES), F32)
            spread[pl.ds(gather.ring.me * rows % 16, rows), :] = master[...]
            own[...] = spread[pl.ds(0, WINDOW), :].astype(BF)
            gather.begin(START["gains"] - windows.first[-1])
        learner_rows = HEAD_PART - START["learner"]
        parts = [(0, HEAD_PART, 0)]
        if gather is None:
            parts.append((START["gains"], ROWS, HEAD_PART))
        windows.load(flat, stage, edges, sems, parts)
        if gather:
            stage[pl.ds(HEAD_PART, 16), :] = gather.gain_rows[...]
        to_matrix(stage, 0, spread, film, SHAPES["film"])
        for side in range(2):
            shifts_out[side] = mm(embedding[...], film[:, CIN * side : CIN * (side + 1)])
        to_matrix(stage, START["conv"], spread, conv_out, SHAPES["conv"])
        packed = stage[pl.ds(START["learner"], learner_rows), :].astype(F32)
        opened = jnp.broadcast_to(packed[:, None, :], (learner_rows, GROUP, LANES)).reshape(D, SLOTS)
        opened = jnp.where(learner_mask(), opened, 0.0).astype(BF)
        learner_out[...] = mm(opened, same_token()).astype(BF)
        gain_rows = stage[pl.ds(HEAD_PART, 16), :].astype(F32)
        for i in range(4):
            for j in range(4):
                gains_out[i : i + 1, LANES * j : LANES * (j + 1)] = gain_rows[4 * i + j : 4 * i + j + 1]

    here = pl.ds(pl.multiple_of(step * GROUP, GROUP), GROUP)
    scale = 1.0 + shifts_out[0, here, :]
    offset = shifts_out[1, here, :]
    modulated[...] = (images[...].astype(F32) * scale[None] + offset[None]).astype(BF).reshape(CELLS, CIN)
    grid = mm(modulated[...], conv_out[...])
    grid_out[...] = grid.astype(BF)
    unit, _ = norm_rows(grid)
    normed = (unit * gains_out[0:1, :]).astype(BF)
    maps = jax.nn.sigmoid(mm(normed, learner_out[...]))
    maps = jnp.where(own_frame(CELLS), maps, 0.0).astype(BF)
    pooled_out[...] = mm_tn(maps, normed) * (1.0 / POS)
    if gather:
        gather.go_on(step, pl.num_programs(0))


def section(windows, images, embedding, flat):
    frames = images.shape[1]
    steps = frames // GROUP
    whole = lambda *shape: pl.BlockSpec(shape, lambda i: (0,) * len(shape))
    gathers = windows.shards > 1
    film_rows = SHAPES["film"][0] * SHAPES["film"][1] // LANES
    return pl.pallas_call(
        functools.partial(section_kernel, windows),
        grid=(steps,),
        in_specs=[
            pl.BlockSpec((POS, GROUP, CIN), lambda i: (0, i, 0)),
            whole(frames, E),
            whole(*flat.shape) if gathers else pl.BlockSpec(memory_space=pl.ANY),
        ],
        out_specs=[
            pl.BlockSpec((CELLS, D), lambda i: (i, 0)),
            pl.BlockSpec((SLOTS, D), lambda i: (i, 0)),
            whole(2, frames, CIN),
            whole(CIN, D),
            whole(D, SLOTS),
            whole(4, D),
        ]
        + [pl.BlockSpec(memory_space=pl.ANY)] * gathers,
        out_shape=[
            jax.ShapeDtypeStruct((steps * CELLS, D), BF),
            jax.ShapeDtypeStruct((frames * NT, D), F32),
            jax.ShapeDtypeStruct((2, frames, CIN), F32),
            jax.ShapeDtypeStruct((CIN, D), BF),
            jax.ShapeDtypeStruct((D, SLOTS), BF),
            jax.ShapeDtypeStruct((4, D), F32),
        ]
        + [jax.ShapeDtypeStruct((windows.shards, WINDOW, LANES), BF)] * gathers,
        scratch_shapes=[
            pltpu.VMEM((HEAD_PART + 16, LANES), BF),
            pltpu.VMEM((film_rows + 32, LANES), F32),
            pltpu.VMEM(SHAPES["film"], BF),
            pltpu.VMEM((CELLS, CIN), BF),
            pltpu.VMEM((8, 2, 16, LANES), BF),
            pltpu.SemaphoreType.DMA((32,)),
        ]
        + GATHER_SCRATCH * gathers,
        compiler_params=pltpu.CompilerParams(
            vmem_limit_bytes=60 * MIB,
            **(dict(collective_id=0, has_side_effects=True) if gathers else {}),
        ),
        cost_estimate=pl.CostEstimate(
            flops=2 * frames * POS * CIN * D, bytes_accessed=frames * POS * CIN * 2, transcendentals=0
        ),
    )(images, embedding, flat)


def gelu_parts(x):
    inner = 0.7978845608028654 * (x + 0.044715 * x * x * x)
    bent = jnp.tanh(inner)
    value = 0.5 * x * (1.0 + bent)
    slope = 0.5 * (1.0 + bent) + 0.5 * x * (1.0 - bent * bent) * 0.7978845608028654 * (
        1.0 + 3.0 * 0.044715 * x * x
    )
    return value, slope


TOP = 256


def layer_part(
    windows,
    refs,
    reduce,
    late_out,
    stage,
    spread,
    triple,
    output,
    upward,
    downward,
    action,
    keys,
    values,
    grad_keys,
    grad_values,
    shares,
    first_normed,
    logits_back,
    edges,
    sems,
):
    start, flat, gains, episode_row, episode_last, valid, targets, grad_start, sums_out = refs
    tokens = start.shape[0]
    frames = tokens // NT
    place = {name: START[name] - HEAD_PART for name in SHAPES}
    windows.load(flat, stage, edges, sems, [(HEAD_PART, START["gains"], 0)])
    for name, matrix in (
        ("triple", triple),
        ("output", output),
        ("upward", upward),
        ("downward", downward),
        ("action", action),
    ):
        to_matrix(stage, place[name], spread, matrix, SHAPES[name], TOP)
    is_last = lax.broadcasted_iota(jnp.int32, (tokens, D), 0) % NT == NT - 1

    def take_last(rows):
        return jnp.sum(jnp.where(is_last, rows, 0.0).reshape(frames, NT, D), axis=1)

    def spread_last(rows):
        wide = jnp.broadcast_to(rows[:, None, :], (frames, NT, D)).reshape(tokens, D)
        return jnp.where(is_last, wide, 0.0)

    gain = [gains[i : i + 1, :] for i in range(4)]

    first_unit, first_inverse = norm_rows(start[...])
    first_normed[...] = (first_unit * gain[1]).astype(BF)
    last_start = take_last(start[...])
    last_unit, _ = norm_rows(last_start)
    last_normed = (last_unit * gain[1]).astype(BF)
    queries = mm(last_normed, triple[:, :D]).astype(BF)
    keys[...] = mm(first_normed[...], triple[:, D : 2 * D]).astype(BF)
    values[...] = mm(first_normed[...], triple[:, 2 * D :]).astype(BF)
    key_place = lax.broadcasted_iota(jnp.int32, (frames, tokens), 1)
    query_place = lax.broadcasted_iota(jnp.int32, (frames, tokens), 0) * NT + (NT - 1)
    allowed = (episode_last[...] == episode_row[...]) & (key_place <= query_place)
    attended = []
    for h in range(HEADS):
        own = slice(HD * h, HD * (h + 1))
        scores = mm_nt(queries[:, own], keys[:, own]) * HD ** (-0.5)
        scores = jnp.where(allowed, scores, -1e30)
        powers = jnp.exp(scores - jnp.max(scores, axis=-1, keepdims=True))
        part = powers / jnp.sum(powers, axis=-1, keepdims=True)
        shares[h] = part
        attended.append(mm(part.astype(BF), values[:, own]))
    merged = jnp.concatenate(attended, axis=1).astype(BF)
    middle = last_start + mm(merged, output[...])
    second_unit, second_inverse = norm_rows(middle)
    second_normed = (second_unit * gain[2]).astype(BF)
    activated, slope = gelu_parts(mm(second_normed, upward[...]))
    hidden = activated.astype(BF)
    end = middle + mm(hidden, downward[...])
    final_unit, final_inverse = norm_rows(end)
    final_rows = (final_unit * gain[3]).astype(BF)

    valid_flags = valid[...].astype(F32)
    bins = lax.broadcasted_iota(jnp.int32, (frames, BINS), 1)
    loss = jnp.zeros((frames, 1), F32)
    for a in range(ACT):
        own = slice(BINS * a, BINS * (a + 1))
        logits = mm(final_rows, action[:, own])
        shifted = logits - jnp.max(logits, axis=-1, keepdims=True)
        powers = jnp.exp(shifted)
        total = jnp.sum(powers, axis=-1, keepdims=True)
        hit = targets[:, a : a + 1] == bins
        loss += jnp.log(total) - jnp.sum(jnp.where(hit, shifted, 0.0), axis=-1, keepdims=True)
        logits_back[:, own] = ((powers / total - hit.astype(F32)) * valid_flags).astype(BF)
    place_row = lax.broadcasted_iota(jnp.int32, (8, LANES), 0)
    sums_out[...] = jnp.where(
        place_row == 0, jnp.sum(loss * valid_flags), jnp.where(place_row == 1, jnp.sum(valid_flags), 0.0)
    )

    def put(name, parts):
        height, breadth = SHAPES[name]
        wide = breadth // LANES
        rows = TOP * wide
        for top in range(0, height, TOP):
            j = 0
            for left, right in parts:
                rounded_left = left[:, top : top + TOP]
                for k in range(0, right.shape[1], 2 * LANES):
                    part = mm_tn(rounded_left, right[:, k : k + 2 * LANES])
                    spread[pl.ds(j, TOP, stride=wide), :] = part[:, :LANES]
                    spread[pl.ds(j + 1, TOP, stride=wide), :] = part[:, LANES:]
                    j += 2
            stage[pl.ds(place[name] + top * wide, rows), :] = spread[pl.ds(0, rows), :].astype(BF)

    def give(devices, unit):
        if reduce:
            for device in devices:
                reduce.give_early(stage, device)
            reduce.advance(unit)

    put("action", [(final_rows, logits_back[...])])
    grad_final = mm_nt(logits_back[...], action[...])
    gain_final = jnp.sum(grad_final * final_unit, axis=0, keepdims=True)
    grad_last = norm_back(final_unit, final_inverse, gain[3], grad_final)
    rounded = grad_last.astype(BF)
    put("downward", [(hidden, rounded)])
    give((7, 6), -5)
    grad_upward = (mm_nt(rounded, downward[...]) * slope).astype(BF)
    put("upward", [(second_normed, grad_upward)])
    give((5, 4), -4)
    grad_second = mm_nt(grad_upward, upward[...])
    gain_second = jnp.sum(grad_second * second_unit, axis=0, keepdims=True)
    grad_last = grad_last + norm_back(second_unit, second_inverse, gain[2], grad_second)
    rounded = grad_last.astype(BF)
    put("output", [(merged, rounded)])
    grad_attended = mm_nt(rounded, output[...]).astype(BF)
    give((), -3)
    grad_queries = []
    for h in range(HEADS):
        own = slice(HD * h, HD * (h + 1))
        part = shares[h]
        grad_shares = mm_nt(grad_attended[:, own], values[:, own])
        grad_values[:, own] = mm_tn(part.astype(BF), grad_attended[:, own]).astype(BF)
        grad_scores = part * (grad_shares - jnp.sum(grad_shares * part, axis=-1, keepdims=True))
        grad_scores = grad_scores.astype(BF)
        grad_queries.append(mm(grad_scores, keys[:, own]) * HD ** (-0.5))
        grad_keys[:, own] = (mm_tn(grad_scores, queries[:, own]) * HD ** (-0.5)).astype(BF)
    grad_queries = jnp.concatenate(grad_queries, axis=1).astype(BF)
    put(
        "triple",
        [
            (last_normed, grad_queries),
            (first_normed[...], grad_keys[...]),
            (first_normed[...], grad_values[...]),
        ],
    )
    grad_start[...] = (
        mm_nt(grad_keys[...], triple[:, D : 2 * D])
        + mm_nt(grad_values[...], triple[:, 2 * D :])
        + spread_last(mm_nt(grad_queries, triple[:, :D]))
    )
    grad_first = grad_start[...]
    gain_first = jnp.sum(grad_first * first_unit, axis=0, keepdims=True)
    rows = []
    for part in (jnp.zeros((1, D), F32), gain_first, gain_second, gain_final):
        rows += [part[:, LANES * j : LANES * (j + 1)] for j in range(4)]
    stage[pl.ds(place["gains"], 16), :] = jnp.concatenate(rows, axis=0).astype(BF)
    stage[pl.ds(place["gains"] + 16, LATE_ROWS - place["gains"] - 16), :] = jnp.zeros(
        (LATE_ROWS - place["gains"] - 16, LANES), BF
    )
    give((3, 2), -2)
    grad_start[...] = norm_back(first_unit, first_inverse, gain[1], grad_first) + spread_last(grad_last)
    if reduce:
        reduce.keep_patch(stage)
        reduce.advance(-1)
        reduce.early_left(stage)
    else:
        out = pltpu.make_async_copy(stage, late_out, sems.at[0])
        out.start()
        out.wait()


def layer_scratch(tokens):
    frames = tokens // NT
    return [
        pltpu.VMEM((LATE_ROWS, LANES), BF),
        pltpu.VMEM((TOP * SHAPES["action"][1] // LANES + 32, LANES), F32),
        pltpu.VMEM(SHAPES["triple"], BF),
        pltpu.VMEM(SHAPES["output"], BF),
        pltpu.VMEM(SHAPES["upward"], BF),
        pltpu.VMEM(SHAPES["downward"], BF),
        pltpu.VMEM(SHAPES["action"], BF),
        pltpu.VMEM((tokens, D), BF),
        pltpu.VMEM((tokens, D), BF),
        pltpu.VMEM((tokens, D), BF),
        pltpu.VMEM((tokens, D), BF),
        pltpu.VMEM((HEADS, frames, tokens), F32),
        pltpu.VMEM((tokens, D), BF),
        pltpu.VMEM((frames, ACT * BINS), BF),
        pltpu.VMEM((8, 2, 16, LANES), BF),
        pltpu.SemaphoreType.DMA((32,)),
    ]


BLOCK = 256
BLOCKS = CIN // BLOCK
EARLY_ITEM = 1152
EARLY = WINDOW // EARLY_ITEM
FIRST_ITEM = 1008
ITEM = 576
LAST_ITEM = 288
ADD_ROWS = 144
SLAB = WINDOW + LAST_ITEM
FILM_ITEMS = 2 * BLOCKS
CONV_ITEMS = 8
LATE_ID = EARLY
LAST_ID = LATE_ID + FILM_ITEMS
IDS = LAST_ID + 1
EARLY_LAG, EARLY_LINE_LAG, LAG, LINE_LAG = 3, 3, 2, 2
EARLY_PACE = 2
EARLY_UNITS = ((99, 0, -3, -3), (99, -2, -3, -1))
FIRST_SCALE, FIRST_OFFSET, FIRST_CONV, LAST_UNIT = 8, 7, 9, 18
COMPUTE_UNITS = 6 + 2 * BLOCKS
UNITS = max(LAST_UNIT + 3 * LAG + 4 * LINE_LAG, 10 + 3 * EARLY_LAG + 4 * EARLY_LINE_LAG) + 1
CONV_BEFORE = (0, 0, 1, 3, 4, 6, 8)
OWN_CONV = 1280
TAIL_CONV = 1152
FILM_FIRST = (0, 272)
FILM_HEIGHT = (288, 240)
SQUARES = 2
RING_PLACE = (0, 0, 1, 3, 3, 1, 2, 2)


def added(parts):
    total = parts[0].astype(F32)
    for part in parts[1:]:
        total = total + part.astype(F32)
    return total


class Reduce:
    def __init__(self, shard_rows, patch, own, sibling, ring_in, z_in, sems, z_sems):
        self.ring = ring = Ring()
        self.shard_rows, self.patch = shard_rows, patch
        self.own, self.sibling, self.ring_in, self.z_in = own, sibling, ring_in, z_in
        self.sems, self.z_sems = sems, z_sems
        self.line = ring.replica + ring.core * (3 - 2 * ring.replica)

    def greet(self):
        barrier = pltpu.get_barrier_semaphore()
        devices = [{"fsdp": other} for other in self.ring.others]
        devices += [{"dp": (self.ring.replica + hops) % 4} for hops in (1, 2, 3)]
        for device in devices:
            pl.semaphore_signal(barrier, inc=1, device_id=device, device_id_type=MESH)
        pl.semaphore_wait(barrier, len(devices))

    def along(self, line):
        return {"dp": line + self.ring.core * (3 - 2 * line)}

    def stage_of(self, q):
        return (self.ring.place + 7 - q) % 4

    def rows(self, row, count):
        return pl.ds(pl.multiple_of(row, 16), count)

    def remote(self, source, target, send_sem, recv_sem, device):
        return pltpu.make_async_remote_copy(
            src_ref=source,
            dst_ref=target,
            send_sem=send_sem,
            recv_sem=recv_sem,
            device_id=device,
            device_id_type=MESH,
        )

    def to_sibling(self, source, q, ident, row, count):
        return self.remote(
            source,
            self.sibling.at[q, self.rows(row, count)],
            self.sems.at[0, q, ident],
            self.sems.at[1, q, ident],
            {"fsdp": self.ring.sibling},
        )

    def to_next(self, q, ident, row, count):
        rows = self.rows(row, count)
        return self.remote(
            self.own.at[q, rows],
            self.ring_in.at[jnp.minimum(self.stage_of(q), 2), rows],
            self.sems.at[2, q, ident],
            self.sems.at[3, q, ident],
            {"fsdp": self.ring.after},
        )

    def to_line(self, which, line, slot, ident, row, count, forward=False):
        rows = self.rows(row, count)
        return self.remote(
            self.z_in.at[1, rows] if forward else self.own.at[self.ring.place, rows],
            self.z_in.at[slot, rows],
            self.z_sems.at[which, ident],
            self.z_sems.at[2 + slot, ident],
            self.along(line),
        )

    def early_items(self, device):
        if device == 2:
            top = WINDOW - 2 * FIRST_ITEM
            items = [(i, top + FIRST_ITEM * i, FIRST_ITEM) for i in range(2)]
        else:
            items = [(i, EARLY_ITEM * i, EARLY_ITEM) for i in range(EARLY)]
        return items, self.shard_rows * device // 16 * 16 - HEAD_PART

    def give_early(self, stage, device):
        q = RING_PLACE[device]
        items, first = self.early_items(device)

        @pl.when(self.ring.core == device % 2)
        def _():
            top, count = items[0][1], sum(item[2] for item in items)
            self.own[q, pl.ds(top, count), :] = stage[pl.ds(first + top, count), :]

        @pl.when(self.ring.core != device % 2)
        def _():
            for ident, row, count in items:
                if device < 7 or ident < EARLY - 1:
                    self.to_sibling(stage.at[pl.ds(first + row, count)], q, ident, row, count).start()

    def keep_patch(self, stage):
        last = self.shard_rows * 7 // 16 * 16 - HEAD_PART + (EARLY - 1) * EARLY_ITEM
        self.patch[...] = stage[pl.ds(last, EARLY_ITEM), :]

    def early_left(self, stage):
        for device in range(2, 8):
            q = RING_PLACE[device]
            items, first = self.early_items(device)

            @pl.when(self.ring.core != device % 2)
            def _():
                for ident, row, count in items:
                    if device < 7 or ident < EARLY - 1:
                        self.to_sibling(stage.at[pl.ds(first + row, count)], q, ident, row, count).wait_send()

    def patch_gains(self, gain_rows):
        place = START["gains"] - (self.shard_rows * 7 // 16 * 16 + (EARLY - 1) * EARLY_ITEM)
        here = pl.ds(place, 16)
        self.patch[here, :] = (self.patch[here, :].astype(F32) + gain_rows).astype(BF)

        @pl.when(self.ring.core == 0)
        def _():
            self.to_sibling(self.patch, 2, EARLY - 1, (EARLY - 1) * EARLY_ITEM, EARLY_ITEM).start()

        @pl.when(self.ring.core == 1)
        def _():
            self.own[2, pl.ds((EARLY - 1) * EARLY_ITEM, EARLY_ITEM), :] = self.patch[...]

    def give_film(self, film, conv, step, half):
        item = 2 * step + half
        row = ITEM * item
        tiles = [half * (CIN // LANES) + 2 * step + a for a in range(2)]
        conv_rows = self.rows(96 * item, 96)
        for core in range(2):
            first, height = FILM_FIRST[core], FILM_HEIGHT[core]

            @pl.when(self.ring.core == core)
            def _():
                for a in range(2):
                    self.own[0, self.rows(row + height * a, height), :] = film[tiles[a], first : first + height, :]
                if core == 1:
                    self.own[0, self.rows(row + 2 * height, 96), :] = conv[conv_rows, :]

            @pl.when(self.ring.core != core)
            def _():
                ident = LATE_ID + item
                for a in range(2):
                    self.to_sibling(
                        film.at[tiles[a], pl.ds(first, height)], 0, ident, row + height * a, height
                    ).start()
                if core == 1:
                    self.to_sibling(conv.at[conv_rows], 0, ident, row + 2 * height, 96).start()

    def give_conv(self, conv, step):
        ring = self.ring

        @pl.loop(ring.pick(CONV_BEFORE, step), ring.pick(CONV_BEFORE, step + 1))
        def _(i):
            source = self.rows(OWN_CONV + ITEM * i, ITEM)

            @pl.when(ring.core == 0)
            def _():
                self.own[1, self.rows(ITEM * i, ITEM), :] = conv[source, :]

            @pl.when(ring.core == 1)
            def _():
                self.to_sibling(conv.at[source], 1, LATE_ID + i, ITEM * i, ITEM).start()

        @pl.when(step == BLOCKS - 1)
        def _():
            mine = pl.ds(OWN_CONV + CONV_ITEMS * ITEM, LAST_ITEM)
            tail = pl.ds(TAIL_CONV, LAST_ITEM)

            @pl.when(ring.core == 0)
            def _():
                self.own[1, pl.ds(CONV_ITEMS * ITEM, LAST_ITEM), :] = conv[mine, :]
                self.to_sibling(conv.at[tail], 0, LAST_ID, WINDOW, LAST_ITEM).start()

            @pl.when(ring.core == 1)
            def _():
                self.own[0, pl.ds(WINDOW, LAST_ITEM), :] = conv[tail, :]
                self.to_sibling(conv.at[mine], 1, LAST_ID, CONV_ITEMS * ITEM, LAST_ITEM).start()

    def add_up(self, q, row, count, others):
        @pl.loop(0, count // ADD_ROWS)
        def _(block):
            rows = self.rows(row + block * ADD_ROWS, ADD_ROWS)
            parts = [self.own[q, rows, :]] + [ref[which, rows, :] for ref, which in others]
            self.own[q, rows, :] = added(parts).astype(BF)

    def hop_ring(self, q, ident, row, count):
        stage = self.stage_of(q)
        self.to_sibling(self.own.at[q, self.rows(row, count)], q, ident, row, count).wait_recv()

        @pl.when(stage == 0)
        def _():
            self.add_up(q, row, count, [(self.sibling, q)])

        @pl.when(stage > 0)
        def _():
            self.to_next(q, ident, row, count).wait_recv()
            self.add_up(q, row, count, [(self.sibling, q), (self.ring_in, stage - 1)])

        @pl.when(stage < 3)
        def _():
            self.to_next(q, ident, row, count).start()

        @pl.when((stage == 3) & (self.line == 0))
        def _():
            self.to_line(0, 1, 0, ident, row, count).start()

        @pl.when((stage == 3) & (self.line == 3))
        def _():
            self.to_line(0, 2, 0, ident, row, count).start()

    def hop_line(self, ident, row, count):
        place = self.ring.place

        @pl.when(self.line == 2)
        def _():
            self.to_line(0, 1, 0, ident, row, count).wait_recv()
            self.add_up(place, row, count, [(self.z_in, 0)])
            self.to_line(0, 1, 1, ident, row, count).start()

        @pl.when(self.line == 1)
        def _():
            self.to_line(0, 1, 0, ident, row, count).wait_recv()
            self.to_line(0, 1, 1, ident, row, count).wait_recv()
            self.add_up(place, row, count, [(self.z_in, 0), (self.z_in, 1)])
            self.to_line(0, 0, 0, ident, row, count).start()
            self.to_line(1, 2, 1, ident, row, count).start()

    def hop_back(self, ident, row, count):
        @pl.when(self.line == 2)
        def _():
            self.to_line(0, 1, 1, ident, row, count).wait_recv()
            self.to_line(1, 3, 0, ident, row, count, forward=True).start()

        @pl.when(self.line != 2)
        def _():
            self.to_line(0, 1, 0, ident, row, count).wait_recv()

    def early(self, q, unit):
        core = self.ring.core
        begin = jnp.where(core == 0, self.ring.pick(EARLY_UNITS[0], q), self.ring.pick(EARLY_UNITS[1], q))
        at = unit - begin
        there = (q >= 2 - core) & (at >= 0) & (at % EARLY_PACE == 0) & (at < EARLY_PACE * EARLY)
        ident = at // EARLY_PACE
        return there, ident, EARLY_ITEM * ident

    def streams(self):
        core = self.ring.core

        def first(unit):
            at = unit - EARLY_UNITS[0][1]
            there = (at >= 0) & (at % EARLY_PACE == 0) & (at < 2 * EARLY_PACE)
            return there, at // EARLY_PACE, WINDOW - 2 * FIRST_ITEM + FIRST_ITEM * (at // EARLY_PACE)

        def scale(unit):
            at = unit - FIRST_SCALE
            return (at >= 0) & (at < FILM_ITEMS) & (at % 2 == 0), LATE_ID + at, ITEM * at

        def offset(unit):
            item = 2 * (unit - FIRST_OFFSET) + 1
            return (item >= 0) & (item < FILM_ITEMS), LATE_ID + item, ITEM * item

        def conv(unit):
            at = unit - FIRST_CONV
            item = at - jnp.where(at > 0, 1, 0) - jnp.where(at > 5, 1, 0)
            there = (at >= 0) & (at != 1) & (at != 5) & (item < CONV_ITEMS)
            return there, LATE_ID + item, ITEM * item

        def last(unit):
            return unit == LAST_UNIT, LAST_ID, jnp.where(core == 0, CONV_ITEMS * ITEM, WINDOW)

        return [
            (1, core == 0, FIRST_ITEM, first, EARLY_LAG, EARLY_LINE_LAG),
            (0, core >= 0, ITEM, scale, LAG, LINE_LAG),
            (0, core >= 0, ITEM, offset, LAG, LINE_LAG),
            (1, core == 0, ITEM, conv, LAG, LINE_LAG),
            (1 - core, core >= 0, LAST_ITEM, last, LAG, LINE_LAG),
        ]

    def advance(self, unit):
        ring, line = self.ring, self.line
        streams = self.streams()

        @pl.loop(2 - ring.core, 4)
        def _(q):
            there, ident, row = self.early(q, unit - EARLY_LAG * self.stage_of(q))

            @pl.when(there)
            def _():
                self.hop_ring(q, ident, row, EARLY_ITEM)

        for q, has, count, item, lag, _ in streams:
            there, ident, row = item(unit - lag * self.stage_of(q))

            @pl.when(has & there)
            def _():
                self.hop_ring(q, ident, row, count)

        owners = [(ring.place >= 0, EARLY_ITEM, functools.partial(self.early, ring.place), EARLY_LAG, EARLY_LINE_LAG)]
        owners += [(has & (ring.place == q), count, item, *lags) for q, has, count, item, *lags in streams]
        for owner, count, item, lag, line_lag in owners:
            there, ident, row = item(unit - 3 * lag - line_lag * jnp.where(line == 2, 1, 2))

            @pl.when(owner & there & ((line == 1) | (line == 2)))
            def _():
                self.hop_line(ident, row, count)

            there, ident, row = item(unit - 3 * lag - line_lag * jnp.where(line == 3, 4, 3))

            @pl.when(owner & there & (line != 1))
            def _():
                self.hop_back(ident, row, count)

    def finish(self):
        ring, line = self.ring, self.line

        def sent(q, ident, row, count, owner):
            @pl.when(self.stage_of(q) < 3)
            def _():
                self.to_next(q, ident, row, count).wait_send()

            @pl.when(owner)
            def _():
                self.to_line(0, 1, 0, ident, row, count).wait_send()

                @pl.when((line == 1) | (line == 2))
                def _():
                    self.to_line(1, 1, 0, ident, row, count).wait_send()

        def given(q, ident, row, count):
            self.to_sibling(self.own.at[q, self.rows(row, count)], q, ident, row, count).wait_send()

        @pl.loop(0, EARLY)
        def _(i):
            @pl.loop(2 - ring.core, 4)
            def _(q):
                sent(q, i, EARLY_ITEM * i, EARLY_ITEM, q == ring.place)

        @pl.loop(0, FILM_ITEMS)
        def _(i):
            sent(0, LATE_ID + i, ITEM * i, ITEM, ring.place == 0)
            given(0, LATE_ID + i, ITEM * i, ITEM)

        @pl.when(ring.core == 0)
        def _():
            for i in range(2):
                sent(1, i, WINDOW - FIRST_ITEM * (2 - i), FIRST_ITEM, ring.place == 1)

            @pl.loop(0, CONV_ITEMS)
            def _(i):
                sent(1, LATE_ID + i, ITEM * i, ITEM, ring.place == 1)

            sent(1, LAST_ID, CONV_ITEMS * ITEM, LAST_ITEM, ring.place == 1)
            given(0, LAST_ID, WINDOW, LAST_ITEM)
            given(2, EARLY - 1, (EARLY - 1) * EARLY_ITEM, EARLY_ITEM)

        @pl.when(ring.core == 1)
        def _():
            @pl.loop(0, CONV_ITEMS)
            def _(i):
                given(1, LATE_ID + i, ITEM * i, ITEM)

            given(1, LAST_ID, CONV_ITEMS * ITEM, LAST_ITEM)
            sent(0, LAST_ID, WINDOW, LAST_ITEM, ring.place == 0)

    def assemble(self, spread):
        ring, line = self.ring, self.line
        place = ring.place

        whole = self.sibling

        @pl.when((line == 0) | (line == 3))
        def _():
            whole[place] = self.z_in[0]

        @pl.when(line == 1)
        def _():
            whole[place] = self.own[place]

        @pl.when(line == 2)
        def _():
            whole[place] = self.z_in[1]

        wide = 2 * CIN // LANES
        for core in range(2):
            height = FILM_HEIGHT[core]

            @pl.when(ring.me == core)
            def _():
                for step in range(BLOCKS):
                    for half in range(2):
                        row = ITEM * (2 * step + half)
                        for a in range(2):
                            tile = half * (CIN // LANES) + 2 * step + a
                            spread[pl.ds(tile, height, stride=wide), :] = whole[
                                0, row + height * a : row + height * (a + 1), :
                            ].astype(F32)
                        if core == 1:
                            spread[pl.ds(height * wide + 96 * (2 * step + half), 96), :] = whole[
                                0, row + 2 * height : row + 2 * height + 96, :
                            ].astype(F32)
                if core == 1:
                    spread[pl.ds(height * wide + TAIL_CONV, LAST_ITEM), :] = whole[0, WINDOW:SLAB, :].astype(F32)

        @pl.when(ring.me > 1)
        def _():
            spread[pl.ds(0, WINDOW), :] = whole[place, 0:WINDOW, :].astype(F32)

    def shard_offset(self):
        me = self.ring.me
        second = self.shard_rows - FILM_FIRST[1] * (2 * CIN // LANES)
        return jnp.where(me == 1, second, self.shard_rows * me % 16)


class Sums:
    def __init__(self, plane, line, plane_sems, line_sems):
        self.ring = Ring()
        self.plane, self.line, self.plane_sems, self.line_sems = plane, line, plane_sems, line_sems

    def plane_copy(self, which, index):
        me = self.ring.me
        return pltpu.make_async_remote_copy(
            src_ref=self.plane.at[which, me],
            dst_ref=self.plane.at[which, me],
            send_sem=self.plane_sems.at[0, which, index],
            recv_sem=self.plane_sems.at[1, which, index],
            device_id={"fsdp": self.ring.others[index]},
            device_id_type=MESH,
        )

    def line_copy(self, hops):
        own = self.ring.replica
        return pltpu.make_async_remote_copy(
            src_ref=self.line.at[own],
            dst_ref=self.line.at[own],
            send_sem=self.line_sems.at[0, hops - 1],
            recv_sem=self.line_sems.at[1, hops - 1],
            device_id={"dp": (own + hops) % 4},
            device_id_type=MESH,
        )

    def give(self, which, value):
        self.plane[which, self.ring.me] = value
        for index in range(self.ring.shards - 1):
            self.plane_copy(which, index).start()

    def take(self, which):
        for index in range(self.ring.shards - 1):
            self.plane_copy(which, index).wait()
        return jnp.sum(self.plane[which], axis=0)

    def give_line(self, value):
        self.line[self.ring.replica] = value
        for hops in (1, 2, 3):
            self.line_copy(hops).start()

    def take_line(self):
        for hops in (1, 2, 3):
            self.line_copy(hops).wait()
        return jnp.sum(self.line[...], axis=0)


def back_kernel(
    windows,
    start,
    flat,
    gains,
    episode_row,
    episode_last,
    valid,
    targets,
    images,
    embedding,
    shifts,
    conv,
    learner,
    grid,
    *rest,
):
    reduces = windows.shards > 1
    if reduces:
        gradient, small_out, grad_start, sums_in, patch, own, sibling, ring_in, z_in, sems, z_sems, *rest = rest
        reduce = Reduce(windows.shard_rows, patch, own, sibling, ring_in, z_in, sems, z_sems)
        sums = Sums(*rest)
        late_out = None
        reduce.greet()
    else:
        film_out, conv_out, late_out, sums_in, gain_out, grad_start = rest
        reduce = None

    refs = (start, flat, gains, episode_row, episode_last, valid, targets, grad_start, sums_in)
    pl.run_scoped(functools.partial(layer_part, windows, refs, reduce, late_out), *layer_scratch(start.shape[0]))
    if reduces:
        sums.give(0, sums_in[...])

    def section_part(
        grad_grid, grad_sum, learner_sum, gain_sum, modulated, grad_scale, conv_sum, conv_spread, film, conv_flat, cells, sems
    ):
        frames = embedding.shape[0]
        groups = frames // GROUP
        wide = D // LANES
        learner_sum[...] = jnp.zeros_like(learner_sum)
        gain_sum[...] = jnp.zeros_like(gain_sum)

        def block_copy(step, slot):
            return pltpu.make_async_copy(
                images.at[:, :, pl.ds(pl.multiple_of(step * BLOCK, BLOCK), BLOCK)], cells.at[slot], sems.at[2 + slot]
            )

        def first_part(fetched):
            def fetch(g, slot):
                return pltpu.make_async_copy(
                    grid.at[pl.ds(pl.multiple_of(g * CELLS, 16), CELLS)], fetched.at[slot], sems.at[slot]
                )

            fetch(0, 0).start()
            block_copy(0, 0).start()

            @pl.loop(0, groups)
            def _(g):
                slot = g % 2
                fetch(g, slot).wait()

                @pl.when(g + 1 < groups)
                def _():
                    fetch(g + 1, 1 - slot).start()

                rows = pl.ds(pl.multiple_of(g * CELLS, 16), CELLS)
                unit, inverse = norm_rows(fetched[slot].astype(F32))
                normed = (unit * gains[0:1, :]).astype(BF)
                maps = jax.nn.sigmoid(mm(normed, learner[...]))
                mask = own_frame(CELLS)
                tokens = grad_start[pl.ds(pl.multiple_of(g * SLOTS, SLOTS), SLOTS), :]
                tokens = (tokens * (1.0 / POS)).astype(BF)
                grad_maps = mm_nt(normed, tokens)
                grad_logit = jnp.where(mask, grad_maps * maps * (1.0 - maps), 0.0).astype(BF)
                maps = jnp.where(mask, maps, 0.0).astype(BF)
                grad_normed = mm(maps, tokens) + mm_nt(grad_logit, learner[...])
                learner_sum[...] += mm_tn(normed, grad_logit)
                gain_sum[...] += jnp.sum(grad_normed * unit, axis=0, keepdims=True)
                back = norm_back(unit, inverse, gains[0:1, :], grad_normed).astype(BF)
                grad_grid[rows, :] = back
                grad_sum[pl.ds(pl.multiple_of(g * GROUP, GROUP), GROUP), :] = jnp.sum(
                    back.astype(F32).reshape(POS, GROUP, D), axis=0
                )
                if reduces:
                    reduce.advance(g)

        pl.run_scoped(first_part, pltpu.VMEM((2, CELLS, D), BF))

        total = learner_sum[...]
        high = total.astype(BF)
        token = same_token()
        spread_learner = mm(high, token) + mm((total - high.astype(F32)).astype(BF), token)
        spread_learner = jnp.where(learner_mask(), spread_learner, 0.0)
        conv_flat[pl.ds(CIN * wide, D * NT // LANES), :] = jnp.sum(
            spread_learner.reshape(D * NT // LANES, GROUP, LANES), axis=1
        ).astype(BF)
        if reduces:
            rows = [gain_sum[:, LANES * j : LANES * (j + 1)] for j in range(wide)]
            reduce.patch_gains(jnp.concatenate(rows + [jnp.zeros((16 - wide, LANES), F32)], axis=0))
            sums.give_line(sums.take(0))
        else:
            gain_out[...] = gain_sum[...]

        def put_film(step, half, grad):
            part = mm_tn(embedding[...], grad.astype(BF)).astype(BF)
            for i in range(BLOCK // LANES):
                film[half * (CIN // LANES) + step * (BLOCK // LANES) + i] = part[:, LANES * i : LANES * (i + 1)]

        total = grad_sum[...]
        high = total.astype(BF)
        low = (total - high.astype(F32)).astype(BF)
        for step in range(BLOCKS):
            weights = conv[BLOCK * step : BLOCK * (step + 1), :]
            put_film(step, 1, mm_nt(high, weights) + mm_nt(low, weights))

        @pl.loop(0, BLOCKS)
        def _(step):
            slot = step % 2
            block_copy(step, slot).wait()

            @pl.when(step + 1 < BLOCKS)
            def _():
                block_copy(step + 1, 1 - slot).start()

            channels = pl.ds(pl.multiple_of(step * BLOCK, BLOCK), BLOCK)
            weights = conv[channels, :]

            conv_sum[...] = jnp.zeros_like(conv_sum)
            for g in range(groups):
                rows = pl.ds(g * CELLS, CELLS)
                here = pl.ds(g * GROUP, GROUP)
                scale = 1.0 + shifts[0, here, channels]
                offset = shifts[1, here, channels]
                block = cells[slot, :, here, :].astype(F32)
                modulated[...] = (block * scale[None] + offset[None]).astype(BF).reshape(CELLS, BLOCK)
                conv_sum[...] += mm_tn(modulated[...], grad_grid[rows, :])
            for j in range(wide):
                conv_spread[pl.ds(j, BLOCK, stride=wide), :] = conv_sum[:, LANES * j : LANES * (j + 1)]
            conv_flat[pl.ds(pl.multiple_of(step * BLOCK * wide, 16), BLOCK * wide), :] = conv_spread[
                pl.ds(0, BLOCK * wide), :
            ].astype(BF)
            if reduces:
                reduce.give_conv(conv_flat, step)

                @pl.when(step == 0)
                def _():
                    for block in range(BLOCKS - 1):
                        reduce.give_film(film, conv_flat, block, 1)

                @pl.when(step == 1)
                def _():
                    reduce.give_film(film, conv_flat, BLOCKS - 1, 1)

                reduce.advance(6 + 2 * step)

            for g in range(groups):
                here = pl.ds(g * GROUP, GROUP)
                back = mm_nt(grad_grid[pl.ds(g * CELLS, CELLS), :], weights).reshape(POS, GROUP, BLOCK)
                grad_scale[here, :] = jnp.sum(back * cells[slot, :, here, :].astype(F32), axis=0)
            put_film(step, 0, grad_scale[...])
            if reduces:
                reduce.give_film(film, conv_flat, step, 0)


                reduce.advance(7 + 2 * step)

        if not reduces:
            copies = [
                pltpu.make_async_copy(film, film_out, sems.at[0]),
                pltpu.make_async_copy(conv_flat, conv_out, sems.at[1]),
            ]
            for copy in copies:
                copy.start()
            for copy in copies:
                copy.wait()
            return

        @pl.loop(COMPUTE_UNITS, UNITS)
        def _(unit):
            reduce.advance(unit)

        reduce.finish()

    frames = embedding.shape[0]
    pl.run_scoped(
        section_part,
        pltpu.VMEM((frames * POS, D), BF),
        pltpu.VMEM((frames, D), F32),
        pltpu.VMEM((D, SLOTS), F32),
        pltpu.VMEM((1, D), F32),
        pltpu.VMEM((CELLS, BLOCK), BF),
        pltpu.VMEM((frames, BLOCK), F32),
        pltpu.VMEM((BLOCK, D), F32),
        pltpu.VMEM((BLOCK * D // LANES + 8, LANES), F32),
        pltpu.VMEM((2 * CIN // LANES, E, LANES), BF),
        pltpu.VMEM(((CIN * D + D * NT) // LANES, LANES), BF),
        pltpu.VMEM((2, POS, frames, BLOCK), BF),
        pltpu.SemaphoreType.DMA((4,)),
    )
    if not reduces:
        return

    def last_part(spread, sems):
        count = gradient.shape[0]
        reduce.assemble(spread)
        offset = reduce.shard_offset()

        def move(block, squares):
            part = spread[pl.ds(offset + block * LANES, LANES), :]
            spread[pl.ds(pl.multiple_of(block * LANES, LANES), LANES), :] = part
            return squares + jnp.sum((part * part).reshape(LANES // 8, 8, LANES), axis=0)

        blocks = windows.shard_rows // LANES
        squares = lax.fori_loop(0, blocks, move, jnp.zeros((8, LANES), F32))
        for row in range(blocks * LANES, count, 8):
            part = spread[pl.ds(offset + row, 8), :]
            spread[pl.ds(row, 8), :] = part
            kept = lax.broadcasted_iota(jnp.int32, (8, LANES), 0) + row < windows.shard_rows
            squares = squares + jnp.where(kept, part * part, 0.0)
        sums.give(1, squares)
        out = pltpu.make_async_copy(spread.at[pl.ds(0, count)], gradient, sems.at[0])
        out.start()
        total = sums.take_line()
        total_squares = jnp.sum(sums.take(1))
        place_row = lax.broadcasted_iota(jnp.int32, (8, LANES), 0)
        small_out[...] = jnp.where(place_row == SQUARES, total_squares, total)
        out.wait()

    pl.run_scoped(last_part, pltpu.VMEM((SLAB + 32, LANES), F32), pltpu.SemaphoreType.DMA((1,)))


def back(windows, start, flat, gains, episode, valid, targets, images, embedding, shifts, conv, learner, grid):
    tokens = start.shape[0]
    frames = tokens // NT
    reduces = windows.shards > 1
    vmem = pl.BlockSpec(memory_space=pltpu.VMEM)
    anywhere = pl.BlockSpec(memory_space=pl.ANY)
    shard_rows = -(-windows.shard_rows // 8) * 8
    slab = lambda count: pltpu.VMEM((count, SLAB, LANES), BF)
    grad_start = pltpu.VMEM((tokens, D), F32)
    if reduces:
        scratch = [
            grad_start,
            pltpu.VMEM((8, LANES), F32),
            pltpu.VMEM((EARLY_ITEM, LANES), BF),
            slab(4),
            slab(4),
            slab(3),
            slab(2),
            pltpu.SemaphoreType.DMA((4, 4, IDS)),
            pltpu.SemaphoreType.DMA((4, IDS)),
            pltpu.VMEM((2, 8, 8, LANES), F32),
            pltpu.VMEM((4, 8, LANES), F32),
            pltpu.SemaphoreType.DMA((2, 2, 7)),
            pltpu.SemaphoreType.DMA((2, 3)),
        ]
        outs = [jax.ShapeDtypeStruct((shard_rows, LANES), F32), jax.ShapeDtypeStruct((8, LANES), F32)]
        out_specs = [anywhere, vmem]
    else:
        scratch = [grad_start]
        outs = [
            jax.ShapeDtypeStruct((2 * CIN // LANES, E, LANES), BF),
            jax.ShapeDtypeStruct(((CIN * D + D * NT) // LANES, LANES), BF),
            jax.ShapeDtypeStruct((LATE_ROWS, LANES), BF),
            jax.ShapeDtypeStruct((8, LANES), F32),
            jax.ShapeDtypeStruct((1, D), F32),
        ]
        out_specs = [anywhere] * 3 + [vmem] * 2
    return pl.pallas_call(
        functools.partial(back_kernel, windows),
        in_specs=[vmem, anywhere] + [vmem] * 5 + [anywhere] + [vmem] * 4 + [anywhere],
        out_specs=out_specs,
        out_shape=outs,
        scratch_shapes=scratch,
        compiler_params=pltpu.CompilerParams(
            vmem_limit_bytes=63 * MIB,
            **(dict(collective_id=1, has_side_effects=True) if reduces else {}),
        ),
        cost_estimate=pl.CostEstimate(
            flops=4 * frames * POS * CIN * D, bytes_accessed=frames * POS * CIN * 2, transcendentals=0
        ),
    )(
        start,
        flat,
        gains,
        episode.reshape(1, tokens),
        episode.reshape(frames, NT)[:, NT - 1 :],
        valid.reshape(frames, 1),
        targets,
        images,
        embedding,
        shifts,
        conv,
        learner,
        grid,
    )


def on_device(
    images, embedding, episode, valid_steps, targets, master, first_moment, second_moment, average
):
    images = images.transpose(1, 0, 2)
    replicas, shards = lax.axis_size("dp"), lax.axis_size("fsdp")
    if fits_ring(replicas, shards, master.shape[0]):
        windows = Windows(shards, master.shape[0] // LANES, WINDOW)
        flat = master.reshape(-1, LANES)
    else:
        whole_flat = lax.all_gather(master.astype(BF), "fsdp", axis=0, tiled=True)
        flat = jnp.pad(whole_flat.reshape(ROWS, LANES), ((0, FLAT_ROWS - ROWS), (0, 0)))[None]
        windows = Windows(1, ROWS, FLAT_ROWS)

    grid, start, shifts, conv, learner, gains, *gathered = section(windows, images, embedding, flat)
    if gathered:
        (flat,) = gathered
    results = back(
        windows, start, flat, gains, episode, valid_steps, targets, images, embedding, shifts, conv, learner, grid
    )
    if gathered:
        shard, small = results
        loss_sum, step_count, squares = small[0, 0], small[1, 0], small[SQUARES, 0]
        inverse_count = 1.0 / step_count
        grad_shard = shard.reshape(-1)[: master.shape[0]] * inverse_count
        squares = squares * inverse_count * inverse_count
    else:
        film, conv_flat, late, sums, gain_grid = results
        at = START["gains"] - HEAD_PART
        late = late[: ROWS - HEAD_PART].at[at : at + 4].set(gain_grid.reshape(4, LANES).astype(BF))
        gradient = jnp.concatenate([film.transpose(1, 0, 2).reshape(-1, LANES), conv_flat, late])
        loss_sum, step_count = lax.psum((sums[0, 0], sums[1, 0]), ("dp", "fsdp"))
        partial_shard = lax.psum_scatter(gradient.reshape(-1), "fsdp", scatter_dimension=0, tiled=True)
        grad_shard = lax.psum(partial_shard.astype(F32), "dp") / step_count
        squares = lax.psum(jnp.sum(grad_shard * grad_shard), "fsdp")
    grad_norm = jnp.sqrt(squares)
    clipped = grad_shard * (CLIP_NORM / jnp.maximum(grad_norm, CLIP_NORM))
    new_first = MOMENT_DECAY * first_moment + (1.0 - MOMENT_DECAY) * clipped
    new_second = MOMENT_DECAY * second_moment + (1.0 - MOMENT_DECAY) * clipped * clipped
    correction = 1.0 - MOMENT_DECAY**STEP
    new_master = master - LEARN_RATE * (
        new_first / correction / (jnp.sqrt(new_second / correction) + ADAM_EPSILON)
        + WEIGHT_DECAY * master
    )
    average_decay = min(AVERAGE_DECAY, (1.0 + STEP) / (10.0 + STEP))
    new_average = average_decay * average + (1.0 - average_decay) * new_master
    return (
        new_master,
        new_first,
        new_second,
        new_average,
        new_master.astype(BF),
        grad_norm,
        loss_sum,
        step_count,
    )


def solution(mesh):
    in_specs = (
        P(("dp", "fsdp"), None, None),
        P(("dp", "fsdp"), None),
        P(("dp", "fsdp")),
        P(("dp", "fsdp")),
        P(("dp", "fsdp"), None),
        P("fsdp"),
        P("fsdp"),
        P("fsdp"),
        P("fsdp"),
    )
    out_specs = (P("fsdp"), P("fsdp"), P("fsdp"), P("fsdp"), P("fsdp"), P(), P(), P())
    return jax.shard_map(
        on_device, mesh=mesh, in_specs=in_specs, out_specs=out_specs, check_vma=False
    )
```

```python
import functools

import jax
import jax.numpy as jnp
from jax import lax
from jax.experimental import pallas as pl
from jax.experimental.pallas import tpu as pltpu
from jax.sharding import PartitionSpec as P

D = 512
HEADS = 8
HD = 64
FF = 2048
E = 512
CIN = 1536
POS = 81
NT = 8
ACT = 11
BINS = 256
STEP = 10
LANES = 128
GROUP = 16
CELLS = POS * GROUP
SLOTS = GROUP * NT

MOMENT_DECAY = 0.5
LEARN_RATE = 0.02
WEIGHT_DECAY = 0.1
CLIP_NORM = 1.0
ADAM_EPSILON = 1e-08
AVERAGE_DECAY = 0.999
BF = jnp.bfloat16
F32 = jnp.float32
MIB = 2**20

SHAPES = {
    "film": (E, 2 * CIN),
    "conv": (CIN, D),
    "learner": (D, NT),
    "triple": (D, 3 * D),
    "output": (D, D),
    "upward": (D, FF),
    "downward": (FF, D),
    "action": (D, ACT * BINS),
    "gains": (4, D),
}


def row_starts():
    starts, row = {}, 0
    for name, (height, breadth) in SHAPES.items():
        starts[name] = row
        row += height * breadth // LANES
    return starts, row


START, ROWS = row_starts()
FLAT_ROWS = ROWS + 16
HEAD_PART = START["triple"]
LATE_ROWS = ROWS - HEAD_PART + 112


def mm(a, b):
    return jnp.dot(a, b, preferred_element_type=F32)


def mm_nt(a, b):
    return lax.dot_general(a, b, (((1,), (1,)), ((), ())), preferred_element_type=F32)


def mm_tn(a, b):
    return lax.dot_general(a, b, (((0,), (0,)), ((), ())), preferred_element_type=F32)


class Windows:
    def __init__(self, shards, shard_rows, size):
        self.shards, self.shard_rows, self.size = shards, shard_rows, size
        self.first = [shard_rows * k // 16 * 16 for k in range(shards)]

    def pieces(self, start, stop):
        inner, shared = [], []
        for k in range(self.shards):
            low, high = self.shard_rows * k, self.shard_rows * (k + 1)
            if k == self.shards - 1:
                high = (high + 15) // 16 * 16
            a, b = max(start, -(-low // 16) * 16), min(stop, high // 16 * 16)
            if a < b:
                inner.append((k, a - self.first[k], a, b - a))
            edge = low // 16 * 16
            if low % 16 and start <= edge < stop:
                shared.append((k - 1, edge - self.first[k - 1], k, edge - self.first[k], edge))
        return inner, shared

    def load(self, flat_ref, stage, edges, sem, parts):
        count, fixed, waits = 0, 0, []
        for start, stop, place in parts:
            copies, fixes = [], []
            inner, shared = self.pieces(start, stop)
            for k, offset, row, rows in inner:
                copies.append((flat_ref.at[k, pl.ds(offset, rows)], stage.at[pl.ds(place + row - start, rows)]))
            for k, offset, l, other, row in shared:
                for side, (window, at) in enumerate(((k, offset), (l, other))):
                    copies.append((flat_ref.at[window, pl.ds(at, 16)], edges.at[fixed, side]))
                fixes.append((fixed, place + row - start))
                fixed += 1
            copies = [pltpu.make_async_copy(*ends, sem.at[count + i]) for i, ends in enumerate(copies)]
            count += len(copies)
            for copy in copies:
                copy.start()
            waits.append(functools.partial(self.loaded, stage, edges, copies, fixes))
        return waits

    @staticmethod
    def loaded(stage, edges, copies, fixes):
        for copy in copies:
            copy.wait()
        for index, row in fixes:
            stage[pl.ds(row, 16), :] = edges[index, 0] + edges[index, 1]


MESH = pl.DeviceIdType.MESH
CHUNK = 576
CHUNKS = 12
WINDOW = CHUNK * CHUNKS
CARRIED = 2 * CHUNKS // 3
TRADED = CHUNKS // 3
NEEDED = 9
READY, READY_TRADED = 6, 3
TAKEN = ((0, 4, 8, 8, 8, 8), (0, 0, 4, 8, 8, 8))


def fits_ring(replicas, shards, shard_size):
    return shards == 8 and replicas == 4 and shard_size % LANES == 0 and shard_size <= LANES * (WINDOW - 16)


def gray(place):
    return place + (place // 2) * (1 - 2 * (place % 2))


class Ring:
    def __init__(self):
        self.me = lax.axis_index("fsdp")
        self.core = self.me % 2
        self.place = self.flip(gray(self.me // 2))
        self.replica = lax.axis_index("dp")
        self.half = self.replica % 2
        self.sibling = self.me + 1 - 2 * self.core
        self.after = self.device(self.place + 1)
        self.before = self.device(self.place + 3)
        self.partner = self.replica + 1 - 2 * self.half
        self.shards = lax.axis_size("fsdp")
        self.others = [(self.me + 1 + index) % self.shards for index in range(self.shards - 1)]

    def flip(self, place):
        return (place + self.core * (4 - 2 * place)) % 4

    def device(self, place):
        return gray(self.flip(place % 4)) * 2 + self.core

    def pick(self, table, place):
        found = jnp.int32(0)
        for index, value in enumerate(table):
            found = found + jnp.where(place == index, value, 0)
        return found


class Gather:
    def __init__(self, own, whole, gain_rows, around, across, trade, own_sems):
        self.ring, self.own, self.whole, self.gain_rows = Ring(), own, whole, gain_rows
        self.around_sems, self.across_sems, self.trade_sems, self.own_sems = around, across, trade, own_sems
        core, place = self.ring.core, self.ring.place
        self.first = [CARRIED, jnp.where(core == 0, READY, 0), 0, 0]
        self.first_traded = [TRADED, jnp.where(core == 0, READY_TRADED, 0), 0, 0]

    def greet(self):
        barrier = pltpu.get_barrier_semaphore()
        for device in [{"fsdp": other} for other in self.ring.others] + [{"dp": self.ring.partner}]:
            pl.semaphore_signal(barrier, inc=1, device_id=device, device_id_type=MESH)
        pl.semaphore_wait(barrier, self.ring.shards)

    def gain_copy(self, index):
        return pltpu.make_async_remote_copy(
            src_ref=self.gain_rows,
            dst_ref=self.gain_rows,
            send_sem=self.own_sems.at[3 + index],
            recv_sem=self.own_sems.at[2],
            device_id={"fsdp": self.ring.others[index]},
            device_id_type=MESH,
        )

    def send_gains(self, place):
        @pl.when(self.ring.me == self.ring.shards - 1)
        def _():
            self.gain_rows[...] = self.own[pl.ds(place, 16), :]
            for index in range(self.ring.shards - 1):
                self.gain_copy(index).start()

    def take_gains(self):
        last = self.ring.me == self.ring.shards - 1

        @pl.when(last)
        def _():
            for index in range(self.ring.shards - 1):
                self.gain_copy(index).wait_send()

        @pl.when(jnp.logical_not(last))
        def _():
            self.gain_copy(0).wait_recv()

    def carried(self, j):
        return (j // 2) * 3 + (1 - j % 2) * (1 + self.ring.half)

    def rows(self, i):
        return pl.ds(pl.multiple_of(i * CHUNK, 16), CHUNK)

    def copy(self, window, i, send_sem, recv_sem, device, own=False):
        source = self.own.at[self.rows(i)] if own else self.whole.at[window, self.rows(i)]
        return pltpu.make_async_remote_copy(
            src_ref=source,
            dst_ref=self.whole.at[window, self.rows(i)],
            send_sem=send_sem,
            recv_sem=recv_sem,
            device_id=device,
            device_id_type=MESH,
        )

    def around(self, origin, j, own=False):
        sems = self.around_sems
        return self.copy(
            self.ring.me if own else self.ring.device(origin),
            self.carried(j),
            sems.at[0, origin, j],
            sems.at[1, origin, j],
            {"fsdp": self.ring.after},
            own,
        )

    def across(self, origin, i):
        sems = self.across_sems
        return self.copy(
            self.ring.device(origin), i, sems.at[0, origin, i], sems.at[1, origin, i], {"fsdp": self.ring.sibling}
        )

    def trade(self, origin, j, half):
        sems = self.trade_sems
        return self.copy(
            self.ring.device(origin),
            3 * j + 1 + half,
            sems.at[0, origin, j],
            sems.at[1, origin, j],
            {"dp": self.ring.partner},
        )

    def own_copies(self):
        ring = self.ring
        keep = pltpu.make_async_copy(self.own, self.whole.at[ring.me], self.own_sems.at[10])
        give = pltpu.make_async_remote_copy(
            src_ref=self.own,
            dst_ref=self.whole.at[ring.me],
            send_sem=self.own_sems.at[1],
            recv_sem=self.own_sems.at[0],
            device_id={"fsdp": ring.sibling},
            device_id_type=MESH,
        )
        return keep, give

    def take(self, origin, low, high):
        low = jnp.where(self.ring.place == origin, high, low)

        @pl.loop(low, high)
        def _(j):
            self.around(origin, j).wait_recv()

            @pl.when(origin != (self.ring.place + 1) % 4)
            def _():
                self.around(origin, j).start()

            @pl.when(j % 2 == 0)
            def _():
                self.trade(origin, j // 2, self.ring.half).start()

            self.across(origin, self.carried(j)).start()

    def take_traded(self, origin, low, high):
        other = 1 - self.ring.half
        low = jnp.where(self.ring.place == origin, high, low)

        @pl.loop(low, high)
        def _(j):
            self.trade(origin, j, other).wait_recv()
            self.across(origin, 3 * j + 1 + other).start()

    def wait_across(self, origin, low, high):
        sibling_place = (4 - self.ring.place) % 4
        low = jnp.where(sibling_place == origin, high, low)

        @pl.loop(low, high)
        def _(i):
            self.across(origin, i).wait_recv()

    def send_own(self, low, high):
        @pl.loop(low, high)
        def _(j):
            self.around(self.ring.place, j, own=True).start()

    def begin(self, gain_place):
        place = self.ring.place
        first = self.first[1]
        self.greet()
        self.send_gains(gain_place)
        self.send_own(0, jnp.where(place == 1, first, jnp.where(place == 2, 0, CARRIED)))
        keep, give = self.own_copies()
        keep.start()
        give.start()
        self.take(3, 0, jnp.where(place == 0, CARRIED, 0))
        self.take(1, 0, first)
        self.take(0, 0, CARRIED)
        self.send_own(jnp.where(place == 1, first, jnp.where(place == 2, 0, CARRIED)), CARRIED)
        self.take(3, 0, jnp.where(place == 1, CARRIED, 0))
        for origin in (1, 0):
            self.take_traded(origin, 0, self.first_traded[origin])
        self.take_gains()
        keep.wait()
        give.wait_recv()
        self.wait_across(0, 0, CHUNKS)
        self.wait_across(1, 0, jnp.where(self.ring.core == 1, NEEDED, 0))

    def taken(self, origin, step):
        hops = (self.ring.place + 4 - origin) % 4
        early = (origin == 3) & (hops < 3)
        count = jnp.where(hops == 2, self.ring.pick(TAKEN[0], step), self.ring.pick(TAKEN[1], step))
        count = jnp.where((hops == 1) | (origin == 3), jnp.where(step >= 0, CARRIED, 0), count)
        return jnp.maximum(jnp.where(early, CARRIED, count), self.first[origin])

    def go_on(self, step, steps):
        for origin in (3, 2, 1):
            self.take(origin, self.taken(origin, step - 1), self.taken(origin, step))
        for origin in (3, 2, 1):
            first = self.first_traded[origin]
            low = jnp.maximum(first, jnp.where(step == 0, 0, (self.taken(origin, step - 2) + 1) // 2))
            high = jnp.maximum(first, jnp.where(step == steps - 1, TRADED, (self.taken(origin, step - 1) + 1) // 2))
            self.take_traded(origin, low, high)

        @pl.when(step == steps - 1)
        def _():
            self.finish()

    def finish(self):
        place = self.ring.place
        self.wait_across(1, jnp.where(self.ring.core == 1, NEEDED, 0), CHUNKS)
        self.wait_across(2, 0, CHUNKS)
        self.wait_across(3, 0, CHUNKS)
        self.own_copies()[1].wait_send()
        for origin in range(4):

            @pl.loop(0, jnp.where((place + 1) % 4 == origin, 0, CARRIED))
            def _(j):
                self.around(origin, j).wait_send()

            @pl.loop(0, jnp.where(place == origin, 0, TRADED))
            def _(j):
                self.trade(origin, j, self.ring.half).wait_send()

            @pl.loop(0, jnp.where(place == origin, 0, CHUNKS))
            def _(i):
                self.across(origin, i).wait_send()


GATHER_SCRATCH = [
    pltpu.VMEM((WINDOW, LANES), BF),
    pltpu.VMEM((16, LANES), BF),
    pltpu.SemaphoreType.DMA((2, 4, CARRIED)),
    pltpu.SemaphoreType.DMA((2, 4, CHUNKS)),
    pltpu.SemaphoreType.DMA((2, 4, TRADED)),
    pltpu.SemaphoreType.DMA((11,)),
]


def to_matrix(stage, place, spread, matrix, shape, height=512):
    wide = shape[1] // LANES
    for top in range(0, shape[0], height):
        rows = height * wide
        spread[pl.ds(0, rows), :] = stage[pl.ds(place + top * wide, rows), :].astype(F32)
        for j in range(wide):
            matrix[top : top + height, LANES * j : LANES * (j + 1)] = spread[
                pl.ds(j, height, stride=wide), :
            ].astype(BF)


def norm_rows(values):
    centre = jnp.mean(values, axis=-1, keepdims=True)
    shifted = values - centre
    inverse = lax.rsqrt(jnp.mean(shifted * shifted, axis=-1, keepdims=True) + 1e-05)
    return shifted * inverse, inverse


def norm_back(unit, inverse, gain, grad):
    scaled = grad * gain
    along = jnp.mean(scaled * unit, axis=-1, keepdims=True)
    return inverse * (scaled - jnp.mean(scaled, axis=-1, keepdims=True) - unit * along)


def own_frame(rows):
    frame = lax.broadcasted_iota(jnp.int32, (rows // GROUP, GROUP, SLOTS), 1).reshape(rows, SLOTS)
    return frame == lax.broadcasted_iota(jnp.int32, (rows, SLOTS), 1) // NT


def same_token():
    a = lax.broadcasted_iota(jnp.int32, (SLOTS, SLOTS), 0) % NT
    b = lax.broadcasted_iota(jnp.int32, (SLOTS, SLOTS), 1) % NT
    return (a == b).astype(BF)


def learner_mask():
    return own_frame(D)


def section_kernel(
    windows,
    images,
    embedding,
    flat,
    grid_out,
    pooled_out,
    shifts_out,
    conv_out,
    learner_out,
    gains_out,
    *rest,
):
    step = pl.program_id(0)
    if windows.shards > 1:
        master = flat
        flat, stage, spread, film, modulated, edges, sems, own, *gather_sems = rest
        gather = Gather(own, flat, *gather_sems)
    else:
        gather = None
        stage, spread, film, modulated, edges, sems = rest

    @pl.when(step == 0)
    def _():
        if gather:
            rows = master.shape[0]
            spread[pl.ds(0, 16), :] = jnp.zeros((16, LANES), F32)
            tail = rows // 16 * 16
            spread[pl.ds(tail, WINDOW - tail), :] = jnp.zeros((WINDOW - tail, LANES), F32)
            spread[pl.ds(gather.ring.me * rows % 16, rows), :] = master[...]
            own[...] = spread[pl.ds(0, WINDOW), :].astype(BF)
            gather.begin(START["gains"] - windows.first[-1])
        learner_rows = HEAD_PART - START["learner"]
        parts = [(0, HEAD_PART, 0)]
        if gather is None:
            parts.append((START["gains"], ROWS, HEAD_PART))
        for wait in windows.load(flat, stage, edges, sems, parts):
            wait()
        if gather:
            stage[pl.ds(HEAD_PART, 16), :] = gather.gain_rows[...]
        to_matrix(stage, 0, spread, film, SHAPES["film"])
        for side in range(2):
            shifts_out[side] = mm(embedding[...], film[:, CIN * side : CIN * (side + 1)])
        to_matrix(stage, START["conv"], spread, conv_out, SHAPES["conv"])
        packed = stage[pl.ds(START["learner"], learner_rows), :].astype(F32)
        opened = jnp.broadcast_to(packed[:, None, :], (learner_rows, GROUP, LANES)).reshape(D, SLOTS)
        opened = jnp.where(learner_mask(), opened, 0.0).astype(BF)
        learner_out[...] = mm(opened, same_token()).astype(BF)
        gain_rows = stage[pl.ds(HEAD_PART, 16), :].astype(F32)
        for i in range(4):
            for j in range(4):
                gains_out[i : i + 1, LANES * j : LANES * (j + 1)] = gain_rows[4 * i + j : 4 * i + j + 1]

    here = pl.ds(pl.multiple_of(step * GROUP, GROUP), GROUP)
    scale = 1.0 + shifts_out[0, here, :]
    offset = shifts_out[1, here, :]
    modulated[...] = (images[...].astype(F32) * scale[None] + offset[None]).astype(BF).reshape(CELLS, CIN)
    grid = mm(modulated[...], conv_out[...])
    grid_out[...] = grid.astype(BF)
    unit, _ = norm_rows(grid)
    normed = (unit * gains_out[0:1, :]).astype(BF)
    maps = jax.nn.sigmoid(mm(normed, learner_out[...]))
    maps = jnp.where(own_frame(CELLS), maps, 0.0).astype(BF)
    pooled_out[...] = mm_tn(maps, normed) * (1.0 / POS)
    if gather:
        gather.go_on(step, pl.num_programs(0))


def section(windows, images, embedding, flat):
    frames = images.shape[1]
    steps = frames // GROUP
    whole = lambda *shape: pl.BlockSpec(shape, lambda i: (0,) * len(shape))
    gathers = windows.shards > 1
    film_rows = SHAPES["film"][0] * SHAPES["film"][1] // LANES
    return pl.pallas_call(
        functools.partial(section_kernel, windows),
        grid=(steps,),
        in_specs=[
            pl.BlockSpec((POS, GROUP, CIN), lambda i: (0, i, 0)),
            whole(frames, E),
            whole(*flat.shape) if gathers else pl.BlockSpec(memory_space=pl.ANY),
        ],
        out_specs=[
            pl.BlockSpec((CELLS, D), lambda i: (i, 0)),
            pl.BlockSpec((SLOTS, D), lambda i: (i, 0)),
            whole(2, frames, CIN),
            whole(CIN, D),
            whole(D, SLOTS),
            whole(4, D),
        ]
        + [pl.BlockSpec(memory_space=pl.ANY)] * gathers,
        out_shape=[
            jax.ShapeDtypeStruct((steps * CELLS, D), BF),
            jax.ShapeDtypeStruct((frames * NT, D), F32),
            jax.ShapeDtypeStruct((2, frames, CIN), F32),
            jax.ShapeDtypeStruct((CIN, D), BF),
            jax.ShapeDtypeStruct((D, SLOTS), BF),
            jax.ShapeDtypeStruct((4, D), F32),
        ]
        + [jax.ShapeDtypeStruct((windows.shards, WINDOW, LANES), BF)] * gathers,
        scratch_shapes=[
            pltpu.VMEM((HEAD_PART + 16, LANES), BF),
            pltpu.VMEM((film_rows + 32, LANES), F32),
            pltpu.VMEM(SHAPES["film"], BF),
            pltpu.VMEM((CELLS, CIN), BF),
            pltpu.VMEM((8, 2, 16, LANES), BF),
            pltpu.SemaphoreType.DMA((32,)),
        ]
        + GATHER_SCRATCH * gathers,
        compiler_params=pltpu.CompilerParams(
            vmem_limit_bytes=60 * MIB,
            **(dict(collective_id=0, has_side_effects=True) if gathers else {}),
        ),
        cost_estimate=pl.CostEstimate(
            flops=2 * frames * POS * CIN * D, bytes_accessed=frames * POS * CIN * 2, transcendentals=0
        ),
    )(images, embedding, flat)


def gelu_parts(x):
    inner = 0.7978845608028654 * (x + 0.044715 * x * x * x)
    bent = jnp.tanh(inner)
    value = 0.5 * x * (1.0 + bent)
    slope = 0.5 * (1.0 + bent) + 0.5 * x * (1.0 - bent * bent) * 0.7978845608028654 * (
        1.0 + 3.0 * 0.044715 * x * x
    )
    return value, slope


TOP = 256


def layer_part(
    windows,
    refs,
    reduce,
    late_out,
    stage,
    spread,
    triple,
    output,
    upward,
    downward,
    action,
    keys,
    values,
    grad_keys,
    grad_values,
    shares,
    first_normed,
    logits_back,
    edges,
    sems,
):
    start, flat, gains, steps_in, targets_in, grad_start, sums_out = refs
    tokens = start.shape[0]
    frames = tokens // NT
    place = {name: START[name] - HEAD_PART for name in SHAPES}
    matrices = dict(triple=triple, output=output, upward=upward, downward=downward, action=action)
    rows_of = lambda name: SHAPES[name][0] * SHAPES[name][1] // LANES
    waits = windows.load(
        flat, stage, edges, sems, [(START[name], START[name] + rows_of(name), place[name]) for name in matrices]
    )

    def bring(name):
        waits[list(matrices).index(name)]()
        to_matrix(stage, place[name], spread, matrices[name], SHAPES[name], TOP)

    is_last = lax.broadcasted_iota(jnp.int32, (tokens, D), 0) % NT == NT - 1

    def take_last(rows):
        return jnp.sum(jnp.where(is_last, rows, 0.0).reshape(frames, NT, D), axis=1)

    def spread_last(rows):
        wide = jnp.broadcast_to(rows[:, None, :], (frames, NT, D)).reshape(tokens, D)
        return jnp.where(is_last, wide, 0.0)

    gain = [gains[i : i + 1, :] for i in range(4)]

    first_unit, first_inverse = norm_rows(start[...])
    first_normed[...] = (first_unit * gain[1]).astype(BF)
    last_start = take_last(start[...])
    last_unit, _ = norm_rows(last_start)
    last_normed = (last_unit * gain[1]).astype(BF)
    bring("triple")
    queries = mm(last_normed, triple[:, :D]).astype(BF)
    keys[...] = mm(first_normed[...], triple[:, D : 2 * D]).astype(BF)
    values[...] = mm(first_normed[...], triple[:, 2 * D :]).astype(BF)
    token_rows = tokens // LANES
    episode_row = jnp.concatenate([steps_in[i : i + 1, :] for i in range(token_rows)], axis=1)
    key_place = lax.broadcasted_iota(jnp.int32, (frames, tokens), 1)
    query_place = lax.broadcasted_iota(jnp.int32, (frames, tokens), 0) * NT + (NT - 1)
    own_key = (key_place == query_place).astype(BF)
    column = lambda row: mm_nt(own_key, jnp.broadcast_to(row, (8, tokens)).astype(F32).astype(BF))[:, :1]
    episode_last = column(episode_row // BINS) * float(BINS) + column(episode_row % BINS)
    allowed = (episode_last.astype(jnp.int32) == episode_row) & (key_place <= query_place)
    diagonal = lax.broadcasted_iota(jnp.int32, (frames, LANES), 0) == lax.broadcasted_iota(
        jnp.int32, (frames, LANES), 1
    )
    valid_row = jnp.broadcast_to(steps_in[token_rows : token_rows + 1, :], (8, LANES))
    valid_flags = mm_nt(diagonal.astype(BF), valid_row.astype(F32).astype(BF))[:, :1]
    targets = mm_nt(diagonal[:, :frames].astype(BF), targets_in[...].astype(F32).astype(BF)).astype(jnp.int32)
    attended = []
    for h in range(HEADS):
        own = slice(HD * h, HD * (h + 1))
        scores = mm_nt(queries[:, own], keys[:, own]) * HD ** (-0.5)
        scores = jnp.where(allowed, scores, -1e30)
        powers = jnp.exp(scores - jnp.max(scores, axis=-1, keepdims=True))
        part = powers / jnp.sum(powers, axis=-1, keepdims=True)
        shares[h] = part
        attended.append(mm(part.astype(BF), values[:, own]))
    merged = jnp.concatenate(attended, axis=1).astype(BF)
    bring("output")
    middle = last_start + mm(merged, output[...])
    second_unit, second_inverse = norm_rows(middle)
    second_normed = (second_unit * gain[2]).astype(BF)
    bring("upward")
    activated, slope = gelu_parts(mm(second_normed, upward[...]))
    hidden = activated.astype(BF)
    bring("downward")
    end = middle + mm(hidden, downward[...])
    final_unit, final_inverse = norm_rows(end)
    final_rows = (final_unit * gain[3]).astype(BF)

    bring("action")
    bins = lax.broadcasted_iota(jnp.int32, (frames, BINS), 1)
    loss = jnp.zeros((frames, 1), F32)
    for a in range(ACT):
        own = slice(BINS * a, BINS * (a + 1))
        logits = mm(final_rows, action[:, own])
        shifted = logits - jnp.max(logits, axis=-1, keepdims=True)
        powers = jnp.exp(shifted)
        total = jnp.sum(powers, axis=-1, keepdims=True)
        hit = targets[:, a : a + 1] == bins
        loss += jnp.log(total) - jnp.sum(jnp.where(hit, shifted, 0.0), axis=-1, keepdims=True)
        logits_back[:, own] = ((powers / total - hit.astype(F32)) * valid_flags).astype(BF)
    place_row = lax.broadcasted_iota(jnp.int32, (8, LANES), 0)
    sums_out[...] = jnp.where(
        place_row == 0, jnp.sum(loss * valid_flags), jnp.where(place_row == 1, jnp.sum(valid_flags), 0.0)
    )

    def put(name, parts):
        height, breadth = SHAPES[name]
        wide = breadth // LANES
        rows = TOP * wide
        for top in range(0, height, TOP):
            j = 0
            for left, right in parts:
                rounded_left = left[:, top : top + TOP]
                for k in range(0, right.shape[1], 2 * LANES):
                    part = mm_tn(rounded_left, right[:, k : k + 2 * LANES])
                    spread[pl.ds(j, TOP, stride=wide), :] = part[:, :LANES]
                    spread[pl.ds(j + 1, TOP, stride=wide), :] = part[:, LANES:]
                    j += 2
            stage[pl.ds(place[name] + top * wide, rows), :] = spread[pl.ds(0, rows), :].astype(BF)

    def give(devices, unit):
        if reduce:
            for device in devices:
                reduce.give_early(stage, device)
            reduce.advance(unit, late=False)

    put("action", [(final_rows, logits_back[...])])
    grad_final = mm_nt(logits_back[...], action[...])
    gain_final = jnp.sum(grad_final * final_unit, axis=0, keepdims=True)
    grad_last = norm_back(final_unit, final_inverse, gain[3], grad_final)
    rounded = grad_last.astype(BF)
    put("downward", [(hidden, rounded)])
    give((7, 6), -5)
    grad_upward = (mm_nt(rounded, downward[...]) * slope).astype(BF)
    put("upward", [(second_normed, grad_upward)])
    give((5, 4), -4)
    grad_second = mm_nt(grad_upward, upward[...])
    gain_second = jnp.sum(grad_second * second_unit, axis=0, keepdims=True)
    grad_last = grad_last + norm_back(second_unit, second_inverse, gain[2], grad_second)
    rounded = grad_last.astype(BF)
    put("output", [(merged, rounded)])
    grad_attended = mm_nt(rounded, output[...]).astype(BF)
    give((), -3)
    grad_queries = []
    for h in range(HEADS):
        own = slice(HD * h, HD * (h + 1))
        part = shares[h]
        grad_shares = mm_nt(grad_attended[:, own], values[:, own])
        grad_values[:, own] = mm_tn(part.astype(BF), grad_attended[:, own]).astype(BF)
        grad_scores = part * (grad_shares - jnp.sum(grad_shares * part, axis=-1, keepdims=True))
        grad_scores = grad_scores.astype(BF)
        grad_queries.append(mm(grad_scores, keys[:, own]) * HD ** (-0.5))
        grad_keys[:, own] = (mm_tn(grad_scores, queries[:, own]) * HD ** (-0.5)).astype(BF)
    grad_queries = jnp.concatenate(grad_queries, axis=1).astype(BF)
    put(
        "triple",
        [
            (last_normed, grad_queries),
            (first_normed[...], grad_keys[...]),
            (first_normed[...], grad_values[...]),
        ],
    )
    grad_start[...] = (
        mm_nt(grad_keys[...], triple[:, D : 2 * D])
        + mm_nt(grad_values[...], triple[:, 2 * D :])
        + spread_last(mm_nt(grad_queries, triple[:, :D]))
    )
    grad_first = grad_start[...]
    gain_first = jnp.sum(grad_first * first_unit, axis=0, keepdims=True)
    rows = []
    for part in (jnp.zeros((1, D), F32), gain_first, gain_second, gain_final):
        rows += [part[:, LANES * j : LANES * (j + 1)] for j in range(4)]
    stage[pl.ds(place["gains"], 16), :] = jnp.concatenate(rows, axis=0).astype(BF)
    stage[pl.ds(place["gains"] + 16, LATE_ROWS - place["gains"] - 16), :] = jnp.zeros(
        (LATE_ROWS - place["gains"] - 16, LANES), BF
    )
    give((3, 2), -2)
    grad_start[...] = norm_back(first_unit, first_inverse, gain[1], grad_first) + spread_last(grad_last)
    if reduce:
        reduce.keep_patch(stage)
        reduce.advance(-1, late=False)
        reduce.early_left(stage)
    else:
        out = pltpu.make_async_copy(stage, late_out, sems.at[0])
        out.start()
        out.wait()


def layer_scratch(tokens):
    frames = tokens // NT
    return [
        pltpu.VMEM((LATE_ROWS, LANES), BF),
        pltpu.VMEM((TOP * SHAPES["action"][1] // LANES + 32, LANES), F32),
        pltpu.VMEM(SHAPES["triple"], BF),
        pltpu.VMEM(SHAPES["output"], BF),
        pltpu.VMEM(SHAPES["upward"], BF),
        pltpu.VMEM(SHAPES["downward"], BF),
        pltpu.VMEM(SHAPES["action"], BF),
        pltpu.VMEM((tokens, D), BF),
        pltpu.VMEM((tokens, D), BF),
        pltpu.VMEM((tokens, D), BF),
        pltpu.VMEM((tokens, D), BF),
        pltpu.VMEM((HEADS, frames, tokens), F32),
        pltpu.VMEM((tokens, D), BF),
        pltpu.VMEM((frames, ACT * BINS), BF),
        pltpu.VMEM((8, 2, 16, LANES), BF),
        pltpu.SemaphoreType.DMA((32,)),
    ]


BLOCK = 256
BLOCKS = CIN // BLOCK
EARLY_ITEM = 1152
EARLY = WINDOW // EARLY_ITEM
FIRST_ITEM = 1008
ITEM = 576
LAST_ITEM = 288
ADD_ROWS = 144
SLAB = WINDOW + LAST_ITEM
FILM_ITEMS = 2 * BLOCKS
CONV_ITEMS = 8
LATE_ID = EARLY
LAST_ID = LATE_ID + FILM_ITEMS
IDS = LAST_ID + 1
EARLY_LAG, EARLY_LINE_LAG, LAG, LINE_LAG = 3, 3, 2, 2
EARLY_PACE = 3
EARLY_UNITS = ((99, 0, -3, -3), (99, -2, -3, -1))
FIRST_SCALE, FIRST_OFFSET, FIRST_CONV, LAST_UNIT = 8, 7, 9, 18
COMPUTE_UNITS = 6 + 2 * BLOCKS
UNITS = max(LAST_UNIT + 3 * LAG + 4 * LINE_LAG, 5 * EARLY_PACE + 3 * EARLY_LAG + 4 * EARLY_LINE_LAG) + 1
CONV_BEFORE = (0, 0, 1, 3, 4, 6, 8)
OWN_CONV = 1280
TAIL_CONV = 1152
FILM_FIRST = (0, 272)
FILM_HEIGHT = (288, 240)
SQUARES = 2
RING_PLACE = (0, 0, 1, 3, 3, 1, 2, 2)


def added(parts):
    total = parts[0].astype(F32)
    for part in parts[1:]:
        total = total + part.astype(F32)
    return total


class Reduce:
    def __init__(self, shard_rows, patch, own, sibling, ring_in, z_in, sems, z_sems):
        self.ring = ring = Ring()
        self.shard_rows, self.patch = shard_rows, patch
        self.own, self.sibling, self.ring_in, self.z_in = own, sibling, ring_in, z_in
        self.sems, self.z_sems = sems, z_sems
        self.line = ring.replica + ring.core * (3 - 2 * ring.replica)

    def greet(self):
        barrier = pltpu.get_barrier_semaphore()
        devices = [{"fsdp": other} for other in self.ring.others]
        devices += [{"dp": (self.ring.replica + hops) % 4} for hops in (1, 2, 3)]
        for device in devices:
            pl.semaphore_signal(barrier, inc=1, device_id=device, device_id_type=MESH)
        pl.semaphore_wait(barrier, len(devices))

    def along(self, line):
        return {"dp": line + self.ring.core * (3 - 2 * line)}

    def stage_of(self, q):
        return (self.ring.place + 7 - q) % 4

    def rows(self, row, count):
        return pl.ds(pl.multiple_of(row, 16), count)

    def remote(self, source, target, send_sem, recv_sem, device):
        return pltpu.make_async_remote_copy(
            src_ref=source,
            dst_ref=target,
            send_sem=send_sem,
            recv_sem=recv_sem,
            device_id=device,
            device_id_type=MESH,
        )

    def to_sibling(self, source, q, ident, row, count):
        return self.remote(
            source,
            self.sibling.at[q, self.rows(row, count)],
            self.sems.at[0, q, ident],
            self.sems.at[1, q, ident],
            {"fsdp": self.ring.sibling},
        )

    def to_next(self, q, ident, row, count):
        rows = self.rows(row, count)
        return self.remote(
            self.own.at[q, rows],
            self.ring_in.at[jnp.minimum(self.stage_of(q), 2), rows],
            self.sems.at[2, q, ident],
            self.sems.at[3, q, ident],
            {"fsdp": self.ring.after},
        )

    def to_line(self, which, line, slot, ident, row, count, forward=False):
        rows = self.rows(row, count)
        return self.remote(
            self.z_in.at[1, rows] if forward else self.own.at[self.ring.place, rows],
            self.z_in.at[slot, rows],
            self.z_sems.at[which, ident],
            self.z_sems.at[2 + slot, ident],
            self.along(line),
        )

    def early_items(self, device):
        if device == 2:
            top = WINDOW - 2 * FIRST_ITEM
            items = [(i, top + FIRST_ITEM * i, FIRST_ITEM) for i in range(2)]
        else:
            items = [(i, EARLY_ITEM * i, EARLY_ITEM) for i in range(EARLY)]
        return items, self.shard_rows * device // 16 * 16 - HEAD_PART

    def give_early(self, stage, device):
        q = RING_PLACE[device]
        items, first = self.early_items(device)

        @pl.when(self.ring.core == device % 2)
        def _():
            top, count = items[0][1], sum(item[2] for item in items)
            self.own[q, pl.ds(top, count), :] = stage[pl.ds(first + top, count), :]

        @pl.when(self.ring.core != device % 2)
        def _():
            for ident, row, count in items:
                if device < 7 or ident < EARLY - 1:
                    self.to_sibling(stage.at[pl.ds(first + row, count)], q, ident, row, count).start()

    def keep_patch(self, stage):
        last = self.shard_rows * 7 // 16 * 16 - HEAD_PART + (EARLY - 1) * EARLY_ITEM
        self.patch[...] = stage[pl.ds(last, EARLY_ITEM), :]

    def early_left(self, stage):
        for device in range(2, 8):
            q = RING_PLACE[device]
            items, first = self.early_items(device)

            @pl.when(self.ring.core != device % 2)
            def _():
                for ident, row, count in items:
                    if device < 7 or ident < EARLY - 1:
                        self.to_sibling(stage.at[pl.ds(first + row, count)], q, ident, row, count).wait_send()

    def patch_gains(self, gain_rows):
        place = START["gains"] - (self.shard_rows * 7 // 16 * 16 + (EARLY - 1) * EARLY_ITEM)
        here = pl.ds(place, 16)
        self.patch[here, :] = (self.patch[here, :].astype(F32) + gain_rows).astype(BF)

        @pl.when(self.ring.core == 0)
        def _():
            self.to_sibling(self.patch, 2, EARLY - 1, (EARLY - 1) * EARLY_ITEM, EARLY_ITEM).start()

        @pl.when(self.ring.core == 1)
        def _():
            self.own[2, pl.ds((EARLY - 1) * EARLY_ITEM, EARLY_ITEM), :] = self.patch[...]

    def give_film(self, film, conv, step, half):
        item = 2 * step + half
        row = ITEM * item
        tiles = [half * (CIN // LANES) + 2 * step + a for a in range(2)]
        conv_rows = self.rows(96 * item, 96)
        for core in range(2):
            first, height = FILM_FIRST[core], FILM_HEIGHT[core]

            @pl.when(self.ring.core == core)
            def _():
                for a in range(2):
                    self.own[0, self.rows(row + height * a, height), :] = film[tiles[a], first : first + height, :]
                if core == 1:
                    self.own[0, self.rows(row + 2 * height, 96), :] = conv[conv_rows, :]

            @pl.when(self.ring.core != core)
            def _():
                ident = LATE_ID + item
                for a in range(2):
                    self.to_sibling(
                        film.at[tiles[a], pl.ds(first, height)], 0, ident, row + height * a, height
                    ).start()
                if core == 1:
                    self.to_sibling(conv.at[conv_rows], 0, ident, row + 2 * height, 96).start()

    def give_conv(self, conv, step):
        ring = self.ring

        @pl.loop(ring.pick(CONV_BEFORE, step), ring.pick(CONV_BEFORE, step + 1))
        def _(i):
            source = self.rows(OWN_CONV + ITEM * i, ITEM)

            @pl.when(ring.core == 0)
            def _():
                self.own[1, self.rows(ITEM * i, ITEM), :] = conv[source, :]

            @pl.when(ring.core == 1)
            def _():
                self.to_sibling(conv.at[source], 1, LATE_ID + i, ITEM * i, ITEM).start()

        @pl.when(step == BLOCKS - 1)
        def _():
            mine = pl.ds(OWN_CONV + CONV_ITEMS * ITEM, LAST_ITEM)
            tail = pl.ds(TAIL_CONV, LAST_ITEM)

            @pl.when(ring.core == 0)
            def _():
                self.own[1, pl.ds(CONV_ITEMS * ITEM, LAST_ITEM), :] = conv[mine, :]
                self.to_sibling(conv.at[tail], 0, LAST_ID, WINDOW, LAST_ITEM).start()

            @pl.when(ring.core == 1)
            def _():
                self.own[0, pl.ds(WINDOW, LAST_ITEM), :] = conv[tail, :]
                self.to_sibling(conv.at[mine], 1, LAST_ID, CONV_ITEMS * ITEM, LAST_ITEM).start()

    def add_up(self, q, row, count, others):
        @pl.loop(0, count // ADD_ROWS)
        def _(block):
            rows = self.rows(row + block * ADD_ROWS, ADD_ROWS)
            parts = [self.own[q, rows, :]] + [ref[which, rows, :] for ref, which in others]
            self.own[q, rows, :] = added(parts).astype(BF)

    def hop_ring(self, q, ident, row, count):
        stage = self.stage_of(q)
        self.to_sibling(self.own.at[q, self.rows(row, count)], q, ident, row, count).wait_recv()

        @pl.when(stage == 0)
        def _():
            self.add_up(q, row, count, [(self.sibling, q)])

        @pl.when(stage > 0)
        def _():
            self.to_next(q, ident, row, count).wait_recv()
            self.add_up(q, row, count, [(self.sibling, q), (self.ring_in, stage - 1)])

        @pl.when(stage < 3)
        def _():
            self.to_next(q, ident, row, count).start()

        @pl.when((stage == 3) & (self.line == 0))
        def _():
            self.to_line(0, 1, 0, ident, row, count).start()

        @pl.when((stage == 3) & (self.line == 3))
        def _():
            self.to_line(0, 2, 0, ident, row, count).start()

    def hop_line(self, ident, row, count):
        place = self.ring.place

        @pl.when(self.line == 2)
        def _():
            self.to_line(0, 1, 0, ident, row, count).wait_recv()
            self.add_up(place, row, count, [(self.z_in, 0)])
            self.to_line(0, 1, 1, ident, row, count).start()

        @pl.when(self.line == 1)
        def _():
            self.to_line(0, 1, 0, ident, row, count).wait_recv()
            self.to_line(0, 1, 1, ident, row, count).wait_recv()
            self.add_up(place, row, count, [(self.z_in, 0), (self.z_in, 1)])
            self.to_line(0, 0, 0, ident, row, count).start()
            self.to_line(1, 2, 1, ident, row, count).start()

    def hop_back(self, ident, row, count):
        @pl.when(self.line == 2)
        def _():
            self.to_line(0, 1, 1, ident, row, count).wait_recv()
            self.to_line(1, 3, 0, ident, row, count, forward=True).start()

        @pl.when(self.line != 2)
        def _():
            self.to_line(0, 1, 0, ident, row, count).wait_recv()

    def early(self, q, unit):
        core = self.ring.core
        begin = jnp.where(core == 0, self.ring.pick(EARLY_UNITS[0], q), self.ring.pick(EARLY_UNITS[1], q))
        at = unit - begin
        there = (q >= 2 - core) & (at >= 0) & (at % EARLY_PACE == 0) & (at < EARLY_PACE * EARLY)
        ident = at // EARLY_PACE
        return there, ident, EARLY_ITEM * ident

    def streams(self):
        core = self.ring.core

        def first(unit):
            at = unit - EARLY_UNITS[0][1]
            there = (at >= 0) & (at % EARLY_PACE == 0) & (at < 2 * EARLY_PACE)
            return there, at // EARLY_PACE, WINDOW - 2 * FIRST_ITEM + FIRST_ITEM * (at // EARLY_PACE)

        def scale(unit):
            at = unit - FIRST_SCALE
            return (at >= 0) & (at < FILM_ITEMS) & (at % 2 == 0), LATE_ID + at, ITEM * at

        def offset(unit):
            item = 2 * (unit - FIRST_OFFSET) + 1
            return (item >= 0) & (item < FILM_ITEMS), LATE_ID + item, ITEM * item

        def conv(unit):
            at = unit - FIRST_CONV
            item = at - jnp.where(at > 0, 1, 0) - jnp.where(at > 5, 1, 0)
            there = (at >= 0) & (at != 1) & (at != 5) & (item < CONV_ITEMS)
            return there, LATE_ID + item, ITEM * item

        def last(unit):
            return unit == LAST_UNIT, LAST_ID, jnp.where(core == 0, CONV_ITEMS * ITEM, WINDOW)

        return [
            (1, core == 0, FIRST_ITEM, first, EARLY_LAG, EARLY_LINE_LAG),
            (0, core >= 0, ITEM, scale, LAG, LINE_LAG),
            (0, core >= 0, ITEM, offset, LAG, LINE_LAG),
            (1, core == 0, ITEM, conv, LAG, LINE_LAG),
            (1 - core, core >= 0, LAST_ITEM, last, LAG, LINE_LAG),
        ]

    def advance(self, unit, late=True):
        ring, line = self.ring, self.line
        streams = self.streams()[: None if late else 1]

        @pl.loop(2 - ring.core, 4)
        def _(q):
            there, ident, row = self.early(q, unit - EARLY_LAG * self.stage_of(q))

            @pl.when(there)
            def _():
                self.hop_ring(q, ident, row, EARLY_ITEM)

        for q, has, count, item, lag, _ in streams:
            there, ident, row = item(unit - lag * self.stage_of(q))

            @pl.when(has & there)
            def _():
                self.hop_ring(q, ident, row, count)

        owners = [(ring.place >= 0, EARLY_ITEM, functools.partial(self.early, ring.place), EARLY_LAG, EARLY_LINE_LAG)]
        owners += [(has & (ring.place == q), count, item, *lags) for q, has, count, item, *lags in streams]
        for owner, count, item, lag, line_lag in owners:
            there, ident, row = item(unit - 3 * lag - line_lag * jnp.where(line == 2, 1, 2))

            @pl.when(owner & there & ((line == 1) | (line == 2)))
            def _():
                self.hop_line(ident, row, count)

            there, ident, row = item(unit - 3 * lag - line_lag * jnp.where(line == 3, 4, 3))

            @pl.when(owner & there & (line != 1))
            def _():
                self.hop_back(ident, row, count)

    def finish(self):
        ring, line = self.ring, self.line

        def sent(q, ident, row, count, owner):
            @pl.when(self.stage_of(q) < 3)
            def _():
                self.to_next(q, ident, row, count).wait_send()

            @pl.when(owner)
            def _():
                self.to_line(0, 1, 0, ident, row, count).wait_send()

                @pl.when((line == 1) | (line == 2))
                def _():
                    self.to_line(1, 1, 0, ident, row, count).wait_send()

        def given(q, ident, row, count):
            self.to_sibling(self.own.at[q, self.rows(row, count)], q, ident, row, count).wait_send()

        @pl.loop(0, EARLY)
        def _(i):
            @pl.loop(2 - ring.core, 4)
            def _(q):
                sent(q, i, EARLY_ITEM * i, EARLY_ITEM, q == ring.place)

        @pl.loop(0, FILM_ITEMS)
        def _(i):
            sent(0, LATE_ID + i, ITEM * i, ITEM, ring.place == 0)
            given(0, LATE_ID + i, ITEM * i, ITEM)

        @pl.when(ring.core == 0)
        def _():
            for i in range(2):
                sent(1, i, WINDOW - FIRST_ITEM * (2 - i), FIRST_ITEM, ring.place == 1)

            @pl.loop(0, CONV_ITEMS)
            def _(i):
                sent(1, LATE_ID + i, ITEM * i, ITEM, ring.place == 1)

            sent(1, LAST_ID, CONV_ITEMS * ITEM, LAST_ITEM, ring.place == 1)
            given(0, LAST_ID, WINDOW, LAST_ITEM)
            given(2, EARLY - 1, (EARLY - 1) * EARLY_ITEM, EARLY_ITEM)

        @pl.when(ring.core == 1)
        def _():
            @pl.loop(0, CONV_ITEMS)
            def _(i):
                given(1, LATE_ID + i, ITEM * i, ITEM)

            given(1, LAST_ID, CONV_ITEMS * ITEM, LAST_ITEM)
            sent(0, LAST_ID, WINDOW, LAST_ITEM, ring.place == 0)

    def assemble(self, spread):
        ring, line = self.ring, self.line
        place = ring.place

        whole = self.sibling

        @pl.when((line == 0) | (line == 3))
        def _():
            whole[place] = self.z_in[0]

        @pl.when(line == 1)
        def _():
            whole[place] = self.own[place]

        @pl.when(line == 2)
        def _():
            whole[place] = self.z_in[1]

        wide = 2 * CIN // LANES
        for core in range(2):
            height = FILM_HEIGHT[core]

            @pl.when(ring.me == core)
            def _():
                for step in range(BLOCKS):
                    for half in range(2):
                        row = ITEM * (2 * step + half)
                        for a in range(2):
                            tile = half * (CIN // LANES) + 2 * step + a
                            spread[pl.ds(tile, height, stride=wide), :] = whole[
                                0, row + height * a : row + height * (a + 1), :
                            ].astype(F32)
                        if core == 1:
                            spread[pl.ds(height * wide + 96 * (2 * step + half), 96), :] = whole[
                                0, row + 2 * height : row + 2 * height + 96, :
                            ].astype(F32)
                if core == 1:
                    spread[pl.ds(height * wide + TAIL_CONV, LAST_ITEM), :] = whole[0, WINDOW:SLAB, :].astype(F32)

        @pl.when(ring.me > 1)
        def _():
            spread[pl.ds(0, WINDOW), :] = whole[place, 0:WINDOW, :].astype(F32)

    def shard_offset(self):
        me = self.ring.me
        second = self.shard_rows - FILM_FIRST[1] * (2 * CIN // LANES)
        return jnp.where(me == 1, second, self.shard_rows * me % 16)


class Sums:
    def __init__(self, plane, line, plane_sems, line_sems):
        self.ring = Ring()
        self.plane, self.line, self.plane_sems, self.line_sems = plane, line, plane_sems, line_sems

    def plane_copy(self, which, index):
        me = self.ring.me
        return pltpu.make_async_remote_copy(
            src_ref=self.plane.at[which, me],
            dst_ref=self.plane.at[which, me],
            send_sem=self.plane_sems.at[0, which, index],
            recv_sem=self.plane_sems.at[1, which, index],
            device_id={"fsdp": self.ring.others[index]},
            device_id_type=MESH,
        )

    def line_copy(self, hops):
        own = self.ring.replica
        return pltpu.make_async_remote_copy(
            src_ref=self.line.at[own],
            dst_ref=self.line.at[own],
            send_sem=self.line_sems.at[0, hops - 1],
            recv_sem=self.line_sems.at[1, hops - 1],
            device_id={"dp": (own + hops) % 4},
            device_id_type=MESH,
        )

    def give(self, which, value):
        self.plane[which, self.ring.me] = value
        for index in range(self.ring.shards - 1):
            self.plane_copy(which, index).start()

    def take(self, which):
        for index in range(self.ring.shards - 1):
            self.plane_copy(which, index).wait()
        return jnp.sum(self.plane[which], axis=0)

    def give_line(self, value):
        self.line[self.ring.replica] = value
        for hops in (1, 2, 3):
            self.line_copy(hops).start()

    def take_line(self):
        for hops in (1, 2, 3):
            self.line_copy(hops).wait()
        return jnp.sum(self.line[...], axis=0)


def back_kernel(
    windows,
    start,
    flat,
    gains,
    steps_in,
    targets,
    images,
    embedding,
    shifts,
    conv,
    learner,
    grid,
    *rest,
):
    reduces = windows.shards > 1
    if reduces:
        gradient, small_out, grad_start, sums_in, patch, own, sibling, ring_in, z_in, sems, z_sems, *rest = rest
        reduce = Reduce(windows.shard_rows, patch, own, sibling, ring_in, z_in, sems, z_sems)
        sums = Sums(*rest)
        late_out = None
        reduce.greet()
    else:
        film_out, conv_out, late_out, sums_in, gain_out, grad_start = rest
        reduce = None

    refs = (start, flat, gains, steps_in, targets, grad_start, sums_in)
    pl.run_scoped(functools.partial(layer_part, windows, refs, reduce, late_out), *layer_scratch(start.shape[0]))
    if reduces:
        sums.give(0, sums_in[...])

    def section_part(
        grad_grid, grad_sum, learner_sum, gain_sum, modulated, grad_scale, conv_sum, conv_spread, film, conv_flat, cells, sems
    ):
        frames = embedding.shape[0]
        groups = frames // GROUP
        wide = D // LANES
        learner_sum[...] = jnp.zeros_like(learner_sum)
        gain_sum[...] = jnp.zeros_like(gain_sum)

        def block_copy(step, slot):
            return pltpu.make_async_copy(
                images.at[:, :, pl.ds(pl.multiple_of(step * BLOCK, BLOCK), BLOCK)], cells.at[slot], sems.at[2 + slot]
            )

        def first_part(fetched):
            def fetch(g, slot):
                return pltpu.make_async_copy(
                    grid.at[pl.ds(pl.multiple_of(g * CELLS, 16), CELLS)], fetched.at[slot], sems.at[slot]
                )

            fetch(0, 0).start()
            block_copy(0, 0).start()

            @pl.loop(0, groups)
            def _(g):
                slot = g % 2
                fetch(g, slot).wait()

                @pl.when(g + 1 < groups)
                def _():
                    fetch(g + 1, 1 - slot).start()

                rows = pl.ds(pl.multiple_of(g * CELLS, 16), CELLS)
                unit, inverse = norm_rows(fetched[slot].astype(F32))
                normed = (unit * gains[0:1, :]).astype(BF)
                maps = jax.nn.sigmoid(mm(normed, learner[...]))
                mask = own_frame(CELLS)
                tokens = grad_start[pl.ds(pl.multiple_of(g * SLOTS, SLOTS), SLOTS), :]
                tokens = (tokens * (1.0 / POS)).astype(BF)
                grad_maps = mm_nt(normed, tokens)
                grad_logit = jnp.where(mask, grad_maps * maps * (1.0 - maps), 0.0).astype(BF)
                maps = jnp.where(mask, maps, 0.0).astype(BF)
                grad_normed = mm(maps, tokens) + mm_nt(grad_logit, learner[...])
                learner_sum[...] += mm_tn(normed, grad_logit)
                gain_sum[...] += jnp.sum(grad_normed * unit, axis=0, keepdims=True)
                back = norm_back(unit, inverse, gains[0:1, :], grad_normed).astype(BF)
                grad_grid[rows, :] = back
                grad_sum[pl.ds(pl.multiple_of(g * GROUP, GROUP), GROUP), :] = jnp.sum(
                    back.astype(F32).reshape(POS, GROUP, D), axis=0
                )
                if reduces:
                    reduce.advance(g, late=False)

        pl.run_scoped(first_part, pltpu.VMEM((2, CELLS, D), BF))

        total = learner_sum[...]
        high = total.astype(BF)
        token = same_token()
        spread_learner = mm(high, token) + mm((total - high.astype(F32)).astype(BF), token)
        spread_learner = jnp.where(learner_mask(), spread_learner, 0.0)
        conv_flat[pl.ds(CIN * wide, D * NT // LANES), :] = jnp.sum(
            spread_learner.reshape(D * NT // LANES, GROUP, LANES), axis=1
        ).astype(BF)
        if reduces:
            rows = [gain_sum[:, LANES * j : LANES * (j + 1)] for j in range(wide)]
            reduce.patch_gains(jnp.concatenate(rows + [jnp.zeros((16 - wide, LANES), F32)], axis=0))
            sums.give_line(sums.take(0))
        else:
            gain_out[...] = gain_sum[...]

        def put_film(step, half, grad):
            part = mm_tn(embedding[...], grad.astype(BF)).astype(BF)
            for i in range(BLOCK // LANES):
                film[half * (CIN // LANES) + step * (BLOCK // LANES) + i] = part[:, LANES * i : LANES * (i + 1)]

        total = grad_sum[...]
        high = total.astype(BF)
        low = (total - high.astype(F32)).astype(BF)
        for step in range(BLOCKS):
            weights = conv[BLOCK * step : BLOCK * (step + 1), :]
            put_film(step, 1, mm_nt(high, weights) + mm_nt(low, weights))

        @pl.loop(0, BLOCKS)
        def _(step):
            slot = step % 2
            block_copy(step, slot).wait()

            @pl.when(step + 1 < BLOCKS)
            def _():
                block_copy(step + 1, 1 - slot).start()

            channels = pl.ds(pl.multiple_of(step * BLOCK, BLOCK), BLOCK)
            weights = conv[channels, :]

            conv_sum[...] = jnp.zeros_like(conv_sum)
            for g in range(groups):
                rows = pl.ds(g * CELLS, CELLS)
                here = pl.ds(g * GROUP, GROUP)
                scale = 1.0 + shifts[0, here, channels]
                offset = shifts[1, here, channels]
                block = cells[slot, :, here, :].astype(F32)
                modulated[...] = (block * scale[None] + offset[None]).astype(BF).reshape(CELLS, BLOCK)
                conv_sum[...] += mm_tn(modulated[...], grad_grid[rows, :])
            for j in range(wide):
                conv_spread[pl.ds(j, BLOCK, stride=wide), :] = conv_sum[:, LANES * j : LANES * (j + 1)]
            conv_flat[pl.ds(pl.multiple_of(step * BLOCK * wide, 16), BLOCK * wide), :] = conv_spread[
                pl.ds(0, BLOCK * wide), :
            ].astype(BF)
            if reduces:
                reduce.give_conv(conv_flat, step)

                @pl.when(step == 0)
                def _():
                    for block in range(BLOCKS - 1):
                        reduce.give_film(film, conv_flat, block, 1)

                @pl.when(step == 1)
                def _():
                    reduce.give_film(film, conv_flat, BLOCKS - 1, 1)

                reduce.advance(6 + 2 * step)

            for g in range(groups):
                here = pl.ds(g * GROUP, GROUP)
                back = mm_nt(grad_grid[pl.ds(g * CELLS, CELLS), :], weights).reshape(POS, GROUP, BLOCK)
                grad_scale[here, :] = jnp.sum(back * cells[slot, :, here, :].astype(F32), axis=0)
            put_film(step, 0, grad_scale[...])
            if reduces:
                reduce.give_film(film, conv_flat, step, 0)


                reduce.advance(7 + 2 * step)

        if not reduces:
            copies = [
                pltpu.make_async_copy(film, film_out, sems.at[0]),
                pltpu.make_async_copy(conv_flat, conv_out, sems.at[1]),
            ]
            for copy in copies:
                copy.start()
            for copy in copies:
                copy.wait()
            return

        @pl.loop(COMPUTE_UNITS, UNITS)
        def _(unit):
            reduce.advance(unit)

        reduce.finish()

    frames = embedding.shape[0]
    pl.run_scoped(
        section_part,
        pltpu.VMEM((frames * POS, D), BF),
        pltpu.VMEM((frames, D), F32),
        pltpu.VMEM((D, SLOTS), F32),
        pltpu.VMEM((1, D), F32),
        pltpu.VMEM((CELLS, BLOCK), BF),
        pltpu.VMEM((frames, BLOCK), F32),
        pltpu.VMEM((BLOCK, D), F32),
        pltpu.VMEM((BLOCK * D // LANES + 8, LANES), F32),
        pltpu.VMEM((2 * CIN // LANES, E, LANES), BF),
        pltpu.VMEM(((CIN * D + D * NT) // LANES, LANES), BF),
        pltpu.VMEM((2, POS, frames, BLOCK), BF),
        pltpu.SemaphoreType.DMA((4,)),
    )
    if not reduces:
        return

    def last_part(spread, sems):
        count = gradient.shape[0]
        reduce.assemble(spread)
        offset = reduce.shard_offset()

        def move(block, squares):
            part = spread[pl.ds(offset + block * LANES, LANES), :]
            spread[pl.ds(pl.multiple_of(block * LANES, LANES), LANES), :] = part
            return squares + jnp.sum((part * part).reshape(LANES // 8, 8, LANES), axis=0)

        blocks = windows.shard_rows // LANES
        squares = lax.fori_loop(0, blocks, move, jnp.zeros((8, LANES), F32))
        for row in range(blocks * LANES, count, 8):
            part = spread[pl.ds(offset + row, 8), :]
            spread[pl.ds(row, 8), :] = part
            kept = lax.broadcasted_iota(jnp.int32, (8, LANES), 0) + row < windows.shard_rows
            squares = squares + jnp.where(kept, part * part, 0.0)
        sums.give(1, squares)
        out = pltpu.make_async_copy(spread.at[pl.ds(0, count)], gradient, sems.at[0])
        out.start()
        total = sums.take_line()
        total_squares = jnp.sum(sums.take(1))
        place_row = lax.broadcasted_iota(jnp.int32, (8, LANES), 0)
        small_out[...] = jnp.where(place_row == SQUARES, total_squares, total)
        out.wait()

    pl.run_scoped(last_part, pltpu.VMEM((SLAB + 32, LANES), F32), pltpu.SemaphoreType.DMA((1,)))


def back(windows, start, flat, gains, episode, valid, targets, images, embedding, shifts, conv, learner, grid):
    tokens = start.shape[0]
    frames = tokens // NT
    reduces = windows.shards > 1
    vmem = pl.BlockSpec(memory_space=pltpu.VMEM)
    anywhere = pl.BlockSpec(memory_space=pl.ANY)
    shard_rows = -(-windows.shard_rows // 8) * 8
    slab = lambda count: pltpu.VMEM((count, SLAB, LANES), BF)
    grad_start = pltpu.VMEM((tokens, D), F32)
    if reduces:
        scratch = [
            grad_start,
            pltpu.VMEM((8, LANES), F32),
            pltpu.VMEM((EARLY_ITEM, LANES), BF),
            slab(4),
            slab(4),
            slab(3),
            slab(2),
            pltpu.SemaphoreType.DMA((4, 4, IDS)),
            pltpu.SemaphoreType.DMA((4, IDS)),
            pltpu.VMEM((2, 8, 8, LANES), F32),
            pltpu.VMEM((4, 8, LANES), F32),
            pltpu.SemaphoreType.DMA((2, 2, 7)),
            pltpu.SemaphoreType.DMA((2, 3)),
        ]
        outs = [jax.ShapeDtypeStruct((shard_rows, LANES), F32), jax.ShapeDtypeStruct((8, LANES), F32)]
        out_specs = [anywhere, vmem]
    else:
        scratch = [grad_start]
        outs = [
            jax.ShapeDtypeStruct((2 * CIN // LANES, E, LANES), BF),
            jax.ShapeDtypeStruct(((CIN * D + D * NT) // LANES, LANES), BF),
            jax.ShapeDtypeStruct((LATE_ROWS, LANES), BF),
            jax.ShapeDtypeStruct((8, LANES), F32),
            jax.ShapeDtypeStruct((1, D), F32),
        ]
        out_specs = [anywhere] * 3 + [vmem] * 2
    return pl.pallas_call(
        functools.partial(back_kernel, windows),
        in_specs=[vmem, anywhere] + [vmem] * 3 + [anywhere] + [vmem] * 4 + [anywhere],
        out_specs=out_specs,
        out_shape=outs,
        scratch_shapes=scratch,
        compiler_params=pltpu.CompilerParams(
            vmem_limit_bytes=63 * MIB,
            **(dict(collective_id=1, has_side_effects=True) if reduces else {}),
        ),
        cost_estimate=pl.CostEstimate(
            flops=4 * frames * POS * CIN * D, bytes_accessed=frames * POS * CIN * 2, transcendentals=0
        ),
    )(
        start,
        flat,
        gains,
        jnp.concatenate([episode, valid, jnp.zeros((-frames % LANES,), jnp.int32)]).reshape(-1, LANES),
        targets.T,
        images,
        embedding,
        shifts,
        conv,
        learner,
        grid,
    )


def on_device(
    images, embedding, episode, valid_steps, targets, master, first_moment, second_moment, average
):
    images = images.transpose(1, 0, 2)
    replicas, shards = lax.axis_size("dp"), lax.axis_size("fsdp")
    if fits_ring(replicas, shards, master.shape[0]):
        windows = Windows(shards, master.shape[0] // LANES, WINDOW)
        flat = master.reshape(-1, LANES)
    else:
        whole_flat = lax.all_gather(master.astype(BF), "fsdp", axis=0, tiled=True)
        flat = jnp.pad(whole_flat.reshape(ROWS, LANES), ((0, FLAT_ROWS - ROWS), (0, 0)))[None]
        windows = Windows(1, ROWS, FLAT_ROWS)

    grid, start, shifts, conv, learner, gains, *gathered = section(windows, images, embedding, flat)
    if gathered:
        (flat,) = gathered
    results = back(
        windows, start, flat, gains, episode, valid_steps, targets, images, embedding, shifts, conv, learner, grid
    )
    if gathered:
        shard, small = results
        loss_sum, step_count, squares = small[0, 0], small[1, 0], small[SQUARES, 0]
        inverse_count = 1.0 / step_count
        grad_shard = shard.reshape(-1)[: master.shape[0]] * inverse_count
        squares = squares * inverse_count * inverse_count
    else:
        film, conv_flat, late, sums, gain_grid = results
        at = START["gains"] - HEAD_PART
        late = late[: ROWS - HEAD_PART].at[at : at + 4].set(gain_grid.reshape(4, LANES).astype(BF))
        gradient = jnp.concatenate([film.transpose(1, 0, 2).reshape(-1, LANES), conv_flat, late])
        loss_sum, step_count = lax.psum((sums[0, 0], sums[1, 0]), ("dp", "fsdp"))
        partial_shard = lax.psum_scatter(gradient.reshape(-1), "fsdp", scatter_dimension=0, tiled=True)
        grad_shard = lax.psum(partial_shard.astype(F32), "dp") / step_count
        squares = lax.psum(jnp.sum(grad_shard * grad_shard), "fsdp")
    grad_norm = jnp.sqrt(squares)
    clipped = grad_shard * (CLIP_NORM / jnp.maximum(grad_norm, CLIP_NORM))
    new_first = MOMENT_DECAY * first_moment + (1.0 - MOMENT_DECAY) * clipped
    new_second = MOMENT_DECAY * second_moment + (1.0 - MOMENT_DECAY) * clipped * clipped
    correction = 1.0 - MOMENT_DECAY**STEP
    new_master = master - LEARN_RATE * (
        new_first / correction / (jnp.sqrt(new_second / correction) + ADAM_EPSILON)
        + WEIGHT_DECAY * master
    )
    average_decay = min(AVERAGE_DECAY, (1.0 + STEP) / (10.0 + STEP))
    new_average = average_decay * average + (1.0 - average_decay) * new_master
    return (
        new_master,
        new_first,
        new_second,
        new_average,
        new_master.astype(BF),
        grad_norm,
        loss_sum,
        step_count,
    )


def solution(mesh):
    in_specs = (
        P(("dp", "fsdp"), None, None),
        P(("dp", "fsdp"), None),
        P(("dp", "fsdp")),
        P(("dp", "fsdp")),
        P(("dp", "fsdp"), None),
        P("fsdp"),
        P("fsdp"),
        P("fsdp"),
        P("fsdp"),
    )
    out_specs = (P("fsdp"), P("fsdp"), P("fsdp"), P("fsdp"), P("fsdp"), P(), P(), P())
    return jax.shard_map(
        on_device, mesh=mesh, in_specs=in_specs, out_specs=out_specs, check_vma=False
    )
```

```python
import functools

import jax
import jax.numpy as jnp
from jax import lax
from jax.experimental import pallas as pl
from jax.experimental.pallas import tpu as pltpu
from jax.sharding import PartitionSpec as P

D = 512
HEADS = 8
HD = 64
FF = 2048
E = 512
CIN = 1536
POS = 81
NT = 8
ACT = 11
BINS = 256
STEP = 10
LANES = 128
GROUP = 16
CELLS = POS * GROUP
SLOTS = GROUP * NT

MOMENT_DECAY = 0.5
LEARN_RATE = 0.02
WEIGHT_DECAY = 0.1
CLIP_NORM = 1.0
ADAM_EPSILON = 1e-08
AVERAGE_DECAY = 0.999
BF = jnp.bfloat16
F32 = jnp.float32
MIB = 2**20

SHAPES = {
    "film": (E, 2 * CIN),
    "conv": (CIN, D),
    "learner": (D, NT),
    "triple": (D, 3 * D),
    "output": (D, D),
    "upward": (D, FF),
    "downward": (FF, D),
    "action": (D, ACT * BINS),
    "gains": (4, D),
}


def row_starts():
    starts, row = {}, 0
    for name, (height, breadth) in SHAPES.items():
        starts[name] = row
        row += height * breadth // LANES
    return starts, row


START, ROWS = row_starts()
FLAT_ROWS = ROWS + 16
HEAD_PART = START["triple"]
LATE_ROWS = ROWS - HEAD_PART + 112


def mm(a, b):
    return jnp.dot(a, b, preferred_element_type=F32)


def mm_nt(a, b):
    return lax.dot_general(a, b, (((1,), (1,)), ((), ())), preferred_element_type=F32)


def mm_tn(a, b):
    return lax.dot_general(a, b, (((0,), (0,)), ((), ())), preferred_element_type=F32)


class Windows:
    def __init__(self, shards, shard_rows, size):
        self.shards, self.shard_rows, self.size = shards, shard_rows, size
        self.first = [shard_rows * k // 16 * 16 for k in range(shards)]

    def pieces(self, start, stop):
        inner, shared = [], []
        for k in range(self.shards):
            low, high = self.shard_rows * k, self.shard_rows * (k + 1)
            if k == self.shards - 1:
                high = (high + 15) // 16 * 16
            a, b = max(start, -(-low // 16) * 16), min(stop, high // 16 * 16)
            if a < b:
                inner.append((k, a - self.first[k], a, b - a))
            edge = low // 16 * 16
            if low % 16 and start <= edge < stop:
                shared.append((k - 1, edge - self.first[k - 1], k, edge - self.first[k], edge))
        return inner, shared

    def load(self, flat_ref, stage, edges, sem, parts):
        count, fixed, waits = 0, 0, []
        for start, stop, place in parts:
            copies, fixes = [], []
            inner, shared = self.pieces(start, stop)
            for k, offset, row, rows in inner:
                copies.append((flat_ref.at[k, pl.ds(offset, rows)], stage.at[pl.ds(place + row - start, rows)]))
            for k, offset, l, other, row in shared:
                for side, (window, at) in enumerate(((k, offset), (l, other))):
                    copies.append((flat_ref.at[window, pl.ds(at, 16)], edges.at[fixed, side]))
                fixes.append((fixed, place + row - start))
                fixed += 1
            copies = [pltpu.make_async_copy(*ends, sem.at[count + i]) for i, ends in enumerate(copies)]
            count += len(copies)
            for copy in copies:
                copy.start()
            waits.append(functools.partial(self.loaded, stage, edges, copies, fixes))
        return waits

    @staticmethod
    def loaded(stage, edges, copies, fixes):
        for copy in copies:
            copy.wait()
        for index, row in fixes:
            stage[pl.ds(row, 16), :] = edges[index, 0] + edges[index, 1]


MESH = pl.DeviceIdType.MESH
CHUNK = 576
CHUNKS = 12
WINDOW = CHUNK * CHUNKS
CARRIED = 2 * CHUNKS // 3
TRADED = CHUNKS // 3
NEEDED = 9
READY, READY_TRADED = 6, 3
TAKEN = ((0, 4, 8, 8, 8, 8), (0, 0, 4, 8, 8, 8))


def fits_ring(replicas, shards, shard_size):
    return shards == 8 and replicas == 4 and shard_size % LANES == 0 and shard_size <= LANES * (WINDOW - 16)


def gray(place):
    return place + (place // 2) * (1 - 2 * (place % 2))


class Ring:
    def __init__(self):
        self.me = lax.axis_index("fsdp")
        self.core = self.me % 2
        self.place = self.flip(gray(self.me // 2))
        self.replica = lax.axis_index("dp")
        self.half = self.replica % 2
        self.sibling = self.me + 1 - 2 * self.core
        self.after = self.device(self.place + 1)
        self.before = self.device(self.place + 3)
        self.partner = self.replica + 1 - 2 * self.half
        self.shards = lax.axis_size("fsdp")
        self.others = [(self.me + 1 + index) % self.shards for index in range(self.shards - 1)]

    def flip(self, place):
        return (place + self.core * (4 - 2 * place)) % 4

    def device(self, place):
        return gray(self.flip(place % 4)) * 2 + self.core

    def pick(self, table, place):
        found = jnp.int32(0)
        for index, value in enumerate(table):
            found = found + jnp.where(place == index, value, 0)
        return found


class Gather:
    def __init__(self, own, whole, gain_rows, around, across, trade, own_sems):
        self.ring, self.own, self.whole, self.gain_rows = Ring(), own, whole, gain_rows
        self.around_sems, self.across_sems, self.trade_sems, self.own_sems = around, across, trade, own_sems
        core, place = self.ring.core, self.ring.place
        self.first = [CARRIED, jnp.where(core == 0, READY, 0), 0, 0]
        self.first_traded = [TRADED, jnp.where(core == 0, READY_TRADED, 0), 0, 0]

    def greet(self):
        barrier = pltpu.get_barrier_semaphore()
        for device in [{"fsdp": other} for other in self.ring.others] + [{"dp": self.ring.partner}]:
            pl.semaphore_signal(barrier, inc=1, device_id=device, device_id_type=MESH)
        pl.semaphore_wait(barrier, self.ring.shards)

    def gain_copy(self, index):
        return pltpu.make_async_remote_copy(
            src_ref=self.gain_rows,
            dst_ref=self.gain_rows,
            send_sem=self.own_sems.at[3 + index],
            recv_sem=self.own_sems.at[2],
            device_id={"fsdp": self.ring.others[index]},
            device_id_type=MESH,
        )

    def send_gains(self, place):
        @pl.when(self.ring.me == self.ring.shards - 1)
        def _():
            self.gain_rows[...] = self.own[pl.ds(place, 16), :]
            for index in range(self.ring.shards - 1):
                self.gain_copy(index).start()

    def take_gains(self):
        last = self.ring.me == self.ring.shards - 1

        @pl.when(last)
        def _():
            for index in range(self.ring.shards - 1):
                self.gain_copy(index).wait_send()

        @pl.when(jnp.logical_not(last))
        def _():
            self.gain_copy(0).wait_recv()

    def carried(self, j):
        return (j // 2) * 3 + (1 - j % 2) * (1 + self.ring.half)

    def rows(self, i):
        return pl.ds(pl.multiple_of(i * CHUNK, 16), CHUNK)

    def copy(self, window, i, send_sem, recv_sem, device, own=False):
        source = self.own.at[self.rows(i)] if own else self.whole.at[window, self.rows(i)]
        return pltpu.make_async_remote_copy(
            src_ref=source,
            dst_ref=self.whole.at[window, self.rows(i)],
            send_sem=send_sem,
            recv_sem=recv_sem,
            device_id=device,
            device_id_type=MESH,
        )

    def around(self, origin, j, own=False):
        sems = self.around_sems
        return self.copy(
            self.ring.me if own else self.ring.device(origin),
            self.carried(j),
            sems.at[0, origin, j],
            sems.at[1, origin, j],
            {"fsdp": self.ring.after},
            own,
        )

    def across(self, origin, i):
        sems = self.across_sems
        return self.copy(
            self.ring.device(origin), i, sems.at[0, origin, i], sems.at[1, origin, i], {"fsdp": self.ring.sibling}
        )

    def trade(self, origin, j, half):
        sems = self.trade_sems
        return self.copy(
            self.ring.device(origin),
            3 * j + 1 + half,
            sems.at[0, origin, j],
            sems.at[1, origin, j],
            {"dp": self.ring.partner},
        )

    def own_copies(self):
        ring = self.ring
        keep = pltpu.make_async_copy(self.own, self.whole.at[ring.me], self.own_sems.at[10])
        give = pltpu.make_async_remote_copy(
            src_ref=self.own,
            dst_ref=self.whole.at[ring.me],
            send_sem=self.own_sems.at[1],
            recv_sem=self.own_sems.at[0],
            device_id={"fsdp": ring.sibling},
            device_id_type=MESH,
        )
        return keep, give

    def take(self, origin, low, high):
        low = jnp.where(self.ring.place == origin, high, low)

        @pl.loop(low, high)
        def _(j):
            self.around(origin, j).wait_recv()

            @pl.when(origin != (self.ring.place + 1) % 4)
            def _():
                self.around(origin, j).start()

            @pl.when(j % 2 == 0)
            def _():
                self.trade(origin, j // 2, self.ring.half).start()

            self.across(origin, self.carried(j)).start()

    def take_traded(self, origin, low, high):
        other = 1 - self.ring.half
        low = jnp.where(self.ring.place == origin, high, low)

        @pl.loop(low, high)
        def _(j):
            self.trade(origin, j, other).wait_recv()
            self.across(origin, 3 * j + 1 + other).start()

    def wait_across(self, origin, low, high):
        sibling_place = (4 - self.ring.place) % 4
        low = jnp.where(sibling_place == origin, high, low)

        @pl.loop(low, high)
        def _(i):
            self.across(origin, i).wait_recv()

    def send_own(self, low, high):
        @pl.loop(low, high)
        def _(j):
            self.around(self.ring.place, j, own=True).start()

    def begin(self, gain_place):
        place = self.ring.place
        first = self.first[1]
        self.send_gains(gain_place)
        self.send_own(0, jnp.where(place == 1, first, jnp.where(place == 2, 0, CARRIED)))
        keep, give = self.own_copies()
        keep.start()
        give.start()
        self.take(3, 0, jnp.where(place == 0, CARRIED, 0))
        self.take(1, 0, first)
        self.take(0, 0, CARRIED)
        self.send_own(jnp.where(place == 1, first, jnp.where(place == 2, 0, CARRIED)), CARRIED)
        self.take(3, 0, jnp.where(place == 1, CARRIED, 0))
        for origin in (1, 0):
            self.take_traded(origin, 0, self.first_traded[origin])
        self.take_gains()
        keep.wait()
        give.wait_recv()
        self.wait_across(0, 0, CHUNKS)
        self.wait_across(1, 0, jnp.where(self.ring.core == 1, NEEDED, 0))

    def taken(self, origin, step):
        hops = (self.ring.place + 4 - origin) % 4
        early = (origin == 3) & (hops < 3)
        count = jnp.where(hops == 2, self.ring.pick(TAKEN[0], step), self.ring.pick(TAKEN[1], step))
        count = jnp.where((hops == 1) | (origin == 3), jnp.where(step >= 0, CARRIED, 0), count)
        return jnp.maximum(jnp.where(early, CARRIED, count), self.first[origin])

    def go_on(self, step, steps):
        for origin in (3, 2, 1):
            self.take(origin, self.taken(origin, step - 1), self.taken(origin, step))
        for origin in (3, 2, 1):
            first = self.first_traded[origin]
            low = jnp.maximum(first, jnp.where(step == 0, 0, (self.taken(origin, step - 2) + 1) // 2))
            high = jnp.maximum(first, jnp.where(step == steps - 1, TRADED, (self.taken(origin, step - 1) + 1) // 2))
            self.take_traded(origin, low, high)

        @pl.when(step == steps - 1)
        def _():
            self.finish()

    def finish(self):
        place = self.ring.place
        self.wait_across(1, jnp.where(self.ring.core == 1, NEEDED, 0), CHUNKS)
        self.wait_across(2, 0, CHUNKS)
        self.wait_across(3, 0, CHUNKS)
        self.own_copies()[1].wait_send()
        for origin in range(4):

            @pl.loop(0, jnp.where((place + 1) % 4 == origin, 0, CARRIED))
            def _(j):
                self.around(origin, j).wait_send()

            @pl.loop(0, jnp.where(place == origin, 0, TRADED))
            def _(j):
                self.trade(origin, j, self.ring.half).wait_send()

            @pl.loop(0, jnp.where(place == origin, 0, CHUNKS))
            def _(i):
                self.across(origin, i).wait_send()


GATHER_SCRATCH = [
    pltpu.VMEM((WINDOW, LANES), BF),
    pltpu.VMEM((16, LANES), BF),
    pltpu.SemaphoreType.DMA((2, 4, CARRIED)),
    pltpu.SemaphoreType.DMA((2, 4, CHUNKS)),
    pltpu.SemaphoreType.DMA((2, 4, TRADED)),
    pltpu.SemaphoreType.DMA((11,)),
]


def to_matrix(stage, place, spread, matrix, shape, height=512):
    wide = shape[1] // LANES
    for top in range(0, shape[0], height):
        rows = height * wide
        spread[pl.ds(0, rows), :] = stage[pl.ds(place + top * wide, rows), :].astype(F32)
        for j in range(wide):
            matrix[top : top + height, LANES * j : LANES * (j + 1)] = spread[
                pl.ds(j, height, stride=wide), :
            ].astype(BF)


def norm_rows(values):
    centre = jnp.mean(values, axis=-1, keepdims=True)
    shifted = values - centre
    inverse = lax.rsqrt(jnp.mean(shifted * shifted, axis=-1, keepdims=True) + 1e-05)
    return shifted * inverse, inverse


def norm_back(unit, inverse, gain, grad):
    scaled = grad * gain
    along = jnp.mean(scaled * unit, axis=-1, keepdims=True)
    return inverse * (scaled - jnp.mean(scaled, axis=-1, keepdims=True) - unit * along)


def own_frame(rows):
    frame = lax.broadcasted_iota(jnp.int32, (rows // GROUP, GROUP, SLOTS), 1).reshape(rows, SLOTS)
    return frame == lax.broadcasted_iota(jnp.int32, (rows, SLOTS), 1) // NT


def same_token():
    a = lax.broadcasted_iota(jnp.int32, (SLOTS, SLOTS), 0) % NT
    b = lax.broadcasted_iota(jnp.int32, (SLOTS, SLOTS), 1) % NT
    return (a == b).astype(BF)


def learner_mask():
    return own_frame(D)


def section_kernel(
    windows,
    images,
    embedding,
    flat,
    grid_out,
    pooled_out,
    shifts_out,
    conv_out,
    learner_out,
    gains_out,
    *rest,
):
    step = pl.program_id(0)
    if windows.shards > 1:
        master = flat
        flat, stage, spread, film, modulated, blocks, edges, sems, master_in, own, *gather_sems = rest
        gather = Gather(own, flat, *gather_sems)
    else:
        gather = None
        stage, spread, film, modulated, blocks, edges, sems = rest

    def block_copy(at):
        return pltpu.make_async_copy(
            images.at[:, pl.ds(pl.multiple_of(at * GROUP, GROUP), GROUP)], blocks.at[at % 2], sems.at[30 + at % 2]
        )

    @pl.when(step == 0)
    def _():
        if gather:
            fetch = pltpu.make_async_copy(master, master_in, sems.at[29])
            fetch.start()
            block_copy(0).start()
            gather.greet()
            fetch.wait()
            rows = master.shape[0]
            spread[pl.ds(0, 16), :] = jnp.zeros((16, LANES), F32)
            tail = rows // 16 * 16
            spread[pl.ds(tail, WINDOW - tail), :] = jnp.zeros((WINDOW - tail, LANES), F32)
            spread[pl.ds(gather.ring.me * rows % 16, rows), :] = master_in[...]
            own[...] = spread[pl.ds(0, WINDOW), :].astype(BF)
            gather.begin(START["gains"] - windows.first[-1])
        else:
            block_copy(0).start()
        learner_rows = HEAD_PART - START["learner"]
        parts = [(0, HEAD_PART, 0)]
        if gather is None:
            parts.append((START["gains"], ROWS, HEAD_PART))
        for wait in windows.load(flat, stage, edges, sems, parts):
            wait()
        if gather:
            stage[pl.ds(HEAD_PART, 16), :] = gather.gain_rows[...]
        to_matrix(stage, 0, spread, film, SHAPES["film"])
        for side in range(2):
            shifts_out[side] = mm(embedding[...], film[:, CIN * side : CIN * (side + 1)])
        to_matrix(stage, START["conv"], spread, conv_out, SHAPES["conv"])
        packed = stage[pl.ds(START["learner"], learner_rows), :].astype(F32)
        opened = jnp.broadcast_to(packed[:, None, :], (learner_rows, GROUP, LANES)).reshape(D, SLOTS)
        opened = jnp.where(learner_mask(), opened, 0.0).astype(BF)
        learner_out[...] = mm(opened, same_token()).astype(BF)
        gain_rows = stage[pl.ds(HEAD_PART, 16), :].astype(F32)
        for i in range(4):
            for j in range(4):
                gains_out[i : i + 1, LANES * j : LANES * (j + 1)] = gain_rows[4 * i + j : 4 * i + j + 1]

    block_copy(step).wait()

    @pl.when(step + 1 < pl.num_programs(0))
    def _():
        block_copy(step + 1).start()

    here = pl.ds(pl.multiple_of(step * GROUP, GROUP), GROUP)
    scale = 1.0 + shifts_out[0, here, :]
    offset = shifts_out[1, here, :]
    modulated[...] = (blocks[step % 2].astype(F32) * scale[None] + offset[None]).astype(BF).reshape(CELLS, CIN)
    grid = mm(modulated[...], conv_out[...])
    grid_out[...] = grid.astype(BF)
    unit, _ = norm_rows(grid)
    normed = (unit * gains_out[0:1, :]).astype(BF)
    maps = jax.nn.sigmoid(mm(normed, learner_out[...]))
    maps = jnp.where(own_frame(CELLS), maps, 0.0).astype(BF)
    pooled_out[...] = mm_tn(maps, normed) * (1.0 / POS)
    if gather:
        gather.go_on(step, pl.num_programs(0))


def section(windows, images, embedding, flat):
    frames = images.shape[1]
    steps = frames // GROUP
    whole = lambda *shape: pl.BlockSpec(shape, lambda i: (0,) * len(shape))
    gathers = windows.shards > 1
    film_rows = SHAPES["film"][0] * SHAPES["film"][1] // LANES
    return pl.pallas_call(
        functools.partial(section_kernel, windows),
        grid=(steps,),
        in_specs=[
            pl.BlockSpec(memory_space=pl.ANY),
            whole(frames, E),
            pl.BlockSpec(memory_space=pl.ANY),
        ],
        out_specs=[
            pl.BlockSpec((CELLS, D), lambda i: (i, 0)),
            pl.BlockSpec((SLOTS, D), lambda i: (i, 0)),
            whole(2, frames, CIN),
            whole(CIN, D),
            whole(D, SLOTS),
            whole(4, D),
        ]
        + [pl.BlockSpec(memory_space=pl.ANY)] * gathers,
        out_shape=[
            jax.ShapeDtypeStruct((steps * CELLS, D), BF),
            jax.ShapeDtypeStruct((frames * NT, D), F32),
            jax.ShapeDtypeStruct((2, frames, CIN), F32),
            jax.ShapeDtypeStruct((CIN, D), BF),
            jax.ShapeDtypeStruct((D, SLOTS), BF),
            jax.ShapeDtypeStruct((4, D), F32),
        ]
        + [jax.ShapeDtypeStruct((windows.shards, WINDOW, LANES), BF)] * gathers,
        scratch_shapes=[
            pltpu.VMEM((HEAD_PART + 16, LANES), BF),
            pltpu.VMEM((film_rows + 32, LANES), F32),
            pltpu.VMEM(SHAPES["film"], BF),
            pltpu.VMEM((CELLS, CIN), BF),
            pltpu.VMEM((2, POS, GROUP, CIN), BF),
            pltpu.VMEM((8, 2, 16, LANES), BF),
            pltpu.SemaphoreType.DMA((32,)),
        ]
        + ([pltpu.VMEM(flat.shape, F32)] + GATHER_SCRATCH if gathers else []),
        compiler_params=pltpu.CompilerParams(
            vmem_limit_bytes=60 * MIB,
            **(dict(collective_id=0, has_side_effects=True) if gathers else {}),
        ),
        cost_estimate=pl.CostEstimate(
            flops=2 * frames * POS * CIN * D, bytes_accessed=frames * POS * CIN * 2, transcendentals=0
        ),
    )(images, embedding, flat)


def gelu_parts(x):
    inner = 0.7978845608028654 * (x + 0.044715 * x * x * x)
    bent = jnp.tanh(inner)
    value = 0.5 * x * (1.0 + bent)
    slope = 0.5 * (1.0 + bent) + 0.5 * x * (1.0 - bent * bent) * 0.7978845608028654 * (
        1.0 + 3.0 * 0.044715 * x * x
    )
    return value, slope


TOP = 256


def layer_part(
    windows,
    refs,
    reduce,
    late_out,
    stage,
    spread,
    triple,
    output,
    upward,
    downward,
    action,
    keys,
    values,
    grad_keys,
    grad_values,
    shares,
    first_normed,
    logits_back,
    edges,
    sems,
):
    start, flat, gains, steps_in, targets_in, grad_start, sums_out = refs
    tokens = start.shape[0]
    frames = tokens // NT
    place = {name: START[name] - HEAD_PART for name in SHAPES}
    matrices = dict(triple=triple, output=output, upward=upward, downward=downward, action=action)
    rows_of = lambda name: SHAPES[name][0] * SHAPES[name][1] // LANES
    waits = windows.load(
        flat, stage, edges, sems, [(START[name], START[name] + rows_of(name), place[name]) for name in matrices]
    )

    def bring(name):
        waits[list(matrices).index(name)]()
        to_matrix(stage, place[name], spread, matrices[name], SHAPES[name], TOP)

    is_last = lax.broadcasted_iota(jnp.int32, (tokens, D), 0) % NT == NT - 1

    def take_last(rows):
        return jnp.sum(jnp.where(is_last, rows, 0.0).reshape(frames, NT, D), axis=1)

    def spread_last(rows):
        wide = jnp.broadcast_to(rows[:, None, :], (frames, NT, D)).reshape(tokens, D)
        return jnp.where(is_last, wide, 0.0)

    gain = [gains[i : i + 1, :] for i in range(4)]

    first_unit, first_inverse = norm_rows(start[...])
    first_normed[...] = (first_unit * gain[1]).astype(BF)
    last_start = take_last(start[...])
    last_unit, _ = norm_rows(last_start)
    last_normed = (last_unit * gain[1]).astype(BF)
    bring("triple")
    queries = mm(last_normed, triple[:, :D]).astype(BF)
    keys[...] = mm(first_normed[...], triple[:, D : 2 * D]).astype(BF)
    values[...] = mm(first_normed[...], triple[:, 2 * D :]).astype(BF)
    token_rows = tokens // LANES
    episode_row = jnp.concatenate([steps_in[i : i + 1, :] for i in range(token_rows)], axis=1)
    key_place = lax.broadcasted_iota(jnp.int32, (frames, tokens), 1)
    query_place = lax.broadcasted_iota(jnp.int32, (frames, tokens), 0) * NT + (NT - 1)
    own_key = (key_place == query_place).astype(BF)
    column = lambda row: mm_nt(own_key, jnp.broadcast_to(row, (8, tokens)).astype(F32).astype(BF))[:, :1]
    episode_last = column(episode_row // BINS) * float(BINS) + column(episode_row % BINS)
    allowed = (episode_last.astype(jnp.int32) == episode_row) & (key_place <= query_place)
    diagonal = lax.broadcasted_iota(jnp.int32, (frames, LANES), 0) == lax.broadcasted_iota(
        jnp.int32, (frames, LANES), 1
    )
    valid_row = jnp.broadcast_to(steps_in[token_rows : token_rows + 1, :], (8, LANES))
    valid_flags = mm_nt(diagonal.astype(BF), valid_row.astype(F32).astype(BF))[:, :1]
    targets = mm_nt(diagonal[:, :frames].astype(BF), targets_in[...].astype(F32).astype(BF)).astype(jnp.int32)
    attended = []
    for h in range(HEADS):
        own = slice(HD * h, HD * (h + 1))
        scores = mm_nt(queries[:, own], keys[:, own]) * HD ** (-0.5)
        scores = jnp.where(allowed, scores, -1e30)
        powers = jnp.exp(scores - jnp.max(scores, axis=-1, keepdims=True))
        part = powers / jnp.sum(powers, axis=-1, keepdims=True)
        shares[h] = part
        attended.append(mm(part.astype(BF), values[:, own]))
    merged = jnp.concatenate(attended, axis=1).astype(BF)
    bring("output")
    middle = last_start + mm(merged, output[...])
    second_unit, second_inverse = norm_rows(middle)
    second_normed = (second_unit * gain[2]).astype(BF)
    bring("upward")
    activated, slope = gelu_parts(mm(second_normed, upward[...]))
    hidden = activated.astype(BF)
    bring("downward")
    end = middle + mm(hidden, downward[...])
    final_unit, final_inverse = norm_rows(end)
    final_rows = (final_unit * gain[3]).astype(BF)

    bring("action")
    bins = lax.broadcasted_iota(jnp.int32, (frames, BINS), 1)
    loss = jnp.zeros((frames, 1), F32)
    for a in range(ACT):
        own = slice(BINS * a, BINS * (a + 1))
        logits = mm(final_rows, action[:, own])
        shifted = logits - jnp.max(logits, axis=-1, keepdims=True)
        powers = jnp.exp(shifted)
        total = jnp.sum(powers, axis=-1, keepdims=True)
        hit = targets[:, a : a + 1] == bins
        loss += jnp.log(total) - jnp.sum(jnp.where(hit, shifted, 0.0), axis=-1, keepdims=True)
        logits_back[:, own] = ((powers / total - hit.astype(F32)) * valid_flags).astype(BF)
    place_row = lax.broadcasted_iota(jnp.int32, (8, LANES), 0)
    sums_out[...] = jnp.where(
        place_row == 0, jnp.sum(loss * valid_flags), jnp.where(place_row == 1, jnp.sum(valid_flags), 0.0)
    )

    def put(name, parts):
        height, breadth = SHAPES[name]
        wide = breadth // LANES
        rows = TOP * wide
        for top in range(0, height, TOP):
            j = 0
            for left, right in parts:
                rounded_left = left[:, top : top + TOP]
                for k in range(0, right.shape[1], 2 * LANES):
                    part = mm_tn(rounded_left, right[:, k : k + 2 * LANES])
                    spread[pl.ds(j, TOP, stride=wide), :] = part[:, :LANES]
                    spread[pl.ds(j + 1, TOP, stride=wide), :] = part[:, LANES:]
                    j += 2
            stage[pl.ds(place[name] + top * wide, rows), :] = spread[pl.ds(0, rows), :].astype(BF)

    def give(devices, unit):
        if reduce:
            for device in devices:
                reduce.give_early(stage, device)
            reduce.advance(unit, late=False)

    put("action", [(final_rows, logits_back[...])])
    grad_final = mm_nt(logits_back[...], action[...])
    gain_final = jnp.sum(grad_final * final_unit, axis=0, keepdims=True)
    grad_last = norm_back(final_unit, final_inverse, gain[3], grad_final)
    rounded = grad_last.astype(BF)
    put("downward", [(hidden, rounded)])
    give((7, 6), -5)
    grad_upward = (mm_nt(rounded, downward[...]) * slope).astype(BF)
    put("upward", [(second_normed, grad_upward)])
    give((5, 4), -4)
    grad_second = mm_nt(grad_upward, upward[...])
    gain_second = jnp.sum(grad_second * second_unit, axis=0, keepdims=True)
    grad_last = grad_last + norm_back(second_unit, second_inverse, gain[2], grad_second)
    rounded = grad_last.astype(BF)
    put("output", [(merged, rounded)])
    grad_attended = mm_nt(rounded, output[...]).astype(BF)
    give((), -3)
    grad_queries = []
    for h in range(HEADS):
        own = slice(HD * h, HD * (h + 1))
        part = shares[h]
        grad_shares = mm_nt(grad_attended[:, own], values[:, own])
        grad_values[:, own] = mm_tn(part.astype(BF), grad_attended[:, own]).astype(BF)
        grad_scores = part * (grad_shares - jnp.sum(grad_shares * part, axis=-1, keepdims=True))
        grad_scores = grad_scores.astype(BF)
        grad_queries.append(mm(grad_scores, keys[:, own]) * HD ** (-0.5))
        grad_keys[:, own] = (mm_tn(grad_scores, queries[:, own]) * HD ** (-0.5)).astype(BF)
    grad_queries = jnp.concatenate(grad_queries, axis=1).astype(BF)
    put(
        "triple",
        [
            (last_normed, grad_queries),
            (first_normed[...], grad_keys[...]),
            (first_normed[...], grad_values[...]),
        ],
    )
    grad_start[...] = (
        mm_nt(grad_keys[...], triple[:, D : 2 * D])
        + mm_nt(grad_values[...], triple[:, 2 * D :])
        + spread_last(mm_nt(grad_queries, triple[:, :D]))
    )
    grad_first = grad_start[...]
    gain_first = jnp.sum(grad_first * first_unit, axis=0, keepdims=True)
    rows = []
    for part in (jnp.zeros((1, D), F32), gain_first, gain_second, gain_final):
        rows += [part[:, LANES * j : LANES * (j + 1)] for j in range(4)]
    stage[pl.ds(place["gains"], 16), :] = jnp.concatenate(rows, axis=0).astype(BF)
    stage[pl.ds(place["gains"] + 16, LATE_ROWS - place["gains"] - 16), :] = jnp.zeros(
        (LATE_ROWS - place["gains"] - 16, LANES), BF
    )
    give((3, 2), -2)
    grad_start[...] = norm_back(first_unit, first_inverse, gain[1], grad_first) + spread_last(grad_last)
    if reduce:
        reduce.keep_patch(stage)
        reduce.advance(-1, late=False)
        reduce.early_left(stage)
    else:
        out = pltpu.make_async_copy(stage, late_out, sems.at[0])
        out.start()
        out.wait()


def layer_scratch(tokens):
    frames = tokens // NT
    return [
        pltpu.VMEM((LATE_ROWS, LANES), BF),
        pltpu.VMEM((TOP * SHAPES["action"][1] // LANES + 32, LANES), F32),
        pltpu.VMEM(SHAPES["triple"], BF),
        pltpu.VMEM(SHAPES["output"], BF),
        pltpu.VMEM(SHAPES["upward"], BF),
        pltpu.VMEM(SHAPES["downward"], BF),
        pltpu.VMEM(SHAPES["action"], BF),
        pltpu.VMEM((tokens, D), BF),
        pltpu.VMEM((tokens, D), BF),
        pltpu.VMEM((tokens, D), BF),
        pltpu.VMEM((tokens, D), BF),
        pltpu.VMEM((HEADS, frames, tokens), F32),
        pltpu.VMEM((tokens, D), BF),
        pltpu.VMEM((frames, ACT * BINS), BF),
        pltpu.VMEM((8, 2, 16, LANES), BF),
        pltpu.SemaphoreType.DMA((32,)),
    ]


BLOCK = 256
BLOCKS = CIN // BLOCK
EARLY_ITEM = 1152
EARLY = WINDOW // EARLY_ITEM
FIRST_ITEM = 1008
ITEM = 576
LAST_ITEM = 288
ADD_ROWS = 288
SLAB = WINDOW + LAST_ITEM
FILM_ITEMS = 2 * BLOCKS
CONV_ITEMS = 8
LATE_ID = EARLY
LAST_ID = LATE_ID + FILM_ITEMS
IDS = LAST_ID + 1
EARLY_LAG, EARLY_LINE_LAG, LAG, LINE_LAG = 3, 3, 2, 2
EARLY_PACE = 3
EARLY_UNITS = ((99, 0, -3, -3), (99, -2, -3, -1))
FIRST_SCALE, FIRST_OFFSET, FIRST_CONV, LAST_UNIT = 8, 7, 9, 18
COMPUTE_UNITS = 6 + 2 * BLOCKS
UNITS = max(LAST_UNIT + 3 * LAG + 4 * LINE_LAG, 5 * EARLY_PACE + 3 * EARLY_LAG + 4 * EARLY_LINE_LAG) + 1
CONV_BEFORE = (0, 0, 1, 3, 4, 6, 8)
OWN_CONV = 1280
TAIL_CONV = 1152
FILM_FIRST = (0, 272)
FILM_HEIGHT = (288, 240)
SQUARES = 2
RING_PLACE = (0, 0, 1, 3, 3, 1, 2, 2)


def added(parts):
    total = parts[0].astype(F32)
    for part in parts[1:]:
        total = total + part.astype(F32)
    return total


class Reduce:
    def __init__(self, shard_rows, patch, own, sibling, ring_in, z_in, sems, z_sems):
        self.ring = ring = Ring()
        self.shard_rows, self.patch = shard_rows, patch
        self.own, self.sibling, self.ring_in, self.z_in = own, sibling, ring_in, z_in
        self.sems, self.z_sems = sems, z_sems
        self.line = ring.replica + ring.core * (3 - 2 * ring.replica)

    def greet(self):
        barrier = pltpu.get_barrier_semaphore()
        devices = [{"fsdp": other} for other in self.ring.others]
        devices += [{"dp": (self.ring.replica + hops) % 4} for hops in (1, 2, 3)]
        for device in devices:
            pl.semaphore_signal(barrier, inc=1, device_id=device, device_id_type=MESH)
        pl.semaphore_wait(barrier, len(devices))

    def along(self, line):
        return {"dp": line + self.ring.core * (3 - 2 * line)}

    def stage_of(self, q):
        return (self.ring.place + 7 - q) % 4

    def rows(self, row, count):
        return pl.ds(pl.multiple_of(row, 16), count)

    def remote(self, source, target, send_sem, recv_sem, device):
        return pltpu.make_async_remote_copy(
            src_ref=source,
            dst_ref=target,
            send_sem=send_sem,
            recv_sem=recv_sem,
            device_id=device,
            device_id_type=MESH,
        )

    def to_sibling(self, source, q, ident, row, count):
        return self.remote(
            source,
            self.sibling.at[q, self.rows(row, count)],
            self.sems.at[0, q, ident],
            self.sems.at[1, q, ident],
            {"fsdp": self.ring.sibling},
        )

    def to_next(self, q, ident, row, count):
        rows = self.rows(row, count)
        return self.remote(
            self.own.at[q, rows],
            self.ring_in.at[jnp.minimum(self.stage_of(q), 2), rows],
            self.sems.at[2, q, ident],
            self.sems.at[3, q, ident],
            {"fsdp": self.ring.after},
        )

    def to_line(self, which, line, slot, ident, row, count, forward=False):
        rows = self.rows(row, count)
        return self.remote(
            self.z_in.at[1, rows] if forward else self.own.at[self.ring.place, rows],
            self.z_in.at[slot, rows],
            self.z_sems.at[which, ident],
            self.z_sems.at[2 + slot, ident],
            self.along(line),
        )

    def early_items(self, device):
        if device == 2:
            top = WINDOW - 2 * FIRST_ITEM
            items = [(i, top + FIRST_ITEM * i, FIRST_ITEM) for i in range(2)]
        else:
            items = [(i, EARLY_ITEM * i, EARLY_ITEM) for i in range(EARLY)]
        return items, self.shard_rows * device // 16 * 16 - HEAD_PART

    def give_early(self, stage, device):
        q = RING_PLACE[device]
        items, first = self.early_items(device)

        @pl.when(self.ring.core == device % 2)
        def _():
            top, count = items[0][1], sum(item[2] for item in items)
            self.own[q, pl.ds(top, count), :] = stage[pl.ds(first + top, count), :]

        @pl.when(self.ring.core != device % 2)
        def _():
            for ident, row, count in items:
                if device < 7 or ident < EARLY - 1:
                    self.to_sibling(stage.at[pl.ds(first + row, count)], q, ident, row, count).start()

    def keep_patch(self, stage):
        last = self.shard_rows * 7 // 16 * 16 - HEAD_PART + (EARLY - 1) * EARLY_ITEM
        self.patch[...] = stage[pl.ds(last, EARLY_ITEM), :]

    def early_left(self, stage):
        for device in range(2, 8):
            q = RING_PLACE[device]
            items, first = self.early_items(device)

            @pl.when(self.ring.core != device % 2)
            def _():
                for ident, row, count in items:
                    if device < 7 or ident < EARLY - 1:
                        self.to_sibling(stage.at[pl.ds(first + row, count)], q, ident, row, count).wait_send()

    def patch_gains(self, gain_rows):
        place = START["gains"] - (self.shard_rows * 7 // 16 * 16 + (EARLY - 1) * EARLY_ITEM)
        here = pl.ds(place, 16)
        self.patch[here, :] = (self.patch[here, :].astype(F32) + gain_rows).astype(BF)

        @pl.when(self.ring.core == 0)
        def _():
            self.to_sibling(self.patch, 2, EARLY - 1, (EARLY - 1) * EARLY_ITEM, EARLY_ITEM).start()

        @pl.when(self.ring.core == 1)
        def _():
            self.own[2, pl.ds((EARLY - 1) * EARLY_ITEM, EARLY_ITEM), :] = self.patch[...]

    def give_film(self, film, conv, step, half):
        item = 2 * step + half
        row = ITEM * item
        tiles = [half * (CIN // LANES) + 2 * step + a for a in range(2)]
        conv_rows = self.rows(96 * item, 96)
        for core in range(2):
            first, height = FILM_FIRST[core], FILM_HEIGHT[core]

            @pl.when(self.ring.core == core)
            def _():
                for a in range(2):
                    self.own[0, self.rows(row + height * a, height), :] = film[tiles[a], first : first + height, :]
                if core == 1:
                    self.own[0, self.rows(row + 2 * height, 96), :] = conv[conv_rows, :]

            @pl.when(self.ring.core != core)
            def _():
                ident = LATE_ID + item
                for a in range(2):
                    self.to_sibling(
                        film.at[tiles[a], pl.ds(first, height)], 0, ident, row + height * a, height
                    ).start()
                if core == 1:
                    self.to_sibling(conv.at[conv_rows], 0, ident, row + 2 * height, 96).start()

    def give_conv(self, conv, step):
        ring = self.ring

        @pl.loop(ring.pick(CONV_BEFORE, step), ring.pick(CONV_BEFORE, step + 1))
        def _(i):
            source = self.rows(OWN_CONV + ITEM * i, ITEM)

            @pl.when(ring.core == 0)
            def _():
                self.own[1, self.rows(ITEM * i, ITEM), :] = conv[source, :]

            @pl.when(ring.core == 1)
            def _():
                self.to_sibling(conv.at[source], 1, LATE_ID + i, ITEM * i, ITEM).start()

        @pl.when(step == BLOCKS - 1)
        def _():
            mine = pl.ds(OWN_CONV + CONV_ITEMS * ITEM, LAST_ITEM)
            tail = pl.ds(TAIL_CONV, LAST_ITEM)

            @pl.when(ring.core == 0)
            def _():
                self.own[1, pl.ds(CONV_ITEMS * ITEM, LAST_ITEM), :] = conv[mine, :]
                self.to_sibling(conv.at[tail], 0, LAST_ID, WINDOW, LAST_ITEM).start()

            @pl.when(ring.core == 1)
            def _():
                self.own[0, pl.ds(WINDOW, LAST_ITEM), :] = conv[tail, :]
                self.to_sibling(conv.at[mine], 1, LAST_ID, CONV_ITEMS * ITEM, LAST_ITEM).start()

    def add_up(self, q, row, count, others):
        height = ADD_ROWS if count % ADD_ROWS == 0 else count // 3

        @pl.loop(0, count // height)
        def _(block):
            rows = self.rows(row + block * height, height)
            parts = [self.own[q, rows, :]] + [ref[which, rows, :] for ref, which in others]
            self.own[q, rows, :] = added(parts).astype(BF)

    def hop_ring(self, q, ident, row, count):
        stage = self.stage_of(q)
        self.to_sibling(self.own.at[q, self.rows(row, count)], q, ident, row, count).wait_recv()

        @pl.when(stage == 0)
        def _():
            self.add_up(q, row, count, [(self.sibling, q)])

        @pl.when(stage > 0)
        def _():
            self.to_next(q, ident, row, count).wait_recv()
            self.add_up(q, row, count, [(self.sibling, q), (self.ring_in, stage - 1)])

        @pl.when(stage < 3)
        def _():
            self.to_next(q, ident, row, count).start()

        @pl.when((stage == 3) & (self.line == 0))
        def _():
            self.to_line(0, 1, 0, ident, row, count).start()

        @pl.when((stage == 3) & (self.line == 3))
        def _():
            self.to_line(0, 2, 0, ident, row, count).start()

    def hop_line(self, ident, row, count):
        place = self.ring.place

        @pl.when(self.line == 2)
        def _():
            self.to_line(0, 1, 0, ident, row, count).wait_recv()
            self.add_up(place, row, count, [(self.z_in, 0)])
            self.to_line(0, 1, 1, ident, row, count).start()

        @pl.when(self.line == 1)
        def _():
            self.to_line(0, 1, 0, ident, row, count).wait_recv()
            self.to_line(0, 1, 1, ident, row, count).wait_recv()
            self.add_up(place, row, count, [(self.z_in, 0), (self.z_in, 1)])
            self.to_line(0, 0, 0, ident, row, count).start()
            self.to_line(1, 2, 1, ident, row, count).start()

    def hop_back(self, ident, row, count):
        @pl.when(self.line == 2)
        def _():
            self.to_line(0, 1, 1, ident, row, count).wait_recv()
            self.to_line(1, 3, 0, ident, row, count, forward=True).start()

        @pl.when(self.line != 2)
        def _():
            self.to_line(0, 1, 0, ident, row, count).wait_recv()

    def early(self, q, unit):
        core = self.ring.core
        begin = jnp.where(core == 0, self.ring.pick(EARLY_UNITS[0], q), self.ring.pick(EARLY_UNITS[1], q))
        at = unit - begin
        there = (q >= 2 - core) & (at >= 0) & (at % EARLY_PACE == 0) & (at < EARLY_PACE * EARLY)
        ident = at // EARLY_PACE
        return there, ident, EARLY_ITEM * ident

    def streams(self):
        core = self.ring.core

        def first(unit):
            at = unit - EARLY_UNITS[0][1]
            there = (at >= 0) & (at % EARLY_PACE == 0) & (at < 2 * EARLY_PACE)
            return there, at // EARLY_PACE, WINDOW - 2 * FIRST_ITEM + FIRST_ITEM * (at // EARLY_PACE)

        def scale(unit):
            at = unit - FIRST_SCALE
            return (at >= 0) & (at < FILM_ITEMS) & (at % 2 == 0), LATE_ID + at, ITEM * at

        def offset(unit):
            item = 2 * (unit - FIRST_OFFSET) + 1
            return (item >= 0) & (item < FILM_ITEMS), LATE_ID + item, ITEM * item

        def conv(unit):
            at = unit - FIRST_CONV
            item = at - jnp.where(at > 0, 1, 0) - jnp.where(at > 5, 1, 0)
            there = (at >= 0) & (at != 1) & (at != 5) & (item < CONV_ITEMS)
            return there, LATE_ID + item, ITEM * item

        def last(unit):
            return unit == LAST_UNIT, LAST_ID, jnp.where(core == 0, CONV_ITEMS * ITEM, WINDOW)

        return [
            (1, core == 0, FIRST_ITEM, first, EARLY_LAG, EARLY_LINE_LAG),
            (0, core >= 0, ITEM, scale, LAG, LINE_LAG),
            (0, core >= 0, ITEM, offset, LAG, LINE_LAG),
            (1, core == 0, ITEM, conv, LAG, LINE_LAG),
            (1 - core, core >= 0, LAST_ITEM, last, LAG, LINE_LAG),
        ]

    def advance(self, unit, late=True):
        ring, line = self.ring, self.line
        streams = self.streams()[: None if late else 1]

        @pl.loop(2 - ring.core, 4)
        def _(q):
            there, ident, row = self.early(q, unit - EARLY_LAG * self.stage_of(q))

            @pl.when(there)
            def _():
                self.hop_ring(q, ident, row, EARLY_ITEM)

        for q, has, count, item, lag, _ in streams:
            there, ident, row = item(unit - lag * self.stage_of(q))

            @pl.when(has & there)
            def _():
                self.hop_ring(q, ident, row, count)

        owners = [(ring.place >= 0, EARLY_ITEM, functools.partial(self.early, ring.place), EARLY_LAG, EARLY_LINE_LAG)]
        owners += [(has & (ring.place == q), count, item, *lags) for q, has, count, item, *lags in streams]
        for owner, count, item, lag, line_lag in owners:
            there, ident, row = item(unit - 3 * lag - line_lag * jnp.where(line == 2, 1, 2))

            @pl.when(owner & there & ((line == 1) | (line == 2)))
            def _():
                self.hop_line(ident, row, count)

            there, ident, row = item(unit - 3 * lag - line_lag * jnp.where(line == 3, 4, 3))

            @pl.when(owner & there & (line != 1))
            def _():
                self.hop_back(ident, row, count)

    def finish(self):
        ring, line = self.ring, self.line

        def sent(q, ident, row, count, owner):
            @pl.when(self.stage_of(q) < 3)
            def _():
                self.to_next(q, ident, row, count).wait_send()

            @pl.when(owner)
            def _():
                self.to_line(0, 1, 0, ident, row, count).wait_send()

                @pl.when((line == 1) | (line == 2))
                def _():
                    self.to_line(1, 1, 0, ident, row, count).wait_send()

        def given(q, ident, row, count):
            self.to_sibling(self.own.at[q, self.rows(row, count)], q, ident, row, count).wait_send()

        @pl.loop(0, EARLY)
        def _(i):
            @pl.loop(2 - ring.core, 4)
            def _(q):
                sent(q, i, EARLY_ITEM * i, EARLY_ITEM, q == ring.place)

        @pl.loop(0, FILM_ITEMS)
        def _(i):
            sent(0, LATE_ID + i, ITEM * i, ITEM, ring.place == 0)
            given(0, LATE_ID + i, ITEM * i, ITEM)

        @pl.when(ring.core == 0)
        def _():
            for i in range(2):
                sent(1, i, WINDOW - FIRST_ITEM * (2 - i), FIRST_ITEM, ring.place == 1)

            @pl.loop(0, CONV_ITEMS)
            def _(i):
                sent(1, LATE_ID + i, ITEM * i, ITEM, ring.place == 1)

            sent(1, LAST_ID, CONV_ITEMS * ITEM, LAST_ITEM, ring.place == 1)
            given(0, LAST_ID, WINDOW, LAST_ITEM)
            given(2, EARLY - 1, (EARLY - 1) * EARLY_ITEM, EARLY_ITEM)

        @pl.when(ring.core == 1)
        def _():
            @pl.loop(0, CONV_ITEMS)
            def _(i):
                given(1, LATE_ID + i, ITEM * i, ITEM)

            given(1, LAST_ID, CONV_ITEMS * ITEM, LAST_ITEM)
            sent(0, LAST_ID, WINDOW, LAST_ITEM, ring.place == 0)

    def assemble(self, spread):
        ring, line = self.ring, self.line
        place = ring.place

        whole = self.sibling

        @pl.when((line == 0) | (line == 3))
        def _():
            whole[place] = self.z_in[0]

        @pl.when(line == 1)
        def _():
            whole[place] = self.own[place]

        @pl.when(line == 2)
        def _():
            whole[place] = self.z_in[1]

        wide = 2 * CIN // LANES
        for core in range(2):
            height = FILM_HEIGHT[core]

            @pl.when(ring.me == core)
            def _():
                for step in range(BLOCKS):
                    for half in range(2):
                        row = ITEM * (2 * step + half)
                        for a in range(2):
                            tile = half * (CIN // LANES) + 2 * step + a
                            spread[pl.ds(tile, height, stride=wide), :] = whole[
                                0, row + height * a : row + height * (a + 1), :
                            ].astype(F32)
                        if core == 1:
                            spread[pl.ds(height * wide + 96 * (2 * step + half), 96), :] = whole[
                                0, row + 2 * height : row + 2 * height + 96, :
                            ].astype(F32)
                if core == 1:
                    spread[pl.ds(height * wide + TAIL_CONV, LAST_ITEM), :] = whole[0, WINDOW:SLAB, :].astype(F32)

        @pl.when(ring.me > 1)
        def _():
            spread[pl.ds(0, WINDOW), :] = whole[place, 0:WINDOW, :].astype(F32)

    def shard_offset(self):
        me = self.ring.me
        second = self.shard_rows - FILM_FIRST[1] * (2 * CIN // LANES)
        return jnp.where(me == 1, second, self.shard_rows * me % 16)


class Sums:
    def __init__(self, plane, line, plane_sems, line_sems):
        self.ring = Ring()
        self.plane, self.line, self.plane_sems, self.line_sems = plane, line, plane_sems, line_sems

    def plane_copy(self, which, index):
        me = self.ring.me
        return pltpu.make_async_remote_copy(
            src_ref=self.plane.at[which, me],
            dst_ref=self.plane.at[which, me],
            send_sem=self.plane_sems.at[0, which, index],
            recv_sem=self.plane_sems.at[1, which, index],
            device_id={"fsdp": self.ring.others[index]},
            device_id_type=MESH,
        )

    def line_copy(self, hops):
        own = self.ring.replica
        return pltpu.make_async_remote_copy(
            src_ref=self.line.at[own],
            dst_ref=self.line.at[own],
            send_sem=self.line_sems.at[0, hops - 1],
            recv_sem=self.line_sems.at[1, hops - 1],
            device_id={"dp": (own + hops) % 4},
            device_id_type=MESH,
        )

    def give(self, which, value):
        self.plane[which, self.ring.me] = value
        for index in range(self.ring.shards - 1):
            self.plane_copy(which, index).start()

    def take(self, which):
        for index in range(self.ring.shards - 1):
            self.plane_copy(which, index).wait()
        return jnp.sum(self.plane[which], axis=0)

    def give_line(self, value):
        self.line[self.ring.replica] = value
        for hops in (1, 2, 3):
            self.line_copy(hops).start()

    def take_line(self):
        for hops in (1, 2, 3):
            self.line_copy(hops).wait()
        return jnp.sum(self.line[...], axis=0)


def back_kernel(
    windows,
    start,
    flat,
    gains,
    steps_in,
    targets,
    images,
    embedding,
    shifts_in,
    conv_in,
    learner,
    grid,
    *rest,
):
    reduces = windows.shards > 1
    *rest, shifts, conv, operand_sems = rest
    operands = [
        pltpu.make_async_copy(shifts_in, shifts, operand_sems.at[0]),
        pltpu.make_async_copy(conv_in, conv, operand_sems.at[1]),
    ]
    for copy in operands:
        copy.start()
    if reduces:
        gradient, small_out, grad_start, sums_in, patch, own, sibling, ring_in, z_in, sems, z_sems, *rest = rest
        reduce = Reduce(windows.shard_rows, patch, own, sibling, ring_in, z_in, sems, z_sems)
        sums = Sums(*rest)
        late_out = None
        reduce.greet()
    else:
        film_out, conv_out, late_out, sums_in, gain_out, grad_start = rest
        reduce = None

    refs = (start, flat, gains, steps_in, targets, grad_start, sums_in)
    pl.run_scoped(functools.partial(layer_part, windows, refs, reduce, late_out), *layer_scratch(start.shape[0]))
    for copy in operands:
        copy.wait()
    if reduces:
        sums.give(0, sums_in[...])

    def section_part(
        grad_grid, grad_sum, learner_sum, gain_sum, modulated, grad_scale, conv_sum, conv_spread, film, conv_flat, cells, sems
    ):
        frames = embedding.shape[0]
        groups = frames // GROUP
        wide = D // LANES
        learner_sum[...] = jnp.zeros_like(learner_sum)
        gain_sum[...] = jnp.zeros_like(gain_sum)

        def block_copy(step, slot):
            return pltpu.make_async_copy(
                images.at[:, :, pl.ds(pl.multiple_of(step * BLOCK, BLOCK), BLOCK)], cells.at[slot], sems.at[2 + slot]
            )

        def first_part(fetched):
            def fetch(g, slot):
                return pltpu.make_async_copy(
                    grid.at[pl.ds(pl.multiple_of(g * CELLS, 16), CELLS)], fetched.at[slot], sems.at[slot]
                )

            fetch(0, 0).start()
            block_copy(0, 0).start()

            @pl.loop(0, groups)
            def _(g):
                slot = g % 2
                fetch(g, slot).wait()

                @pl.when(g + 1 < groups)
                def _():
                    fetch(g + 1, 1 - slot).start()

                rows = pl.ds(pl.multiple_of(g * CELLS, 16), CELLS)
                unit, inverse = norm_rows(fetched[slot].astype(F32))
                normed = (unit * gains[0:1, :]).astype(BF)
                maps = jax.nn.sigmoid(mm(normed, learner[...]))
                mask = own_frame(CELLS)
                tokens = grad_start[pl.ds(pl.multiple_of(g * SLOTS, SLOTS), SLOTS), :]
                tokens = (tokens * (1.0 / POS)).astype(BF)
                grad_maps = mm_nt(normed, tokens)
                grad_logit = jnp.where(mask, grad_maps * maps * (1.0 - maps), 0.0).astype(BF)
                maps = jnp.where(mask, maps, 0.0).astype(BF)
                grad_normed = mm(maps, tokens) + mm_nt(grad_logit, learner[...])
                learner_sum[...] += mm_tn(normed, grad_logit)
                gain_sum[...] += jnp.sum(grad_normed * unit, axis=0, keepdims=True)
                back = norm_back(unit, inverse, gains[0:1, :], grad_normed).astype(BF)
                grad_grid[rows, :] = back
                grad_sum[pl.ds(pl.multiple_of(g * GROUP, GROUP), GROUP), :] = jnp.sum(
                    back.astype(F32).reshape(POS, GROUP, D), axis=0
                )
                if reduces:
                    reduce.advance(g, late=False)

        pl.run_scoped(first_part, pltpu.VMEM((2, CELLS, D), BF))

        total = learner_sum[...]
        high = total.astype(BF)
        token = same_token()
        spread_learner = mm(high, token) + mm((total - high.astype(F32)).astype(BF), token)
        spread_learner = jnp.where(learner_mask(), spread_learner, 0.0)
        conv_flat[pl.ds(CIN * wide, D * NT // LANES), :] = jnp.sum(
            spread_learner.reshape(D * NT // LANES, GROUP, LANES), axis=1
        ).astype(BF)
        if reduces:
            rows = [gain_sum[:, LANES * j : LANES * (j + 1)] for j in range(wide)]
            reduce.patch_gains(jnp.concatenate(rows + [jnp.zeros((16 - wide, LANES), F32)], axis=0))
            sums.give_line(sums.take(0))
        else:
            gain_out[...] = gain_sum[...]

        def put_film(step, half, grad):
            part = mm_tn(embedding[...], grad.astype(BF)).astype(BF)
            for i in range(BLOCK // LANES):
                film[half * (CIN // LANES) + step * (BLOCK // LANES) + i] = part[:, LANES * i : LANES * (i + 1)]

        total = grad_sum[...]
        high = total.astype(BF)
        low = (total - high.astype(F32)).astype(BF)
        for step in range(BLOCKS):
            weights = conv[BLOCK * step : BLOCK * (step + 1), :]
            put_film(step, 1, mm_nt(high, weights) + mm_nt(low, weights))

        @pl.loop(0, BLOCKS)
        def _(step):
            slot = step % 2
            block_copy(step, slot).wait()

            @pl.when(step + 1 < BLOCKS)
            def _():
                block_copy(step + 1, 1 - slot).start()

            channels = pl.ds(pl.multiple_of(step * BLOCK, BLOCK), BLOCK)
            weights = conv[channels, :]

            conv_sum[...] = jnp.zeros_like(conv_sum)
            for g in range(groups):
                rows = pl.ds(g * CELLS, CELLS)
                here = pl.ds(g * GROUP, GROUP)
                scale = 1.0 + shifts[0, here, channels]
                offset = shifts[1, here, channels]
                block = cells[slot, :, here, :].astype(F32)
                modulated[...] = (block * scale[None] + offset[None]).astype(BF).reshape(CELLS, BLOCK)
                conv_sum[...] += mm_tn(modulated[...], grad_grid[rows, :])
            for j in range(wide):
                conv_spread[pl.ds(j, BLOCK, stride=wide), :] = conv_sum[:, LANES * j : LANES * (j + 1)]
            conv_flat[pl.ds(pl.multiple_of(step * BLOCK * wide, 16), BLOCK * wide), :] = conv_spread[
                pl.ds(0, BLOCK * wide), :
            ].astype(BF)
            if reduces:
                reduce.give_conv(conv_flat, step)

                @pl.when(step == 0)
                def _():
                    for block in range(BLOCKS - 1):
                        reduce.give_film(film, conv_flat, block, 1)

                @pl.when(step == 1)
                def _():
                    reduce.give_film(film, conv_flat, BLOCKS - 1, 1)

                reduce.advance(6 + 2 * step)

            for g in range(groups):
                here = pl.ds(g * GROUP, GROUP)
                back = mm_nt(grad_grid[pl.ds(g * CELLS, CELLS), :], weights).reshape(POS, GROUP, BLOCK)
                grad_scale[here, :] = jnp.sum(back * cells[slot, :, here, :].astype(F32), axis=0)
            put_film(step, 0, grad_scale[...])
            if reduces:
                reduce.give_film(film, conv_flat, step, 0)


                reduce.advance(7 + 2 * step)

        if not reduces:
            copies = [
                pltpu.make_async_copy(film, film_out, sems.at[0]),
                pltpu.make_async_copy(conv_flat, conv_out, sems.at[1]),
            ]
            for copy in copies:
                copy.start()
            for copy in copies:
                copy.wait()
            return

        @pl.loop(COMPUTE_UNITS, UNITS)
        def _(unit):
            reduce.advance(unit)

        reduce.finish()

    frames = embedding.shape[0]
    pl.run_scoped(
        section_part,
        pltpu.VMEM((frames * POS, D), BF),
        pltpu.VMEM((frames, D), F32),
        pltpu.VMEM((D, SLOTS), F32),
        pltpu.VMEM((1, D), F32),
        pltpu.VMEM((CELLS, BLOCK), BF),
        pltpu.VMEM((frames, BLOCK), F32),
        pltpu.VMEM((BLOCK, D), F32),
        pltpu.VMEM((BLOCK * D // LANES + 8, LANES), F32),
        pltpu.VMEM((2 * CIN // LANES, E, LANES), BF),
        pltpu.VMEM(((CIN * D + D * NT) // LANES, LANES), BF),
        pltpu.VMEM((2, POS, frames, BLOCK), BF),
        pltpu.SemaphoreType.DMA((4,)),
    )
    if not reduces:
        return

    def last_part(spread, sems):
        count = -(-gradient.shape[0] // 8) * 8
        reduce.assemble(spread)
        offset = reduce.shard_offset()

        def move(block, squares):
            part = spread[pl.ds(offset + block * LANES, LANES), :]
            spread[pl.ds(pl.multiple_of(block * LANES, LANES), LANES), :] = part
            return squares + jnp.sum((part * part).reshape(LANES // 8, 8, LANES), axis=0)

        blocks = windows.shard_rows // LANES
        squares = lax.fori_loop(0, blocks, move, jnp.zeros((8, LANES), F32))
        for row in range(blocks * LANES, count, 8):
            part = spread[pl.ds(offset + row, 8), :]
            spread[pl.ds(row, 8), :] = part
            kept = lax.broadcasted_iota(jnp.int32, (8, LANES), 0) + row < windows.shard_rows
            squares = squares + jnp.where(kept, part * part, 0.0)
        sums.give(1, squares)
        out = pltpu.make_async_copy(spread.at[pl.ds(0, gradient.shape[0])], gradient, sems.at[0])
        out.start()
        total = sums.take_line()
        total_squares = jnp.sum(sums.take(1))
        place_row = lax.broadcasted_iota(jnp.int32, (8, LANES), 0)
        small_out[...] = jnp.where(place_row == SQUARES, total_squares, total)
        out.wait()

    pl.run_scoped(last_part, pltpu.VMEM((SLAB + 32, LANES), F32), pltpu.SemaphoreType.DMA((1,)))


def back(windows, start, flat, gains, episode, valid, targets, images, embedding, shifts, conv, learner, grid):
    tokens = start.shape[0]
    frames = tokens // NT
    reduces = windows.shards > 1
    vmem = pl.BlockSpec(memory_space=pltpu.VMEM)
    anywhere = pl.BlockSpec(memory_space=pl.ANY)
    shard_rows = windows.shard_rows
    slab = lambda count: pltpu.VMEM((count, SLAB, LANES), BF)
    grad_start = pltpu.VMEM((tokens, D), F32)
    if reduces:
        scratch = [
            grad_start,
            pltpu.VMEM((8, LANES), F32),
            pltpu.VMEM((EARLY_ITEM, LANES), BF),
            slab(4),
            slab(4),
            slab(3),
            slab(2),
            pltpu.SemaphoreType.DMA((4, 4, IDS)),
            pltpu.SemaphoreType.DMA((4, IDS)),
            pltpu.VMEM((2, 8, 8, LANES), F32),
            pltpu.VMEM((4, 8, LANES), F32),
            pltpu.SemaphoreType.DMA((2, 2, 7)),
            pltpu.SemaphoreType.DMA((2, 3)),
        ]
        outs = [jax.ShapeDtypeStruct((shard_rows, LANES), F32), jax.ShapeDtypeStruct((8, LANES), F32)]
        out_specs = [anywhere, vmem]
    else:
        scratch = [grad_start]
        outs = [
            jax.ShapeDtypeStruct((2 * CIN // LANES, E, LANES), BF),
            jax.ShapeDtypeStruct(((CIN * D + D * NT) // LANES, LANES), BF),
            jax.ShapeDtypeStruct((LATE_ROWS, LANES), BF),
            jax.ShapeDtypeStruct((8, LANES), F32),
            jax.ShapeDtypeStruct((1, D), F32),
        ]
        out_specs = [anywhere] * 3 + [vmem] * 2
    return pl.pallas_call(
        functools.partial(back_kernel, windows),
        in_specs=[vmem, anywhere] + [vmem] * 3 + [anywhere, vmem, anywhere, anywhere, vmem, anywhere],
        out_specs=out_specs,
        out_shape=outs,
        scratch_shapes=scratch
        + [pltpu.VMEM(shifts.shape, F32), pltpu.VMEM(conv.shape, BF), pltpu.SemaphoreType.DMA((2,))],
        compiler_params=pltpu.CompilerParams(
            vmem_limit_bytes=63 * MIB,
            **(dict(collective_id=1, has_side_effects=True) if reduces else {}),
        ),
        cost_estimate=pl.CostEstimate(
            flops=4 * frames * POS * CIN * D, bytes_accessed=frames * POS * CIN * 2, transcendentals=0
        ),
    )(
        start,
        flat,
        gains,
        jnp.concatenate([episode, valid, jnp.zeros((-frames % LANES,), jnp.int32)]).reshape(-1, LANES),
        targets.T,
        images,
        embedding,
        shifts,
        conv,
        learner,
        grid,
    )


def on_device(
    images, embedding, episode, valid_steps, targets, master, first_moment, second_moment, average
):
    images = images.transpose(1, 0, 2)
    replicas, shards = lax.axis_size("dp"), lax.axis_size("fsdp")
    if fits_ring(replicas, shards, master.shape[0]):
        windows = Windows(shards, master.shape[0] // LANES, WINDOW)
        flat = master.reshape(-1, LANES)
    else:
        whole_flat = lax.all_gather(master.astype(BF), "fsdp", axis=0, tiled=True)
        flat = jnp.pad(whole_flat.reshape(ROWS, LANES), ((0, FLAT_ROWS - ROWS), (0, 0)))[None]
        windows = Windows(1, ROWS, FLAT_ROWS)

    grid, start, shifts, conv, learner, gains, *gathered = section(windows, images, embedding, flat)
    if gathered:
        (flat,) = gathered
    results = back(
        windows, start, flat, gains, episode, valid_steps, targets, images, embedding, shifts, conv, learner, grid
    )
    if gathered:
        shard, small = results
        loss_sum, step_count, squares = small[0, 0], small[1, 0], small[SQUARES, 0]
        inverse_count = 1.0 / step_count
        grad_shard = shard.reshape(-1) * inverse_count
        squares = squares * inverse_count * inverse_count
    else:
        film, conv_flat, late, sums, gain_grid = results
        at = START["gains"] - HEAD_PART
        late = late[: ROWS - HEAD_PART].at[at : at + 4].set(gain_grid.reshape(4, LANES).astype(BF))
        gradient = jnp.concatenate([film.transpose(1, 0, 2).reshape(-1, LANES), conv_flat, late])
        loss_sum, step_count = lax.psum((sums[0, 0], sums[1, 0]), ("dp", "fsdp"))
        partial_shard = lax.psum_scatter(gradient.reshape(-1), "fsdp", scatter_dimension=0, tiled=True)
        grad_shard = lax.psum(partial_shard.astype(F32), "dp") / step_count
        squares = lax.psum(jnp.sum(grad_shard * grad_shard), "fsdp")
    grad_norm = jnp.sqrt(squares)
    clipped = grad_shard * (CLIP_NORM / jnp.maximum(grad_norm, CLIP_NORM))
    new_first = MOMENT_DECAY * first_moment + (1.0 - MOMENT_DECAY) * clipped
    new_second = MOMENT_DECAY * second_moment + (1.0 - MOMENT_DECAY) * clipped * clipped
    correction = 1.0 - MOMENT_DECAY**STEP
    new_master = master - LEARN_RATE * (
        new_first / correction / (jnp.sqrt(new_second / correction) + ADAM_EPSILON)
        + WEIGHT_DECAY * master
    )
    average_decay = min(AVERAGE_DECAY, (1.0 + STEP) / (10.0 + STEP))
    new_average = average_decay * average + (1.0 - average_decay) * new_master
    return (
        new_master,
        new_first,
        new_second,
        new_average,
        new_master.astype(BF),
        grad_norm,
        loss_sum,
        step_count,
    )


def solution(mesh):
    in_specs = (
        P(("dp", "fsdp"), None, None),
        P(("dp", "fsdp"), None),
        P(("dp", "fsdp")),
        P(("dp", "fsdp")),
        P(("dp", "fsdp"), None),
        P("fsdp"),
        P("fsdp"),
        P("fsdp"),
        P("fsdp"),
    )
    out_specs = (P("fsdp"), P("fsdp"), P("fsdp"), P("fsdp"), P("fsdp"), P(), P(), P())
    return jax.shard_map(
        on_device, mesh=mesh, in_specs=in_specs, out_specs=out_specs, check_vma=False
    )
```
